512 devices in a mesh: sector: 64 (over y, z_hi, core), span: 8 (over x, z_lo).
Axes of the slice: x: 4, y: 8, z: 8 (z_hi: 4, z_lo: 2; z = z_hi * 2 + z_lo), core: 2. Of those that a mesh axis runs over, the one named last changes fastest.
Arguments:
- node_latents: bfloat16 [131072, 128], P(('sector', 'span')), may hold values from -6 to 6
- edge_latents: bfloat16 [524288, 128], P(('sector', 'span')), may hold values from -6 to 6
- senders: int32 [524288], P(('sector', 'span')), may hold values from 0 to 383
- receivers: int32 [524288], P(('sector', 'span')), may hold values from 0 to 255
- halo_rows: int32 [512, 4, 32], P(('sector', 'span')), may hold values from 0 to 255
- counts: int32 [512], P(('sector', 'span')), may hold values from 128 to 1024, as said below
- cotangent: bfloat16 [131072, 128], P(('sector', 'span')), may hold values from -8 to 8
- edge_first: bfloat16 [2, 384, 128], replicated, may hold values from -0.3125 to 0.3125
- edge_bias: float32 [2, 128], replicated, may hold values from -3 to 3
- edge_second: bfloat16 [2, 128, 128], replicated, may hold values from -0.5 to 0.5
- edge_gain: float32 [2, 128], replicated, may hold values from 2 to 4
- node_first: bfloat16 [2, 256, 128], replicated, may hold values from -0.375 to 0.375
- node_bias: float32 [2, 128], replicated, may hold values from -3 to 3
- node_second: bfloat16 [2, 128, 128], replicated, may hold values from -0.5 to 0.5
- node_gain: float32 [2, 128], replicated, may hold values from 2 to 4
Outputs:
- node_grad: bfloat16 [131072, 128], P(('sector', 'span'))
- edge_grad: bfloat16 [524288, 128], P(('sector', 'span'))
- edge_first_grad: float32 [2, 384, 128], replicated
- edge_bias_grad: float32 [2, 128], replicated
- edge_second_grad: float32 [2, 128, 128], replicated
- edge_gain_grad: float32 [2, 128], replicated
- node_first_grad: float32 [2, 256, 128], replicated
- node_bias_grad: float32 [2, 128], replicated
- node_second_grad: float32 [2, 128, 128], replicated
- node_gain_grad: float32 [2, 128], replicated
The draws below stay inside these ranges and needn't reach their ends.
Inputs may be any that keep to these rules, and one draw needn't show every extreme that they name: `counts`: some tile uses all 1024 slots.
All inputs are finite; a program needn't handle non-finite values.
Results may differ from the reference program's by a relative error of at most 0.03.
Values may be sent and summed in bfloat16 or wider, within the bound.
A program may use at most 64 MiB of HBM per device.

```python
import math
import jax
import jax.numpy as jnp
from jax import lax

D = 128
NODE_DEV = 256
STEPS = 2
EDGES_DEV = 1024
HALO = 32
TILES = 512
NODES = 131072
EDGES = 524288
N_SECTOR = 64
N_SPAN = 8


def draw_counts(key, part):
    key = jax.random.fold_in(key, 7)
    values = jax.random.randint(key, (TILES,), EDGES_DEV // 8, EDGES_DEV + 1)
    chosen = jax.random.randint(jax.random.fold_in(key, 1), (), 0, TILES)
    return jnp.where(jnp.arange(TILES) == chosen, EDGES_DEV, values).astype(jnp.int32)


def draw_cotangent(key, part):
    key = jax.random.fold_in(key, 11)
    rows = jnp.arange(NODES, dtype=jnp.float32)[:, None]
    rising = 0.5 + rows / NODES
    values = rising * jax.random.normal(key, (NODES, D), jnp.float32)
    return jnp.clip(values, -8.0, 8.0).astype(jnp.bfloat16)


def set_ends(result, rng, smallest, high):
    longest = result.shape.index(max(result.shape))
    spots = []
    for shift in (0, 1):
        where = [jax.random.randint(jax.random.fold_in(rng, axis), (), 0, length) for axis, length in enumerate(result.shape)]
        where[longest] = (where[longest] + shift) % result.shape[longest]
        spots.append(tuple(where))
    return result.at[spots[0]].set(smallest).at[spots[1]].set(high)


def block_levels(rng, extent, shards, smallest, top_value):
    loudness, own = 1.0, jax.random.fold_in(rng, 6)
    for dim, blocks in shards:
        draws = jnp.exp(jax.random.uniform(jax.random.fold_in(own, dim), (blocks,), jnp.float32, smallest / len(shards), top_value / len(shards)))
        loudness = loudness * jnp.repeat(draws, extent[dim] // blocks).reshape([-1 if axis == dim else 1 for axis in range(len(extent))])
    return loudness


def gaussian(own_key, extent, deviation, reach, split=(), kind=jnp.bfloat16):
    level = block_levels(own_key, extent, split, -0.22, 0.18) if split else 1.0
    array = jax.random.normal(own_key, extent, jnp.float32) * deviation * level
    return jnp.minimum(jnp.maximum(array, -reach), reach).astype(kind)


def setup_inputs(seed: int = 0) -> dict:
    key_list = jax.random.split(jax.random.key(seed), 16)
    node_latents = gaussian(key_list[0], (NODES, D), 1.0, 6.0, ((0, 512),))
    edge_latents = gaussian(key_list[1], (EDGES, D), 1.0, 6.0, ((0, 512),))
    senders = set_ends(jax.random.randint(key_list[2], (EDGES,), 0, NODE_DEV + 4 * HALO), jax.random.fold_in(key_list[2], 1), 0, (NODE_DEV + 4 * HALO) - 1).astype(jnp.int32)
    receivers = set_ends(jax.random.randint(key_list[3], (EDGES,), 0, NODE_DEV), jax.random.fold_in(key_list[3], 1), 0, NODE_DEV - 1).astype(jnp.int32)
    halo_rows = set_ends(jax.random.randint(key_list[4], (TILES, 4, HALO), 0, NODE_DEV), jax.random.fold_in(key_list[4], 1), 0, NODE_DEV - 1).astype(jnp.int32)
    counts = draw_counts(jax.random.fold_in(key_list[15], 71), 0)
    cotangent = draw_cotangent(jax.random.fold_in(key_list[15], 71), 0)
    edge_first = gaussian(key_list[7], (STEPS, 3 * D, D), (3 * D) ** -0.5, 0.3125)
    edge_bias = gaussian(key_list[8], (STEPS, D), 0.7, 3.0, (), jnp.float32)
    edge_second = gaussian(key_list[9], (STEPS, D, D), D ** -0.5, 0.5)
    edge_gain = jnp.clip(jnp.exp(jax.random.uniform(key_list[10], (STEPS, D), jnp.float32, math.log(2.0), math.log(4.0))), 2.0, 4.0)
    node_first = gaussian(key_list[11], (STEPS, 2 * D, D), (2 * D) ** -0.5, 0.375)
    node_bias = gaussian(key_list[12], (STEPS, D), 0.7, 3.0, (), jnp.float32)
    node_second = gaussian(key_list[13], (STEPS, D, D), D ** -0.5, 0.5)
    node_gain = jnp.clip(jnp.exp(jax.random.uniform(key_list[14], (STEPS, D), jnp.float32, math.log(2.0), math.log(4.0))), 2.0, 4.0)
    return dict(node_latents=node_latents, edge_latents=edge_latents, senders=senders, receivers=receivers, halo_rows=halo_rows, counts=counts, cotangent=cotangent, edge_first=edge_first, edge_bias=edge_bias, edge_second=edge_second, edge_gain=edge_gain, node_first=node_first, node_bias=node_bias, node_second=node_second, node_gain=node_gain)


EPS = 1e-05

def normalize(projected, gain):
    average = lax.optimization_barrier(jnp.mean(projected, axis=-1, keepdims=True))
    centred = projected - average
    spread = lax.optimization_barrier(jnp.mean(centred * centred, axis=-1, keepdims=True))
    return centred * lax.rsqrt(spread + EPS) * gain

def network(inputs, first, bias, second, gain):
    linear = jnp.dot(inputs, first.astype(jnp.bfloat16), preferred_element_type=jnp.float32) + bias
    activated = jax.nn.silu(linear).astype(jnp.bfloat16)
    projected = jnp.dot(activated, second.astype(jnp.bfloat16), preferred_element_type=jnp.float32)
    return normalize(projected, gain)

def tile_step(own_rows, halo_in, edge_rows, sender_ids, receiver_ids, live_mask, params):
    edge_first, edge_bias, edge_second, edge_gain, node_first, node_bias, node_second, node_gain = params
    extended = jnp.concatenate([own_rows, halo_in], axis=0).astype(jnp.bfloat16)
    own_half = own_rows.astype(jnp.bfloat16)
    edge_half = edge_rows.astype(jnp.bfloat16)
    edge_input = jnp.concatenate([jnp.take(extended, sender_ids, axis=0), jnp.take(own_half, receiver_ids, axis=0), edge_half], axis=1)
    update = network(edge_input, edge_first, edge_bias, edge_second, edge_gain)
    new_edge = (edge_rows + live_mask[:, None] * update).astype(jnp.bfloat16)
    new_edge_f = lax.optimization_barrier(new_edge).astype(jnp.float32)
    summed = jax.ops.segment_sum(live_mask[:, None] * new_edge_f, receiver_ids, num_segments=own_rows.shape[0]).astype(jnp.bfloat16)
    node_input = jnp.concatenate([own_half, summed], axis=1)
    node_update = network(node_input, node_first, node_bias, node_second, node_gain)
    new_node = (own_rows + node_update).astype(jnp.bfloat16)
    return (new_node, new_edge_f)

def pick_rows(rows, row_lists):
    return rows[row_lists]

def receive_rows(node_f, halo_rows):
    outgoing = jax.vmap(pick_rows)(node_f, halo_rows)
    outgoing = outgoing.reshape((N_SECTOR, N_SPAN) + outgoing.shape[1:])
    from_lower = jnp.roll(outgoing[:, :, 1], 1, axis=0)
    from_upper = jnp.roll(outgoing[:, :, 0], -1, axis=0)
    blank = jnp.zeros_like(outgoing[:, :1, 3])
    from_below = jnp.concatenate([blank, outgoing[:, :-1, 3]], axis=1)
    from_above = jnp.concatenate([outgoing[:, 1:, 2], blank], axis=1)
    joined = jnp.concatenate([from_lower, from_upper, from_below, from_above], axis=2)
    return joined.reshape((N_SECTOR * N_SPAN, -1, node_f.shape[-1]))

def reference(node_latents, edge_latents, senders, receivers, halo_rows, counts, cotangent, edge_first, edge_bias, edge_second, edge_gain, node_first, node_bias, node_second, node_gain):
    tiles = N_SECTOR * N_SPAN
    live_mask = (jnp.arange(EDGES_DEV, dtype=jnp.int32)[None, :] < counts[:, None]).astype(jnp.float32)
    sender_ids = senders.reshape(tiles, EDGES_DEV)
    receiver_ids = receivers.reshape(tiles, EDGES_DEV)
    weights = (edge_first.astype(jnp.float32), edge_bias, edge_second.astype(jnp.float32), edge_gain, node_first.astype(jnp.float32), node_bias, node_second.astype(jnp.float32), node_gain)

    def forward(node_half, edge_half, weight_set):
        node_f = node_half.astype(jnp.float32).reshape(tiles, NODE_DEV, -1)
        edge_f = edge_half.astype(jnp.float32).reshape(tiles, EDGES_DEV, -1)
        new_node = node_half.reshape(tiles, NODE_DEV, -1)
        for layer_index in range(STEPS):
            params = tuple((weight[layer_index] for weight in weight_set))
            received = receive_rows(node_f, halo_rows)

            def per_tile(pieces):
                own_rows, halo_in, edge_rows, sender_row, receiver_row, live_row = pieces
                return tile_step(own_rows, halo_in, edge_rows, sender_row, receiver_row, live_row, params)
            new_node, edge_f = lax.map(jax.checkpoint(per_tile), (node_f, received, edge_f, sender_ids, receiver_ids, live_mask))
            node_f = new_node.astype(jnp.float32)
        return new_node.reshape(NODES, -1)
    final_nodes, pullback = jax.vjp(forward, node_latents, edge_latents, weights)
    node_grad, edge_grad, weight_grads = pullback(cotangent)
    scale = jnp.float32(NODES) ** (-0.5)
    scaled = tuple((grad * scale for grad in weight_grads))
    return (node_grad, edge_grad, scaled[0], scaled[1], scaled[2], scaled[3], scaled[4], scaled[5], scaled[6], scaled[7])
```

```python
import jax
import jax.numpy as jnp
from jax import lax
from jax.experimental import pallas as pl
from jax.experimental.pallas import tpu as pltpu
from jax.sharding import PartitionSpec as P

F32, BF16 = jnp.float32, jnp.bfloat16
MESH = pl.DeviceIdType.MESH
STEPS = 2
EPS = 1e-05
Y, ZH, C, X, ZL = 8, 4, 2, 4, 2
NODES, SLOTS, D, HALO = 256, 1024, 128, 32
CHUNK = 256
AT_EF, AT_ES, AT_NF, AT_NS, AT_SMALL, ROWS = 0, 384, 512, 768, 896, 1024


def dot(a, b):
    return jnp.dot(a, b, preferred_element_type=F32)


def dot_first(a, b):
    return lax.dot_general(a, b, (((0,), (0,)), ((), ())), preferred_element_type=F32)


def dot_last(a, b):
    return lax.dot_general(a, b, (((1,), (1,)), ((), ())), preferred_element_type=F32)


def ones_where(mask):
    return jnp.where(mask, 1.0, 0.0).astype(BF16)


def activate(lin):
    sig = 0.5 * jnp.tanh(0.5 * lin) + 0.5
    act = lin * sig
    return act, sig + act * (1.0 - sig)


def normalized(proj):
    mean = jnp.mean(proj, axis=-1, keepdims=True)
    centred = proj - mean
    var = jnp.mean(centred * centred, axis=-1, keepdims=True)
    inv = lax.rsqrt(var + EPS)
    return centred * inv, inv


def normalized_back(dout, xhat, inv, gain):
    prod = dout * xhat
    dx = dout * gain
    mean = jnp.mean(dx, axis=-1, keepdims=True)
    along = jnp.mean(prod * gain, axis=-1, keepdims=True)
    return inv * (dx - mean - xhat * along), jnp.sum(prod, axis=0, keepdims=True)


def kernel(
    nodes, edges, snd, rcv, halo, counts, cot, ef, eb, es, eg, nf, nb, ns, ng,
    node_grad, edge_grad, o_ef, o_eb, o_es, o_eg, o_nf, o_nb, o_ns, o_ng,
    own_pick, rest, spread, hal_pad, h1, part, act_e, slope_e, xhat_e, inv_e, act_n, slope_n, xhat_n, inv_n,
    node_in, edge_new, de, dlin, dproj, dh,
    halo_out, halo_in, grads, got1, got2, mid, total,
    halo_ssem, halo_rsem, red_ssem, red_rsem,
):
    sector, span = lax.axis_index("sector"), lax.axis_index("span")
    n_sector, n_span = Y * ZH * C, X * ZL
    y, zh, c = sector // (ZH * C), lax.rem(sector // C, ZH), lax.rem(sector, C)
    x, zl = span // ZL, lax.rem(span, ZL)
    g1, g2 = ZH * X * C, Y * ZL
    me1, me2 = (zh * X + x) * C + c, y * ZL + zl
    unit = ROWS // g1

    def peer1(j):
        return ((y * ZH + j // (X * C)) * C + lax.rem(j, C), lax.rem(j // C, X) * ZL + zl)

    def peer2(j):
        return ((j // ZL * ZH + zh) * C + c, x * ZL + lax.rem(j, ZL))

    around = (
        (lax.rem(sector + n_sector - 1, n_sector), span),
        (lax.rem(sector + 1, n_sector), span),
        (sector, lax.rem(span + n_span - 1, n_span)),
        (sector, lax.rem(span + 1, n_span)),
    )

    barrier = pltpu.get_barrier_semaphore()
    for peer in around:
        pl.semaphore_signal(barrier, inc=1, device_id=peer, device_id_type=MESH)

    def greet1(k, _):
        pl.semaphore_signal(barrier, inc=1, device_id=peer1(lax.rem(me1 + k, g1)), device_id_type=MESH)
        return 0

    def greet2(k, _):
        pl.semaphore_signal(barrier, inc=1, device_id=peer2(lax.rem(me2 + k, g2)), device_id_type=MESH)
        return 0

    lax.fori_loop(1, g1, greet1, 0)
    lax.fori_loop(1, g2, greet2, 0)

    hal_pad[...] = jnp.zeros_like(hal_pad)
    hal_pad[0:4, 0:HALO] = halo[0].astype(F32)
    padded = hal_pad[...]
    lane = lax.broadcasted_iota(jnp.int32, (1, D), 1)
    flat = jnp.zeros((1, D), F32)
    for k in range(4):
        row = padded[k : k + 1, :] if k == 0 else pltpu.roll(padded, HALO * k, 1)[k : k + 1, :]
        flat = jnp.where((lane >= HALO * k) & (lane < HALO * (k + 1)), row, flat)
    lane_f = lax.broadcasted_iota(jnp.int32, (D, D), 1).astype(F32)
    down = jnp.broadcast_to(flat, (D, D)).T
    halo_pick = jnp.concatenate([ones_where(down == lane_f), ones_where(down == lane_f + D)], axis=1)
    halo_spread = ones_where(lax.broadcasted_iota(jnp.int32, (NODES, D), 0).astype(F32) == flat)

    row_id = lax.broadcasted_iota(jnp.int32, (4 * HALO, 1), 0)
    outside = ((row_id >= 2 * HALO) & (row_id < 3 * HALO) & (span == 0)) | (
        (row_id >= 3 * HALO) & (span == n_span - 1)
    )

    def exchange_start(t):
        for k in range(4):
            pltpu.make_async_remote_copy(
                src_ref=halo_out.at[t, pl.ds(k * HALO, HALO)],
                dst_ref=halo_in.at[t, pl.ds((k ^ 1) * HALO, HALO)],
                send_sem=halo_ssem.at[t],
                recv_sem=halo_rsem.at[t],
                device_id=around[k],
                device_id_type=MESH,
            ).start()

    def exchange_wait(t):
        pltpu.make_async_copy(halo_in.at[t], halo_in.at[t], halo_rsem.at[t]).wait()

    halo_out[0] = dot(halo_pick, nodes[...]).astype(BF16)
    pl.semaphore_wait(barrier, 4 + g1 - 1 + g2 - 1)
    exchange_start(0)

    used = counts[0]
    slot = lax.broadcasted_iota(jnp.int32, (SLOTS // D, D), 0) * D + lax.broadcasted_iota(
        jnp.int32, (SLOTS // D, D), 1
    )
    snd_f = jnp.where(slot < used, snd[...], -1).astype(F32)
    rcv_f = jnp.where(slot < used, rcv[...], -1).astype(F32)
    down_f = lax.broadcasted_iota(jnp.int32, (NODES + 4 * HALO, D), 0).astype(F32)
    for r in range(SLOTS // D):
        at = pl.ds(r * D, D)
        s_row, r_row = snd_f[r : r + 1, :], rcv_f[r : r + 1, :]
        spread[0:384, at] = ones_where(down_f == s_row)
        spread[384:640, at] = ones_where(down_f[0:256] == r_row)
        s_col = jnp.broadcast_to(s_row, (D, D)).T
        r_col = jnp.broadcast_to(r_row, (D, D)).T
        own_pick[at, 0:128] = ones_where(s_col == lane_f)
        own_pick[at, 128:256] = ones_where(s_col == lane_f + 128.0)
        own_pick[at, 256:384] = ones_where(r_col == lane_f)
        own_pick[at, 384:512] = ones_where(r_col == lane_f + 128.0)
        rest[at, 0:128] = ones_where(s_col == lane_f + 256.0)
    rest[:, 128:256] = edges[...]

    def forward(t):
        h = nodes[...] if t == 0 else h1[...]
        own_table = jnp.concatenate(
            [dot(h, ef[t, 0:128, :]).astype(BF16), dot(h, ef[t, 128:256, :]).astype(BF16)], axis=0
        )
        bias, gain = eb[t : t + 1, :], eg[t : t + 1, :]
        for i in range(SLOTS // CHUNK):
            at = pl.ds(i * CHUNK, CHUNK)
            part[at, :] = dot(own_pick[at, :], own_table) + bias
        exchange_wait(t)
        halo_in[t] = jnp.where(outside, 0.0, halo_in[t].astype(F32)).astype(BF16)
        rest_table = jnp.concatenate(
            [dot(halo_in[t], ef[t, 0:128, :]).astype(BF16), ef[t, 256:384, :]], axis=0
        )
        for i in range(SLOTS // CHUNK):
            at = pl.ds(i * CHUNK, CHUNK)
            lin = part[at, :] + dot(rest[at, :], rest_table)
            act, slope = activate(lin)
            act = act.astype(BF16)
            act_e[t, at, :] = act
            slope_e[t, at, :] = slope
            xhat, inv = normalized(dot(act, es[t]))
            xhat_e[t, at, :] = xhat
            inv_e[t, at, :] = inv
            new = (rest[at, 128:256].astype(F32) + xhat * gain).astype(BF16)
            edge_new[at, :] = new
        summed = dot(spread[384:640, :], edge_new[...]).astype(BF16)
        if t + 1 < STEPS:
            rest[:, 128:256] = edge_new[...]
        node_in[t, :, 0:128] = h
        node_in[t, :, 128:256] = summed
        act, slope = activate(dot(node_in[t], nf[t]) + nb[t : t + 1, :])
        act = act.astype(BF16)
        act_n[t] = act
        slope_n[t] = slope
        xhat, inv = normalized(dot(act, ns[t]))
        xhat_n[t] = xhat
        inv_n[t] = inv
        if t + 1 < STEPS:
            new_h = (h.astype(F32) + xhat * ng[t : t + 1, :]).astype(BF16)
            h1[...] = new_h
            halo_out[t + 1] = dot(halo_pick, new_h).astype(BF16)
            exchange_start(t + 1)

    def reduce_start(t):
        def send(k, _):
            j = lax.rem(me1 + k, g1)
            pltpu.make_async_remote_copy(
                src_ref=grads.at[t, pl.ds(pl.multiple_of(j * unit, unit), unit)],
                dst_ref=got1.at[t, k],
                send_sem=red_ssem.at[t, 0],
                recv_sem=red_rsem.at[t, 0],
                device_id=peer1(j),
                device_id_type=MESH,
            ).start()
            return 0

        lax.fori_loop(1, g1, send, 0)

    def reduce_middle(t):
        others = got1.at[t, pl.ds(1, g1 - 1)]
        pltpu.make_async_copy(others, others, red_rsem.at[t, 0]).wait()
        acc = grads[t, pl.ds(pl.multiple_of(me1 * unit, unit), unit), :].astype(F32)
        for k in range(1, g1):
            acc = acc + got1[t, k].astype(F32)
        acc = acc.astype(BF16)
        mid[t] = acc
        got2[t, me2] = acc

        def send(k, _):
            j = lax.rem(me2 + k, g2)
            pltpu.make_async_remote_copy(
                src_ref=mid.at[t],
                dst_ref=got2.at[t, me2],
                send_sem=red_ssem.at[t, 1],
                recv_sem=red_rsem.at[t, 1],
                device_id=peer2(j),
                device_id_type=MESH,
            ).start()
            return 0

        lax.fori_loop(1, g2, send, 0)

    def reduce_last(t):
        others = got2.at[t, pl.ds(1, g2 - 1)]
        pltpu.make_async_copy(others, others, red_rsem.at[t, 1]).wait()
        acc = got2[t, 0].astype(F32)
        for k in range(1, g2):
            acc = acc + got2[t, k].astype(F32)
        scale = jnp.float32(NODES * n_sector * n_span) ** (-0.5)
        mine = pl.ds(pl.multiple_of(me1 * unit, unit), unit)
        total[t, mine, :] = (acc * scale).astype(BF16)

        def send(k, _):
            j = lax.rem(me1 + k, g1)
            pltpu.make_async_remote_copy(
                src_ref=total.at[t, mine],
                dst_ref=total.at[t, mine],
                send_sem=red_ssem.at[t, 2],
                recv_sem=red_rsem.at[t, 2],
                device_id=peer1(j),
                device_id_type=MESH,
            ).start()
            return 0

        lax.fori_loop(1, g1, send, 0)

    def reduce_finish(t):
        others = total.at[t, pl.ds(unit, ROWS - unit)]
        pltpu.make_async_copy(others, others, red_rsem.at[t, 2]).wait()
        for ref, start, count in ((o_ef, AT_EF, 384), (o_es, AT_ES, 128), (o_nf, AT_NF, 256), (o_ns, AT_NS, 128)):
            ref[t] = total[t, start : start + count, :].astype(F32)
        small = total[t, AT_SMALL : AT_SMALL + 16, :].astype(F32)
        o_eb[t : t + 1, :] = small[0:1, :]
        o_eg[t : t + 1, :] = small[1:2, :]
        o_nb[t : t + 1, :] = small[2:3, :]
        o_ng[t : t + 1, :] = small[3:4, :]

    def reduce_sent(t):
        for phase, ref, count in ((0, got1, g1), (1, got2, g2), (2, got1, g1)):
            sent = ref.at[t, pl.ds(1, count - 1)]
            pltpu.make_async_copy(sent, sent, red_ssem.at[t, phase]).wait()

    def backward(t):
        last = t + 1 == STEPS
        h = nodes[...] if t == 0 else h1[...]
        dy = cot[...].astype(F32) if last else dh[...]
        dproj_n, dgain_n = normalized_back(dy, xhat_n[t], inv_n[t], ng[t : t + 1, :])
        dproj_n = dproj_n.astype(BF16)
        dlin_n = dot_last(dproj_n, ns[t]) * slope_n[t]
        dbias_n = jnp.sum(dlin_n, axis=0, keepdims=True)
        dlin_n = dlin_n.astype(BF16)
        dsummed = dot_last(dlin_n, nf[t, 128:256, :]).astype(BF16)
        dgain_e = jnp.zeros((1, D), F32)
        gain = eg[t : t + 1, :]
        for i in range(SLOTS // CHUNK):
            at = pl.ds(i * CHUNK, CHUNK)
            dnew = dot(own_pick[at, 256:512], dsummed)
            if not last:
                dnew = dnew + de[at, :]
            dp, dg = normalized_back(dnew, xhat_e[t, at, :], inv_e[t, at, :], gain)
            dgain_e = dgain_e + dg
            dp = dp.astype(BF16)
            dproj[at, :] = dp
            dl = (dot_last(dp, es[t]) * slope_e[t, at, :]).astype(BF16)
            dlin[at, :] = dl
            dold = dnew + dot_last(dl, ef[t, 256:384, :])
            if last:
                de[at, :] = dold
            else:
                edge_grad[at, :] = dold.astype(BF16)
        sums = dot(spread[...], dlin[...])
        sums_b = sums.astype(BF16)
        dbias_e = jnp.sum(sums[384:640], axis=0, keepdims=True)
        dhalo = dot_last(sums_b[256:384], ef[t, 0:128, :])
        halo_out[STEPS + t] = jnp.where(outside, 0.0, dhalo).astype(BF16)
        exchange_start(STEPS + t)
        grads[t, AT_EF : AT_EF + 128, :] = (
            dot_first(h, sums_b[0:256]) + dot_first(halo_in[t], sums_b[256:384])
        ).astype(BF16)
        grads[t, AT_EF + 128 : AT_EF + 256, :] = dot_first(h, sums_b[384:640]).astype(BF16)
        old = edges[...] if t == 0 else rest[:, 128:256]
        grads[t, AT_EF + 256 : AT_EF + 384, :] = dot_first(old, dlin[...]).astype(BF16)
        grads[t, AT_ES : AT_ES + 128, :] = dot_first(act_e[t], dproj[...]).astype(BF16)
        grads[t, AT_NF : AT_NF + 256, :] = dot_first(node_in[t], dlin_n).astype(BF16)
        grads[t, AT_NS : AT_NS + 128, :] = dot_first(act_n[t], dproj_n).astype(BF16)
        grads[t, AT_SMALL : AT_SMALL + 128, :] = jnp.concatenate(
            [dbias_e, dgain_e, dbias_n, dgain_n, jnp.zeros((124, D), F32)], axis=0
        ).astype(BF16)
        reduce_start(t)
        own = (
            dy
            + dot_last(dlin_n, nf[t, 0:128, :])
            + dot_last(sums_b[0:256], ef[t, 0:128, :])
            + dot_last(sums_b[384:640], ef[t, 128:256, :])
        )
        exchange_wait(STEPS + t)
        own = (own + dot(halo_spread, halo_in[STEPS + t])).astype(BF16)
        if t == 0:
            node_grad[...] = own
        else:
            dh[...] = own.astype(F32)

    forward(0)
    forward(1)
    backward(1)
    reduce_middle(1)
    backward(0)
    reduce_last(1)
    reduce_middle(0)
    reduce_finish(1)
    reduce_last(0)
    reduce_finish(0)
    for t in range(STEPS):
        reduce_sent(t)
    for t in range(2 * STEPS):
        pltpu.make_async_copy(halo_out.at[t], halo_out.at[t], halo_ssem.at[t]).wait()


def per_device(
    node_latents, edge_latents, senders, receivers, halo_rows, counts, cotangent,
    edge_first, edge_bias, edge_second, edge_gain, node_first, node_bias, node_second, node_gain,
):
    g1, g2 = ZH * X * C, Y * ZL
    unit = ROWS // g1
    vmem, smem = pl.BlockSpec(memory_space=pltpu.VMEM), pl.BlockSpec(memory_space=pltpu.SMEM)
    weights = (edge_first, edge_bias, edge_second, edge_gain, node_first, node_bias, node_second, node_gain)
    return pl.pallas_call(
        kernel,
        out_shape=(
            jax.ShapeDtypeStruct((NODES, D), BF16),
            jax.ShapeDtypeStruct((SLOTS, D), BF16),
            *(jax.ShapeDtypeStruct(w.shape, F32) for w in weights),
        ),
        in_specs=[vmem] * 5 + [smem] + [vmem] * 9,
        out_specs=[vmem] * 10,
        scratch_shapes=[
            pltpu.VMEM((SLOTS, 512), BF16),
            pltpu.VMEM((SLOTS, 256), BF16),
            pltpu.VMEM((640, SLOTS), BF16),
            pltpu.VMEM((8, D), F32),
            pltpu.VMEM((NODES, D), BF16),
            pltpu.VMEM((SLOTS, D), F32),
            pltpu.VMEM((STEPS, SLOTS, D), BF16),
            pltpu.VMEM((STEPS, SLOTS, D), F32),
            pltpu.VMEM((STEPS, SLOTS, D), F32),
            pltpu.VMEM((STEPS, SLOTS, 1), F32),
            pltpu.VMEM((STEPS, NODES, D), BF16),
            pltpu.VMEM((STEPS, NODES, D), F32),
            pltpu.VMEM((STEPS, NODES, D), F32),
            pltpu.VMEM((STEPS, NODES, 1), F32),
            pltpu.VMEM((STEPS, NODES, 256), BF16),
            pltpu.VMEM((SLOTS, D), BF16),
            pltpu.VMEM((SLOTS, D), F32),
            pltpu.VMEM((SLOTS, D), BF16),
            pltpu.VMEM((SLOTS, D), BF16),
            pltpu.VMEM((NODES, D), F32),
            pltpu.VMEM((2 * STEPS, 4 * HALO, D), BF16),
            pltpu.VMEM((2 * STEPS, 4 * HALO, D), BF16),
            pltpu.VMEM((STEPS, ROWS, D), BF16),
            pltpu.VMEM((STEPS, g1, unit, D), BF16),
            pltpu.VMEM((STEPS, g2, unit, D), BF16),
            pltpu.VMEM((STEPS, unit, D), BF16),
            pltpu.VMEM((STEPS, ROWS, D), BF16),
            pltpu.SemaphoreType.DMA((2 * STEPS,)),
            pltpu.SemaphoreType.DMA((2 * STEPS,)),
            pltpu.SemaphoreType.DMA((STEPS, 3)),
            pltpu.SemaphoreType.DMA((STEPS, 3)),
        ],
        compiler_params=pltpu.CompilerParams(
            collective_id=0, has_side_effects=True, vmem_limit_bytes=40 * 1024 * 1024
        ),
    )(
        node_latents, edge_latents, senders.reshape(SLOTS // D, D), receivers.reshape(SLOTS // D, D),
        halo_rows, counts, cotangent, *weights,
    )


def solution(mesh):
    tile = P(("sector", "span"))
    rows = P(("sector", "span"), None)
    return jax.shard_map(
        per_device,
        mesh=mesh,
        in_specs=(rows, rows, tile, tile, P(("sector", "span"), None, None), tile, rows) + (P(),) * 8,
        out_specs=(rows, rows) + (P(),) * 8,
        check_vma=False,
    )
```

```python
import jax
import jax.numpy as jnp
from jax import lax
from jax.experimental import pallas as pl
from jax.experimental.pallas import tpu as pltpu
from jax.sharding import PartitionSpec as P

F32, BF16 = jnp.float32, jnp.bfloat16
MESH = pl.DeviceIdType.MESH
STEPS = 2
EPS = 1e-05
YH, YL, ZH, C, X, ZL = 4, 2, 4, 2, 4, 2
NODES, SLOTS, D, HALO = 256, 1024, 128, 32
CHUNK = 256
AT_EF, AT_ES, AT_NF, AT_NS, AT_SMALL, ROWS = 0, 384, 512, 768, 896, 1024


def dot(a, b):
    return jnp.dot(a, b, preferred_element_type=F32)


def dot_first(a, b):
    return lax.dot_general(a, b, (((0,), (0,)), ((), ())), preferred_element_type=F32)


def dot_last(a, b):
    return lax.dot_general(a, b, (((1,), (1,)), ((), ())), preferred_element_type=F32)


def ones_where(mask):
    return jnp.where(mask, 1.0, 0.0).astype(BF16)


def activate(lin):
    sig = 0.5 * jnp.tanh(0.5 * lin) + 0.5
    act = lin * sig
    return act, sig + act * (1.0 - sig)


def normalized(proj):
    mean = jnp.mean(proj, axis=-1, keepdims=True)
    centred = proj - mean
    var = jnp.mean(centred * centred, axis=-1, keepdims=True)
    inv = lax.rsqrt(var + EPS)
    return centred * inv, inv


def normalized_back(dout, xhat, inv, gain):
    prod = dout * xhat
    dx = dout * gain
    mean = jnp.mean(dx, axis=-1, keepdims=True)
    along = jnp.mean(prod * gain, axis=-1, keepdims=True)
    return inv * (dx - mean - xhat * along), jnp.sum(prod, axis=0, keepdims=True)


def kernel(
    *refs,
):
    sources, counts, outs, here, refs = refs[:5] + refs[6:15], refs[5], refs[15:18], refs[18:32], refs[32:]
    nodes, edges, snd, rcv, halo, cot, ef, eb, es, eg, nf, nb, ns, ng = here
    node_grad, edge_grad, total = outs
    (
    own_pick, rest, spread, hal_pad, h1, part, act_e, slope_e, xhat_e, inv_e, act_n, slope_n, xhat_n, inv_n,
    node_in, edge_new, de, dlin, dproj, dh,
    halo_out, halo_in, grads, got1, got2, mid,
    in_sem, halo_ssem, halo_rsem, red_ssem, red_rsem,
    ) = refs
    sector, span = lax.axis_index("sector"), lax.axis_index("span")
    n_sector, n_span = YH * YL * ZH * C, X * ZL
    yh, yl = sector // (YL * ZH * C), lax.rem(sector // (ZH * C), YL)
    zh, c = lax.rem(sector // C, ZH), lax.rem(sector, C)
    x, zl = span // ZL, lax.rem(span, ZL)
    g1, g2 = YL * ZL * X * C, YH * ZH
    me1, me2 = ((yl * ZL + zl) * X + x) * C + c, yh * ZH + zh
    unit = ROWS // g1

    def peer1(j):
        py, pz = j // (ZL * X * C), lax.rem(j // (X * C), ZL)
        return (((yh * YL + py) * ZH + zh) * C + lax.rem(j, C), lax.rem(j // C, X) * ZL + pz)

    def peer2(j):
        return (((j // ZH * YL + yl) * ZH + lax.rem(j, ZH)) * C + c, span)

    around = (
        (lax.rem(sector + n_sector - 1, n_sector), span),
        (lax.rem(sector + 1, n_sector), span),
        (sector, lax.rem(span + n_span - 1, n_span)),
        (sector, lax.rem(span + 1, n_span)),
    )

    barrier = pltpu.get_barrier_semaphore()
    for peer in around:
        pl.semaphore_signal(barrier, inc=1, device_id=peer, device_id_type=MESH)

    def greet1(k, _):
        pl.semaphore_signal(barrier, inc=1, device_id=peer1(lax.rem(me1 + k, g1)), device_id_type=MESH)
        return 0

    def greet2(k, _):
        pl.semaphore_signal(barrier, inc=1, device_id=peer2(lax.rem(me2 + k, g2)), device_id_type=MESH)
        return 0

    lax.fori_loop(1, g1, greet1, 0)
    lax.fori_loop(1, g2, greet2, 0)

    loads = [pltpu.make_async_copy(a, b, in_sem.at[i]) for i, (a, b) in enumerate(zip(sources, here))]
    first = (4, 0, 2, 3, 1)
    rest_loads = [i for i in range(14) if i not in first]
    for i in (*first, *rest_loads):
        loads[i].start()
    loads[4].wait()
    loads[0].wait()

    hal_pad[...] = jnp.zeros_like(hal_pad)
    hal_pad[0:4, 0:HALO] = halo[0].astype(F32)
    padded = hal_pad[...]
    lane = lax.broadcasted_iota(jnp.int32, (1, D), 1)
    flat = jnp.zeros((1, D), F32)
    for k in range(4):
        row = padded[k : k + 1, :] if k == 0 else pltpu.roll(padded, HALO * k, 1)[k : k + 1, :]
        flat = jnp.where((lane >= HALO * k) & (lane < HALO * (k + 1)), row, flat)
    lane_f = lax.broadcasted_iota(jnp.int32, (D, D), 1).astype(F32)
    down = jnp.broadcast_to(flat, (D, D)).T
    halo_pick = jnp.concatenate([ones_where(down == lane_f), ones_where(down == lane_f + D)], axis=1)
    halo_spread = ones_where(lax.broadcasted_iota(jnp.int32, (NODES, D), 0).astype(F32) == flat)

    row_id = lax.broadcasted_iota(jnp.int32, (4 * HALO, 1), 0)
    outside = ((row_id >= 2 * HALO) & (row_id < 3 * HALO) & (span == 0)) | (
        (row_id >= 3 * HALO) & (span == n_span - 1)
    )

    def exchange_start(t):
        for k in range(4):
            pltpu.make_async_remote_copy(
                src_ref=halo_out.at[t, pl.ds(k * HALO, HALO)],
                dst_ref=halo_in.at[t, pl.ds((k ^ 1) * HALO, HALO)],
                send_sem=halo_ssem.at[t],
                recv_sem=halo_rsem.at[t],
                device_id=around[k],
                device_id_type=MESH,
            ).start()

    def exchange_wait(t):
        pltpu.make_async_copy(halo_in.at[t], halo_in.at[t], halo_rsem.at[t]).wait()

    halo_out[0] = dot(halo_pick, nodes[...]).astype(BF16)
    pl.semaphore_wait(barrier, 4 + g1 - 1 + g2 - 1)
    exchange_start(0)

    for i in first[2:]:
        loads[i].wait()
    used = counts[0]
    slot = lax.broadcasted_iota(jnp.int32, (SLOTS // D, D), 0) * D + lax.broadcasted_iota(
        jnp.int32, (SLOTS // D, D), 1
    )
    snd_f = jnp.where(slot < used, snd[...], -1).astype(F32)
    rcv_f = jnp.where(slot < used, rcv[...], -1).astype(F32)
    down_f = lax.broadcasted_iota(jnp.int32, (NODES + 4 * HALO, D), 0).astype(F32)
    for r in range(SLOTS // D):
        at = pl.ds(r * D, D)
        s_row, r_row = snd_f[r : r + 1, :], rcv_f[r : r + 1, :]
        spread[0:384, at] = ones_where(down_f == s_row)
        spread[384:640, at] = ones_where(down_f[0:256] == r_row)
        s_col = jnp.broadcast_to(s_row, (D, D)).T
        r_col = jnp.broadcast_to(r_row, (D, D)).T
        own_pick[at, 0:128] = ones_where(s_col == lane_f)
        own_pick[at, 128:256] = ones_where(s_col == lane_f + 128.0)
        own_pick[at, 256:384] = ones_where(r_col == lane_f)
        own_pick[at, 384:512] = ones_where(r_col == lane_f + 128.0)
        rest[at, 0:128] = ones_where(s_col == lane_f + 256.0)
    rest[:, 128:256] = edges[...]
    for i in rest_loads:
        loads[i].wait()

    def forward(t):
        h = nodes[...] if t == 0 else h1[...]
        own_table = jnp.concatenate(
            [dot(h, ef[t, 0:128, :]).astype(BF16), dot(h, ef[t, 128:256, :]).astype(BF16)], axis=0
        )
        bias, gain = eb[t : t + 1, :], eg[t : t + 1, :]
        for i in range(SLOTS // CHUNK):
            at = pl.ds(i * CHUNK, CHUNK)
            part[at, :] = dot(own_pick[at, :], own_table) + bias
        exchange_wait(t)
        halo_in[t] = jnp.where(outside, 0.0, halo_in[t].astype(F32)).astype(BF16)
        rest_table = jnp.concatenate(
            [dot(halo_in[t], ef[t, 0:128, :]).astype(BF16), ef[t, 256:384, :]], axis=0
        )
        for i in range(SLOTS // CHUNK):
            at = pl.ds(i * CHUNK, CHUNK)
            lin = part[at, :] + dot(rest[at, :], rest_table)
            act, slope = activate(lin)
            act = act.astype(BF16)
            act_e[t, at, :] = act
            slope_e[t, at, :] = slope
            xhat, inv = normalized(dot(act, es[t]))
            xhat_e[t, at, :] = xhat
            inv_e[t, at, :] = inv
            new = (rest[at, 128:256].astype(F32) + xhat * gain).astype(BF16)
            edge_new[at, :] = new
        summed = dot(spread[384:640, :], edge_new[...]).astype(BF16)
        if t + 1 < STEPS:
            rest[:, 128:256] = edge_new[...]
        node_in[t, :, 0:128] = h
        node_in[t, :, 128:256] = summed
        act, slope = activate(dot(node_in[t], nf[t]) + nb[t : t + 1, :])
        act = act.astype(BF16)
        act_n[t] = act
        slope_n[t] = slope
        xhat, inv = normalized(dot(act, ns[t]))
        xhat_n[t] = xhat
        inv_n[t] = inv
        if t + 1 < STEPS:
            new_h = (h.astype(F32) + xhat * ng[t : t + 1, :]).astype(BF16)
            h1[...] = new_h
            halo_out[t + 1] = dot(halo_pick, new_h).astype(BF16)
            exchange_start(t + 1)

    def reduce_start(t):
        def send(k, _):
            j = lax.rem(me1 + k, g1)
            pltpu.make_async_remote_copy(
                src_ref=grads.at[t, pl.ds(pl.multiple_of(j * unit, unit), unit)],
                dst_ref=got1.at[t, k],
                send_sem=red_ssem.at[t, 0],
                recv_sem=red_rsem.at[t, 0],
                device_id=peer1(j),
                device_id_type=MESH,
            ).start()
            return 0

        lax.fori_loop(1, g1, send, 0)

    def reduce_middle(t):
        others = got1.at[t, pl.ds(1, g1 - 1)]
        pltpu.make_async_copy(others, others, red_rsem.at[t, 0]).wait()
        acc = grads[t, pl.ds(pl.multiple_of(me1 * unit, unit), unit), :].astype(F32)
        for k in range(1, g1):
            acc = acc + got1[t, k].astype(F32)
        acc = acc.astype(BF16)
        mid[t] = acc
        got2[t, me2] = acc

        def send(k, _):
            j = lax.rem(me2 + k, g2)
            pltpu.make_async_remote_copy(
                src_ref=mid.at[t],
                dst_ref=got2.at[t, me2],
                send_sem=red_ssem.at[t, 1],
                recv_sem=red_rsem.at[t, 1],
                device_id=peer2(j),
                device_id_type=MESH,
            ).start()
            return 0

        lax.fori_loop(1, g2, send, 0)

    def reduce_last(t):
        others = got2.at[t, pl.ds(1, g2 - 1)]
        pltpu.make_async_copy(others, others, red_rsem.at[t, 1]).wait()
        acc = got2[t, 0].astype(F32)
        for k in range(1, g2):
            acc = acc + got2[t, k].astype(F32)
        scale = jnp.float32(NODES * n_sector * n_span) ** (-0.5)
        mine = pl.ds(pl.multiple_of(me1 * unit, unit), unit)
        total[t, mine, :] = (acc * scale).astype(BF16)

        def send(k, _):
            j = lax.rem(me1 + k, g1)
            pltpu.make_async_remote_copy(
                src_ref=total.at[t, mine],
                dst_ref=total.at[t, mine],
                send_sem=red_ssem.at[t, 2],
                recv_sem=red_rsem.at[t, 2],
                device_id=peer1(j),
                device_id_type=MESH,
            ).start()
            return 0

        lax.fori_loop(1, g1, send, 0)

    def reduce_finish(t):
        others = total.at[t, pl.ds(unit, ROWS - unit)]
        pltpu.make_async_copy(others, others, red_rsem.at[t, 2]).wait()

    def reduce_sent(t):
        for phase, ref, count in ((0, got1, g1), (1, got2, g2), (2, got1, g1)):
            sent = ref.at[t, pl.ds(1, count - 1)]
            pltpu.make_async_copy(sent, sent, red_ssem.at[t, phase]).wait()

    def backward(t):
        last = t + 1 == STEPS
        h = nodes[...] if t == 0 else h1[...]
        dy = cot[...].astype(F32) if last else dh[...]
        dproj_n, dgain_n = normalized_back(dy, xhat_n[t], inv_n[t], ng[t : t + 1, :])
        dproj_n = dproj_n.astype(BF16)
        dlin_n = dot_last(dproj_n, ns[t]) * slope_n[t]
        dbias_n = jnp.sum(dlin_n, axis=0, keepdims=True)
        dlin_n = dlin_n.astype(BF16)
        dsummed = dot_last(dlin_n, nf[t, 128:256, :]).astype(BF16)
        dgain_e = jnp.zeros((1, D), F32)
        gain = eg[t : t + 1, :]
        for i in range(SLOTS // CHUNK):
            at = pl.ds(i * CHUNK, CHUNK)
            dnew = dot(own_pick[at, 256:512], dsummed)
            if not last:
                dnew = dnew + de[at, :]
            dp, dg = normalized_back(dnew, xhat_e[t, at, :], inv_e[t, at, :], gain)
            dgain_e = dgain_e + dg
            dp = dp.astype(BF16)
            dproj[at, :] = dp
            dl = (dot_last(dp, es[t]) * slope_e[t, at, :]).astype(BF16)
            dlin[at, :] = dl
            dold = dnew + dot_last(dl, ef[t, 256:384, :])
            if last:
                de[at, :] = dold
            else:
                edge_grad[at, :] = dold.astype(BF16)
        sums = dot(spread[...], dlin[...])
        sums_b = sums.astype(BF16)
        dbias_e = jnp.sum(sums[384:640], axis=0, keepdims=True)

        def send_back():
            dhalo = dot_last(sums_b[256:384], ef[t, 0:128, :])
            halo_out[STEPS + t] = jnp.where(outside, 0.0, dhalo).astype(BF16)
            exchange_start(STEPS + t)

        if last:
            send_back()
        grads[t, AT_EF : AT_EF + 128, :] = (
            dot_first(h, sums_b[0:256]) + dot_first(halo_in[t], sums_b[256:384])
        ).astype(BF16)
        grads[t, AT_EF + 128 : AT_EF + 256, :] = dot_first(h, sums_b[384:640]).astype(BF16)
        old = edges[...] if t == 0 else rest[:, 128:256]
        grads[t, AT_EF + 256 : AT_EF + 384, :] = dot_first(old, dlin[...]).astype(BF16)
        grads[t, AT_ES : AT_ES + 128, :] = dot_first(act_e[t], dproj[...]).astype(BF16)
        grads[t, AT_NF : AT_NF + 256, :] = dot_first(node_in[t], dlin_n).astype(BF16)
        grads[t, AT_NS : AT_NS + 128, :] = dot_first(act_n[t], dproj_n).astype(BF16)
        grads[t, AT_SMALL : AT_SMALL + 128, :] = jnp.concatenate(
            [dbias_e, dgain_e, dbias_n, dgain_n, jnp.zeros((124, D), F32)], axis=0
        ).astype(BF16)
        if not last:
            reduce_start(t)
            send_back()
        own = (
            dy
            + dot_last(dlin_n, nf[t, 0:128, :])
            + dot_last(sums_b[0:256], ef[t, 0:128, :])
            + dot_last(sums_b[384:640], ef[t, 128:256, :])
        )
        if not last:
            reduce_middle(1)
        exchange_wait(STEPS + t)
        own = (own + dot(halo_spread, halo_in[STEPS + t])).astype(BF16)
        if last:
            reduce_start(t)
            dh[...] = own.astype(F32)
        else:
            node_grad[...] = own

    forward(0)
    forward(1)
    backward(1)
    backward(0)
    reduce_middle(0)
    reduce_last(1)
    reduce_last(0)
    reduce_finish(1)
    reduce_finish(0)
    for t in range(STEPS):
        reduce_sent(t)
    for t in range(2 * STEPS):
        pltpu.make_async_copy(halo_out.at[t], halo_out.at[t], halo_ssem.at[t]).wait()


def finish(node_grad, edge_grad, total, *refs):
    outs, wide, small, sem = refs[:10], refs[10], refs[11], refs[12]
    copies = [pltpu.make_async_copy(edge_grad, outs[1], sem.at[0]), pltpu.make_async_copy(node_grad, outs[0], sem.at[1])]
    for copy in copies:
        copy.start()
    big = ((2, AT_EF, 384), (4, AT_ES, 128), (6, AT_NF, 256), (8, AT_NS, 128))
    for out, start, count in big:
        wide[:, start : start + count, :] = total[:, start : start + count, :].astype(F32)
        copy = pltpu.make_async_copy(wide.at[:, pl.ds(start, count), :], outs[out], sem.at[out])
        copy.start()
        copies.append(copy)
    for k, out in enumerate((3, 5, 7, 9)):
        for t in range(STEPS):
            small[k, t : t + 1, :] = total[t, AT_SMALL : AT_SMALL + 16, :].astype(F32)[k : k + 1, :]
        copy = pltpu.make_async_copy(small.at[k], outs[out], sem.at[out])
        copy.start()
        copies.append(copy)
    for copy in copies:
        copy.wait()


def per_device(
    node_latents, edge_latents, senders, receivers, halo_rows, counts, cotangent,
    edge_first, edge_bias, edge_second, edge_gain, node_first, node_bias, node_second, node_gain,
):
    g1, g2 = YL * ZL * X * C, YH * ZH
    unit = ROWS // g1
    vmem, anywhere = pl.BlockSpec(memory_space=pltpu.VMEM), pl.BlockSpec(memory_space=pl.ANY)
    smem, hbm = pl.BlockSpec(memory_space=pltpu.SMEM), pl.BlockSpec(memory_space=pltpu.HBM)
    weights = (edge_first, edge_bias, edge_second, edge_gain, node_first, node_bias, node_second, node_gain)
    args = (
        node_latents, edge_latents, senders.reshape(SLOTS // D, D), receivers.reshape(SLOTS // D, D),
        halo_rows, counts, cotangent, *weights,
    )
    parts = pl.pallas_call(
        kernel,
        out_shape=(
            jax.ShapeDtypeStruct((NODES, D), BF16),
            jax.ShapeDtypeStruct((SLOTS, D), BF16),
            jax.ShapeDtypeStruct((STEPS, ROWS, D), BF16),
        ),
        in_specs=[smem if i == 5 else hbm for i in range(15)],
        out_specs=[vmem] * 3,
        scratch_shapes=[
            *(pltpu.VMEM(a.shape, a.dtype) for i, a in enumerate(args) if i != 5),
            pltpu.VMEM((SLOTS, 512), BF16),
            pltpu.VMEM((SLOTS, 256), BF16),
            pltpu.VMEM((640, SLOTS), BF16),
            pltpu.VMEM((8, D), F32),
            pltpu.VMEM((NODES, D), BF16),
            pltpu.VMEM((SLOTS, D), F32),
            pltpu.VMEM((STEPS, SLOTS, D), BF16),
            pltpu.VMEM((STEPS, SLOTS, D), F32),
            pltpu.VMEM((STEPS, SLOTS, D), F32),
            pltpu.VMEM((STEPS, SLOTS, 1), F32),
            pltpu.VMEM((STEPS, NODES, D), BF16),
            pltpu.VMEM((STEPS, NODES, D), F32),
            pltpu.VMEM((STEPS, NODES, D), F32),
            pltpu.VMEM((STEPS, NODES, 1), F32),
            pltpu.VMEM((STEPS, NODES, 256), BF16),
            pltpu.VMEM((SLOTS, D), BF16),
            pltpu.VMEM((SLOTS, D), F32),
            pltpu.VMEM((SLOTS, D), BF16),
            pltpu.VMEM((SLOTS, D), BF16),
            pltpu.VMEM((NODES, D), F32),
            pltpu.VMEM((2 * STEPS, 4 * HALO, D), BF16),
            pltpu.VMEM((2 * STEPS, 4 * HALO, D), BF16),
            pltpu.VMEM((STEPS, ROWS, D), BF16),
            pltpu.VMEM((STEPS, g1, unit, D), BF16),
            pltpu.VMEM((STEPS, g2, unit, D), BF16),
            pltpu.VMEM((STEPS, unit, D), BF16),
            pltpu.SemaphoreType.DMA((14,)),
            pltpu.SemaphoreType.DMA((2 * STEPS,)),
            pltpu.SemaphoreType.DMA((2 * STEPS,)),
            pltpu.SemaphoreType.DMA((STEPS, 3)),
            pltpu.SemaphoreType.DMA((STEPS, 3)),
        ],
        compiler_params=pltpu.CompilerParams(
            collective_id=0, has_side_effects=True, vmem_limit_bytes=40 * 1024 * 1024
        ),
        name="steps",
    )(*(a if i == 5 else pltpu.with_memory_space_constraint(a, pltpu.HBM) for i, a in enumerate(args)))
    return pl.pallas_call(
        finish,
        out_shape=(
            jax.ShapeDtypeStruct((NODES, D), BF16),
            jax.ShapeDtypeStruct((SLOTS, D), BF16),
            *(jax.ShapeDtypeStruct(w.shape, F32) for w in weights),
        ),
        in_specs=[vmem] * 3,
        out_specs=[anywhere] * 10,
        scratch_shapes=[
            pltpu.VMEM((STEPS, ROWS, D), F32),
            pltpu.VMEM((4, STEPS, D), F32),
            pltpu.SemaphoreType.DMA((10,)),
        ],
        compiler_params=pltpu.CompilerParams(vmem_limit_bytes=40 * 1024 * 1024),
        name="finish",
    )(*parts)


def solution(mesh):
    tile = P(("sector", "span"))
    rows = P(("sector", "span"), None)
    return jax.shard_map(
        per_device,
        mesh=mesh,
        in_specs=(rows, rows, tile, tile, P(("sector", "span"), None, None), tile, rows) + (P(),) * 8,
        out_specs=(rows, rows) + (P(),) * 8,
        check_vma=False,
    )
```

```python
import jax
import jax.numpy as jnp
from jax import lax
from jax.experimental import pallas as pl
from jax.experimental.pallas import tpu as pltpu
from jax.sharding import PartitionSpec as P

F32, BF16 = jnp.float32, jnp.bfloat16
MESH = pl.DeviceIdType.MESH
STEPS = 2
EPS = 1e-05
YH, YL, ZH, C, X, ZL = 4, 2, 4, 2, 4, 2
NODES, SLOTS, D, HALO = 256, 1024, 128, 32
CHUNK = 256
STEP1, NODE0, EDGE0 = 0, 1, 2
ROWS = (1024, 512, 512)
BASE = (0, 1024, 1536)
SMALL = (896, 384)


def dot(a, b):
    return jnp.dot(a, b, preferred_element_type=F32)


def dot_first(a, b):
    return lax.dot_general(a, b, (((0,), (0,)), ((), ())), preferred_element_type=F32)


def dot_last(a, b):
    return lax.dot_general(a, b, (((1,), (1,)), ((), ())), preferred_element_type=F32)


def ones_where(mask):
    return jnp.where(mask, 1.0, 0.0).astype(BF16)


def activate(lin):
    sig = 0.5 * jnp.tanh(0.5 * lin) + 0.5
    act = lin * sig
    return act, sig + act * (1.0 - sig)


def normalized(proj):
    mean = jnp.mean(proj, axis=-1, keepdims=True)
    centred = proj - mean
    var = jnp.mean(centred * centred, axis=-1, keepdims=True)
    inv = lax.rsqrt(var + EPS)
    return centred * inv, inv


def normalized_back(dout, xhat, inv, gain):
    prod = dout * xhat
    dx = dout * gain
    mean = jnp.mean(dx, axis=-1, keepdims=True)
    along = jnp.mean(prod * gain, axis=-1, keepdims=True)
    return inv * (dx - mean - xhat * along), jnp.sum(prod, axis=0, keepdims=True)


def kernel(
    *refs,
):
    sources, counts, outs, here, refs = refs[:5] + refs[6:15], refs[5], refs[15:18], refs[18:32], refs[32:]
    nodes, edges, snd, rcv, halo, cot, ef, eb, es, eg, nf, nb, ns, ng = here
    node_grad, edge_grad, total = outs
    (
    own_pick, rest, spread, hal_pad, h1, part, act_e, slope_e, xhat_e, inv_e, act_n, slope_n, xhat_n, inv_n,
    node_in, edge_new, de, dlin, dproj, dh,
    halo_out, halo_in, grads, mid, got1_a, got1_b, got1_c, got2_a, got2_b, got2_c,
    in_sem, halo_ssem, halo_rsem, red_ssem, red_rsem, ready,
    ) = refs
    sector, span = lax.axis_index("sector"), lax.axis_index("span")
    n_sector, n_span = YH * YL * ZH * C, X * ZL
    yh, yl = sector // (YL * ZH * C), lax.rem(sector // (ZH * C), YL)
    zh, c = lax.rem(sector // C, ZH), lax.rem(sector, C)
    x, zl = span // ZL, lax.rem(span, ZL)
    g1, g2 = YL * ZL * X * C, YH * ZH
    me1, me2 = ((yl * ZL + zl) * X + x) * C + c, yh * ZH + zh
    units = tuple(n // g1 for n in ROWS)
    got1, got2 = (got1_a, got1_b, got1_c), (got2_a, got2_b, got2_c)

    def peer1(j):
        py, pz = j // (ZL * X * C), lax.rem(j // (X * C), ZL)
        return (((yh * YL + py) * ZH + zh) * C + lax.rem(j, C), lax.rem(j // C, X) * ZL + pz)

    def peer2(j):
        return (((j // ZH * YL + yl) * ZH + lax.rem(j, ZH)) * C + c, span)

    around = (
        (lax.rem(sector + n_sector - 1, n_sector), span),
        (lax.rem(sector + 1, n_sector), span),
        (sector, lax.rem(span + n_span - 1, n_span)),
        (sector, lax.rem(span + 1, n_span)),
    )

    barrier = pltpu.get_barrier_semaphore()
    for peer in around:
        pl.semaphore_signal(barrier, inc=1, device_id=peer, device_id_type=MESH)

    def greet1(k, _):
        pl.semaphore_signal(barrier, inc=1, device_id=peer1(lax.rem(me1 + k, g1)), device_id_type=MESH)
        return 0

    lax.fori_loop(1, g1, greet1, 0)
    lines = [peer2(lax.rem(yh + k, YH) * ZH + zh) for k in range(1, YH)]
    for peer in lines + [peer2(yh * ZH + lax.rem(zh + k, ZH)) for k in range(1, ZH)]:
        pl.semaphore_signal(barrier, inc=1, device_id=peer, device_id_type=MESH)

    loads = [pltpu.make_async_copy(a, b, in_sem.at[i]) for i, (a, b) in enumerate(zip(sources, here))]
    first = (4, 0, 2, 3, 1)
    rest_loads = [i for i in range(14) if i not in first]
    for i in (*first, *rest_loads):
        loads[i].start()
    loads[4].wait()
    loads[0].wait()

    hal_pad[...] = jnp.zeros_like(hal_pad)
    hal_pad[0:4, 0:HALO] = halo[0].astype(F32)
    padded = hal_pad[...]
    lane = lax.broadcasted_iota(jnp.int32, (1, D), 1)
    flat = jnp.zeros((1, D), F32)
    for k in range(4):
        row = padded[k : k + 1, :] if k == 0 else pltpu.roll(padded, HALO * k, 1)[k : k + 1, :]
        flat = jnp.where((lane >= HALO * k) & (lane < HALO * (k + 1)), row, flat)
    lane_f = lax.broadcasted_iota(jnp.int32, (D, D), 1).astype(F32)
    down = jnp.broadcast_to(flat, (D, D)).T
    halo_pick = jnp.concatenate([ones_where(down == lane_f), ones_where(down == lane_f + D)], axis=1)
    halo_spread = ones_where(lax.broadcasted_iota(jnp.int32, (NODES, D), 0).astype(F32) == flat)

    row_id = lax.broadcasted_iota(jnp.int32, (4 * HALO, 1), 0)
    outside = ((row_id >= 2 * HALO) & (row_id < 3 * HALO) & (span == 0)) | (
        (row_id >= 3 * HALO) & (span == n_span - 1)
    )

    def exchange_start(t):
        for k in range(4):
            pltpu.make_async_remote_copy(
                src_ref=halo_out.at[t, pl.ds(k * HALO, HALO)],
                dst_ref=halo_in.at[t, pl.ds((k ^ 1) * HALO, HALO)],
                send_sem=halo_ssem.at[t],
                recv_sem=halo_rsem.at[t],
                device_id=around[k],
                device_id_type=MESH,
            ).start()

    def exchange_wait(t):
        pltpu.make_async_copy(halo_in.at[t], halo_in.at[t], halo_rsem.at[t]).wait()

    halo_out[0] = dot(halo_pick, nodes[...]).astype(BF16)
    pl.semaphore_wait(barrier, 4 + g1 - 1 + YH - 1 + ZH - 1)
    exchange_start(0)
    for peer in lines:
        pl.semaphore_signal(ready, inc=1, device_id=peer, device_id_type=MESH)

    for i in first[2:]:
        loads[i].wait()
    used = counts[0]
    slot = lax.broadcasted_iota(jnp.int32, (SLOTS // D, D), 0) * D + lax.broadcasted_iota(
        jnp.int32, (SLOTS // D, D), 1
    )
    snd_f = jnp.where(slot < used, snd[...], -1).astype(F32)
    rcv_f = jnp.where(slot < used, rcv[...], -1).astype(F32)
    down_f = lax.broadcasted_iota(jnp.int32, (NODES + 4 * HALO, D), 0).astype(F32)
    for r in range(SLOTS // D):
        at = pl.ds(r * D, D)
        s_row, r_row = snd_f[r : r + 1, :], rcv_f[r : r + 1, :]
        spread[0:384, at] = ones_where(down_f == s_row)
        spread[384:640, at] = ones_where(down_f[0:256] == r_row)
        s_col = jnp.broadcast_to(s_row, (D, D)).T
        r_col = jnp.broadcast_to(r_row, (D, D)).T
        own_pick[at, 0:128] = ones_where(s_col == lane_f)
        own_pick[at, 128:256] = ones_where(s_col == lane_f + 128.0)
        own_pick[at, 256:384] = ones_where(r_col == lane_f)
        own_pick[at, 384:512] = ones_where(r_col == lane_f + 128.0)
        rest[at, 0:128] = ones_where(s_col == lane_f + 256.0)
    rest[:, 128:256] = edges[...]
    for i in rest_loads:
        loads[i].wait()

    def forward(t):
        h = nodes[...] if t == 0 else h1[...]
        own_table = jnp.concatenate(
            [dot(h, ef[t, 0:128, :]).astype(BF16), dot(h, ef[t, 128:256, :]).astype(BF16)], axis=0
        )
        bias, gain = eb[t : t + 1, :], eg[t : t + 1, :]
        for i in range(SLOTS // CHUNK):
            at = pl.ds(i * CHUNK, CHUNK)
            part[at, :] = dot(own_pick[at, :], own_table) + bias
        exchange_wait(t)
        halo_in[t] = jnp.where(outside, 0.0, halo_in[t].astype(F32)).astype(BF16)
        rest_table = jnp.concatenate(
            [dot(halo_in[t], ef[t, 0:128, :]).astype(BF16), ef[t, 256:384, :]], axis=0
        )
        for i in range(SLOTS // CHUNK):
            at = pl.ds(i * CHUNK, CHUNK)
            lin = part[at, :] + dot(rest[at, :], rest_table)
            act, slope = activate(lin)
            act = act.astype(BF16)
            act_e[t, at, :] = act
            slope_e[t, at, :] = slope
            xhat, inv = normalized(dot(act, es[t]))
            xhat_e[t, at, :] = xhat
            inv_e[t, at, :] = inv
            new = (rest[at, 128:256].astype(F32) + xhat * gain).astype(BF16)
            edge_new[at, :] = new
        summed = dot(spread[384:640, :], edge_new[...]).astype(BF16)
        if t + 1 < STEPS:
            rest[:, 128:256] = edge_new[...]
        node_in[t, :, 0:128] = h
        node_in[t, :, 128:256] = summed
        act, slope = activate(dot(node_in[t], nf[t]) + nb[t : t + 1, :])
        act = act.astype(BF16)
        act_n[t] = act
        slope_n[t] = slope
        xhat, inv = normalized(dot(act, ns[t]))
        xhat_n[t] = xhat
        inv_n[t] = inv
        if t + 1 < STEPS:
            new_h = (h.astype(F32) + xhat * ng[t : t + 1, :]).astype(BF16)
            h1[...] = new_h
            halo_out[t + 1] = dot(halo_pick, new_h).astype(BF16)
            exchange_start(t + 1)

    def reduce_start(i, held=None, only=None):
        unit = units[i]

        def copy(j):
            pltpu.make_async_remote_copy(
                src_ref=grads.at[pl.ds(pl.multiple_of(BASE[i] + j * unit, unit), unit)],
                dst_ref=got1[i].at[me1],
                send_sem=red_ssem.at[i, 0],
                recv_sem=red_rsem.at[i, 0],
                device_id=peer1(j),
                device_id_type=MESH,
            ).start()

        def send(k, _):
            j = lax.rem(me1 + k, g1)
            if held is None:
                copy(j)
            else:
                pl.when(j != held)(lambda: copy(j))
            return 0

        if only is None:
            lax.fori_loop(1, g1, send, 0)
        else:
            pl.when(me1 != only)(lambda: copy(only))

    def reduce_middle(i):
        unit = units[i]
        others = got1[i].at[pl.ds(1, g1 - 1)]
        pltpu.make_async_copy(others, others, red_rsem.at[i, 0]).wait()
        got1[i][me1] = grads[pl.ds(pl.multiple_of(BASE[i] + me1 * unit, unit), unit), :]
        acc = got1[i][0].astype(F32)
        for k in range(1, g1):
            acc = acc + got1[i][k].astype(F32)
        acc = acc.astype(BF16)
        block = pl.ds(BASE[i] // g1, unit)
        mid[block, :] = acc
        got2[i][me2] = acc

        def send(k, _):
            j = lax.rem(me2 + k, g2)
            pltpu.make_async_remote_copy(
                src_ref=mid.at[block],
                dst_ref=got2[i].at[me2],
                send_sem=red_ssem.at[i, 1],
                recv_sem=red_rsem.at[i, 1],
                device_id=peer2(j),
                device_id_type=MESH,
            ).start()
            return 0

        lax.fori_loop(1, g2, send, 0)

    def reduce_last(i):
        unit = units[i]
        others = got2[i].at[pl.ds(1, g2 - 1)]
        pltpu.make_async_copy(others, others, red_rsem.at[i, 1]).wait()
        acc = got2[i][0].astype(F32)
        for k in range(1, g2):
            acc = acc + got2[i][k].astype(F32)
        scale = jnp.float32(NODES * n_sector * n_span) ** (-0.5)
        mine = pl.ds(pl.multiple_of(BASE[i] + me1 * unit, unit), unit)
        total[mine, :] = (acc * scale).astype(BF16)

        def send(k, _):
            j = lax.rem(me1 + k, g1)
            pltpu.make_async_remote_copy(
                src_ref=total.at[mine],
                dst_ref=total.at[mine],
                send_sem=red_ssem.at[i, 2],
                recv_sem=red_rsem.at[i, 2],
                device_id=peer1(j),
                device_id_type=MESH,
            ).start()
            return 0

        lax.fori_loop(1, g1, send, 0)

    def reduce_finish(i):
        others = total.at[pl.ds(BASE[i], ROWS[i] - units[i])]
        pltpu.make_async_copy(others, others, red_rsem.at[i, 2]).wait()

    def reduce_sent(i):
        for phase, ref, count in ((0, got1[i], g1), (1, got2[i], g2), (2, got1[i], g1)):
            sent = ref.at[pl.ds(1, count - 1)]
            pltpu.make_async_copy(sent, sent, red_ssem.at[i, phase]).wait()

    def backward(t):
        last = t + 1 == STEPS
        h = nodes[...] if t == 0 else h1[...]
        dy = cot[...].astype(F32) if last else dh[...]
        dproj_n, dgain_n = normalized_back(dy, xhat_n[t], inv_n[t], ng[t : t + 1, :])
        dproj_n = dproj_n.astype(BF16)
        dlin_n = dot_last(dproj_n, ns[t]) * slope_n[t]
        dbias_n = jnp.sum(dlin_n, axis=0, keepdims=True)
        dlin_n = dlin_n.astype(BF16)
        dsummed = dot_last(dlin_n, nf[t, 128:256, :]).astype(BF16)
        node_at = BASE[STEP1] + 512 if last else BASE[NODE0]
        small_at = BASE[STEP1] + SMALL[STEP1] if last else BASE[NODE0] + SMALL[NODE0]
        held = SMALL[NODE0] // units[NODE0]

        def node_grads():
            grads[node_at : node_at + 256, :] = dot_first(node_in[t], dlin_n).astype(BF16)
            grads[node_at + 256 : node_at + 384, :] = dot_first(act_n[t], dproj_n).astype(BF16)

        small_rows = 128 if last else units[NODE0]
        if not last:
            node_grads()
            if small_rows < 128:
                grads[small_at + small_rows : small_at + 128, :] = jnp.zeros((128 - small_rows, D), BF16)
            reduce_start(NODE0, held=held)
        dgain_e = jnp.zeros((1, D), F32)
        gain = eg[t : t + 1, :]
        for i in range(SLOTS // CHUNK):
            at = pl.ds(i * CHUNK, CHUNK)
            dnew = dot(own_pick[at, 256:512], dsummed)
            if not last:
                dnew = dnew + de[at, :]
            dp, dg = normalized_back(dnew, xhat_e[t, at, :], inv_e[t, at, :], gain)
            dgain_e = dgain_e + dg
            dp = dp.astype(BF16)
            dproj[at, :] = dp
            dl = (dot_last(dp, es[t]) * slope_e[t, at, :]).astype(BF16)
            dlin[at, :] = dl
            dold = dnew + dot_last(dl, ef[t, 256:384, :])
            if last:
                de[at, :] = dold
            else:
                edge_grad[at, :] = dold.astype(BF16)
        sums = dot(spread[...], dlin[...])
        sums_b = sums.astype(BF16)
        dbias_e = jnp.sum(sums[384:640], axis=0, keepdims=True)

        def send_back():
            dhalo = dot_last(sums_b[256:384], ef[t, 0:128, :])
            halo_out[STEPS + t] = jnp.where(outside, 0.0, dhalo).astype(BF16)
            exchange_start(STEPS + t)

        edge_at = BASE[STEP1] if last else BASE[EDGE0]
        if last:
            send_back()
        grads[edge_at : edge_at + 128, :] = (
            dot_first(h, sums_b[0:256]) + dot_first(halo_in[t], sums_b[256:384])
        ).astype(BF16)
        grads[edge_at + 128 : edge_at + 256, :] = dot_first(h, sums_b[384:640]).astype(BF16)
        old = edges[...] if t == 0 else rest[:, 128:256]
        grads[edge_at + 256 : edge_at + 384, :] = dot_first(old, dlin[...]).astype(BF16)
        grads[edge_at + 384 : edge_at + 512, :] = dot_first(act_e[t], dproj[...]).astype(BF16)
        grads[small_at : small_at + small_rows, :] = jnp.concatenate(
            [dbias_e, dgain_e, dbias_n, dgain_n, jnp.zeros((small_rows - 4, D), F32)], axis=0
        ).astype(BF16)
        if last:
            node_grads()
            reduce_start(STEP1)
        else:
            reduce_start(EDGE0)
            reduce_start(NODE0, only=held)
            send_back()
        own = (
            dy
            + dot_last(dlin_n, nf[t, 0:128, :])
            + dot_last(sums_b[0:256], ef[t, 0:128, :])
            + dot_last(sums_b[384:640], ef[t, 128:256, :])
        )
        if not last:
            pl.semaphore_wait(ready, YH - 1)
            reduce_middle(STEP1)
            reduce_middle(NODE0)
        exchange_wait(STEPS + t)
        own = (own + dot(halo_spread, halo_in[STEPS + t])).astype(BF16)
        if last:
            dh[...] = own.astype(F32)
        else:
            node_grad[...] = own

    forward(0)
    forward(1)
    backward(1)
    backward(0)
    reduce_middle(EDGE0)
    for i in (STEP1, NODE0, EDGE0):
        reduce_last(i)
    for i in (STEP1, NODE0, EDGE0):
        reduce_finish(i)
    for i in (STEP1, NODE0, EDGE0):
        reduce_sent(i)
    for t in range(2 * STEPS):
        pltpu.make_async_copy(halo_out.at[t], halo_out.at[t], halo_ssem.at[t]).wait()


def finish(node_grad, edge_grad, total, *refs):
    outs, wide, small, sem = refs[:10], refs[10], refs[11], refs[12]
    copies = [pltpu.make_async_copy(edge_grad, outs[1], sem.at[0]), pltpu.make_async_copy(node_grad, outs[0], sem.at[1])]
    for copy in copies:
        copy.start()
    where = ((BASE[EDGE0], BASE[STEP1]), (BASE[NODE0], BASE[STEP1] + 512))
    for out, part, first, count in ((2, 0, 0, 384), (4, 0, 384, 128), (6, 1, 0, 256), (8, 1, 256, 128)):
        to = part * 512 + first
        for t in range(STEPS):
            start = where[part][t] + first
            wide[t, to : to + count, :] = total[start : start + count, :].astype(F32)
        copy = pltpu.make_async_copy(wide.at[:, pl.ds(to, count), :], outs[out], sem.at[out])
        copy.start()
        copies.append(copy)
    smalls = (BASE[NODE0] + SMALL[NODE0], BASE[STEP1] + SMALL[STEP1])
    for t in range(STEPS):
        rows = total[smalls[t] : smalls[t] + 16, :].astype(F32)
        for k in range(4):
            small[k, t : t + 1, :] = rows[k : k + 1, :]
    for k, out in enumerate((3, 5, 7, 9)):
        copy = pltpu.make_async_copy(small.at[k], outs[out], sem.at[out])
        copy.start()
        copies.append(copy)
    for copy in copies:
        copy.wait()


def per_device(
    node_latents, edge_latents, senders, receivers, halo_rows, counts, cotangent,
    edge_first, edge_bias, edge_second, edge_gain, node_first, node_bias, node_second, node_gain,
):
    g1, g2 = YL * ZL * X * C, YH * ZH
    vmem, anywhere = pl.BlockSpec(memory_space=pltpu.VMEM), pl.BlockSpec(memory_space=pl.ANY)
    smem, hbm = pl.BlockSpec(memory_space=pltpu.SMEM), pl.BlockSpec(memory_space=pltpu.HBM)
    weights = (edge_first, edge_bias, edge_second, edge_gain, node_first, node_bias, node_second, node_gain)
    args = (
        node_latents, edge_latents, senders.reshape(SLOTS // D, D), receivers.reshape(SLOTS // D, D),
        halo_rows, counts, cotangent, *weights,
    )
    parts = pl.pallas_call(
        kernel,
        out_shape=(
            jax.ShapeDtypeStruct((NODES, D), BF16),
            jax.ShapeDtypeStruct((SLOTS, D), BF16),
            jax.ShapeDtypeStruct((sum(ROWS), D), BF16),
        ),
        in_specs=[smem if i == 5 else hbm for i in range(15)],
        out_specs=[vmem] * 3,
        scratch_shapes=[
            *(pltpu.VMEM(a.shape, a.dtype) for i, a in enumerate(args) if i != 5),
            pltpu.VMEM((SLOTS, 512), BF16),
            pltpu.VMEM((SLOTS, 256), BF16),
            pltpu.VMEM((640, SLOTS), BF16),
            pltpu.VMEM((8, D), F32),
            pltpu.VMEM((NODES, D), BF16),
            pltpu.VMEM((SLOTS, D), F32),
            pltpu.VMEM((STEPS, SLOTS, D), BF16),
            pltpu.VMEM((STEPS, SLOTS, D), F32),
            pltpu.VMEM((STEPS, SLOTS, D), F32),
            pltpu.VMEM((STEPS, SLOTS, 1), F32),
            pltpu.VMEM((STEPS, NODES, D), BF16),
            pltpu.VMEM((STEPS, NODES, D), F32),
            pltpu.VMEM((STEPS, NODES, D), F32),
            pltpu.VMEM((STEPS, NODES, 1), F32),
            pltpu.VMEM((STEPS, NODES, 256), BF16),
            pltpu.VMEM((SLOTS, D), BF16),
            pltpu.VMEM((SLOTS, D), F32),
            pltpu.VMEM((SLOTS, D), BF16),
            pltpu.VMEM((SLOTS, D), BF16),
            pltpu.VMEM((NODES, D), F32),
            pltpu.VMEM((2 * STEPS, 4 * HALO, D), BF16),
            pltpu.VMEM((2 * STEPS, 4 * HALO, D), BF16),
            pltpu.VMEM((sum(ROWS), D), BF16),
            pltpu.VMEM((sum(ROWS) // g1, D), BF16),
            *(pltpu.VMEM((g1, n // g1, D), BF16) for n in ROWS),
            *(pltpu.VMEM((g2, n // g1, D), BF16) for n in ROWS),
            pltpu.SemaphoreType.DMA((14,)),
            pltpu.SemaphoreType.DMA((2 * STEPS,)),
            pltpu.SemaphoreType.DMA((2 * STEPS,)),
            pltpu.SemaphoreType.DMA((3, 3)),
            pltpu.SemaphoreType.DMA((3, 3)),
            pltpu.SemaphoreType.REGULAR,
        ],
        compiler_params=pltpu.CompilerParams(
            collective_id=0, has_side_effects=True, vmem_limit_bytes=40 * 1024 * 1024
        ),
        name="steps",
    )(*(a if i == 5 else pltpu.with_memory_space_constraint(a, pltpu.HBM) for i, a in enumerate(args)))
    return pl.pallas_call(
        finish,
        out_shape=(
            jax.ShapeDtypeStruct((NODES, D), BF16),
            jax.ShapeDtypeStruct((SLOTS, D), BF16),
            *(jax.ShapeDtypeStruct(w.shape, F32) for w in weights),
        ),
        in_specs=[vmem] * 3,
        out_specs=[anywhere] * 10,
        scratch_shapes=[
            pltpu.VMEM((STEPS, 896, D), F32),
            pltpu.VMEM((4, STEPS, D), F32),
            pltpu.SemaphoreType.DMA((10,)),
        ],
        compiler_params=pltpu.CompilerParams(vmem_limit_bytes=40 * 1024 * 1024),
        name="finish",
    )(*parts)


def solution(mesh):
    tile = P(("sector", "span"))
    rows = P(("sector", "span"), None)
    return jax.shard_map(
        per_device,
        mesh=mesh,
        in_specs=(rows, rows, tile, tile, P(("sector", "span"), None, None), tile, rows) + (P(),) * 8,
        out_specs=(rows, rows) + (P(),) * 8,
        check_vma=False,
    )
```

```python
import functools

import jax
import jax.numpy as jnp
from jax import lax
from jax.experimental import pallas as pl
from jax.experimental.pallas import tpu as pltpu
from jax.sharding import PartitionSpec as P

F32, BF16 = jnp.float32, jnp.bfloat16
MESH = pl.DeviceIdType.MESH
STEPS = 2
EPS = 1e-05
YH, YL, ZH, C, X, ZL = 4, 2, 4, 2, 4, 2
NODES, SLOTS, D, HALO = 256, 1024, 128, 32
CHUNK = 256
STEP1, NODE0, EDGE0 = 0, 1, 2
ROWS = (1024, 512, 512)
BASE = (0, 1024, 1536)
SMALL = (896, 384)


def dot(a, b):
    return jnp.dot(a, b, preferred_element_type=F32)


def dot_first(a, b):
    return lax.dot_general(a, b, (((0,), (0,)), ((), ())), preferred_element_type=F32)


def dot_last(a, b):
    return lax.dot_general(a, b, (((1,), (1,)), ((), ())), preferred_element_type=F32)


def ones_where(mask):
    return jnp.where(mask, 1.0, 0.0).astype(BF16)


def activate(lin):
    sig = 0.5 * jnp.tanh(0.5 * lin) + 0.5
    act = lin * sig
    return act, sig + act * (1.0 - sig)


def normalized(proj):
    mean = jnp.mean(proj, axis=-1, keepdims=True)
    centred = proj - mean
    var = jnp.mean(centred * centred, axis=-1, keepdims=True)
    inv = lax.rsqrt(var + EPS)
    return centred * inv, inv


def normalized_back(dout, xhat, inv, gain):
    prod = dout * xhat
    dx = dout * gain
    mean = jnp.mean(dx, axis=-1, keepdims=True)
    along = jnp.mean(prod * gain, axis=-1, keepdims=True)
    return inv * (dx - mean - xhat * along), jnp.sum(prod, axis=0, keepdims=True)


def kernel(
    *refs,
):
    sources, counts, outs, here, refs = refs[:5] + refs[6:15], refs[5], refs[15:18], refs[18:32], refs[32:]
    nodes, edges, snd, rcv, halo, cot, ef, eb, es, eg, nf, nb, ns, ng = here
    node_grad, edge_grad, total = outs
    (
    own_pick, rest, spread, hal_pad, h1, part, act_e, slope_e, xhat_e, inv_e, act_n, slope_n, xhat_n, inv_n,
    node_in, edge_new, de, dlin, dproj, dh,
    halo_out, halo_in, grads, mid, got1_a, got1_b, got1_c, got2_a, got2_b, got2_c,
    in_sem, halo_ssem, halo_rsem, red_ssem, red_rsem, ready,
    ) = refs
    sector, span = lax.axis_index("sector"), lax.axis_index("span")
    n_sector, n_span = YH * YL * ZH * C, X * ZL
    yh, yl = sector // (YL * ZH * C), lax.rem(sector // (ZH * C), YL)
    zh, c = lax.rem(sector // C, ZH), lax.rem(sector, C)
    x, zl = span // ZL, lax.rem(span, ZL)
    g1, g2 = YL * ZL * X * C, YH * ZH
    me1, me2 = ((yl * ZL + zl) * X + x) * C + c, yh * ZH + zh
    units = tuple(n // g1 for n in ROWS)
    got1, got2 = (got1_a, got1_b, got1_c), (got2_a, got2_b, got2_c)

    def turned(at, size):
        return [at] + [lax.rem(at + k, size) for k in range(1, size)]

    yls, zls, xs, cs = turned(yl, YL), turned(zl, ZL), turned(x, X), turned(c, C)
    yhs, zhs = turned(yh, YH), turned(zh, ZH)
    offsets1 = [(a, b, d, e) for a in range(YL) for b in range(ZL) for d in range(X) for e in range(C)][1:]
    offsets1.sort(key=lambda o: -(o[0] + o[1] + min(o[2], X - o[2]) + 0.5 * o[3]))
    peers1 = [
        (
            ((yls[a] * ZL + zls[b]) * X + xs[d]) * C + cs[e],
            (((yh * YL + yls[a]) * ZH + zh) * C + cs[e], xs[d] * ZL + zls[b]),
        )
        for a, b, d, e in offsets1
    ]
    offsets2 = [(a, b) for a in range(YH) for b in range(ZH)][1:]
    offsets2.sort(key=lambda o: -(min(o[0], YH - o[0]) + min(o[1], ZH - o[1])))
    peers2 = [(((yhs[a] * YL + yl) * ZH + zhs[b]) * C + c, span) for a, b in offsets2]

    around = (
        (lax.rem(sector + n_sector - 1, n_sector), span),
        (lax.rem(sector + 1, n_sector), span),
        (sector, lax.rem(span + n_span - 1, n_span)),
        (sector, lax.rem(span + 1, n_span)),
    )

    barrier = pltpu.get_barrier_semaphore()
    for peer in around:
        pl.semaphore_signal(barrier, inc=1, device_id=peer, device_id_type=MESH)

    lines = [peer for peer, (a, b) in zip(peers2, offsets2) if b == 0]
    greeted = [peer for _, peer in peers1] + [peer for peer, (a, b) in zip(peers2, offsets2) if a == 0 or b == 0]
    for peer in greeted:
        pl.semaphore_signal(barrier, inc=1, device_id=peer, device_id_type=MESH)

    loads = [pltpu.make_async_copy(a, b, in_sem.at[i]) for i, (a, b) in enumerate(zip(sources, here))]
    first = (4, 0, 2, 3, 1)
    rest_loads = [i for i in range(14) if i not in first]
    for i in (*first, *rest_loads):
        loads[i].start()
    loads[4].wait()
    loads[0].wait()

    hal_pad[...] = jnp.zeros_like(hal_pad)
    hal_pad[0:4, 0:HALO] = halo[0].astype(F32)
    padded = hal_pad[...]
    lane = lax.broadcasted_iota(jnp.int32, (1, D), 1)
    flat = jnp.zeros((1, D), F32)
    for k in range(4):
        row = padded[k : k + 1, :] if k == 0 else pltpu.roll(padded, HALO * k, 1)[k : k + 1, :]
        flat = jnp.where((lane >= HALO * k) & (lane < HALO * (k + 1)), row, flat)
    lane_f = lax.broadcasted_iota(jnp.int32, (D, D), 1).astype(F32)
    down = jnp.broadcast_to(flat, (D, D)).T
    halo_pick = jnp.concatenate([ones_where(down == lane_f), ones_where(down == lane_f + D)], axis=1)
    halo_spread = ones_where(lax.broadcasted_iota(jnp.int32, (NODES, D), 0).astype(F32) == flat)

    row_id = lax.broadcasted_iota(jnp.int32, (4 * HALO, 1), 0)
    outside = ((row_id >= 2 * HALO) & (row_id < 3 * HALO) & (span == 0)) | (
        (row_id >= 3 * HALO) & (span == n_span - 1)
    )

    def exchange_start(t):
        for k in range(4):
            pltpu.make_async_remote_copy(
                src_ref=halo_out.at[t, pl.ds(k * HALO, HALO)],
                dst_ref=halo_in.at[t, pl.ds((k ^ 1) * HALO, HALO)],
                send_sem=halo_ssem.at[t],
                recv_sem=halo_rsem.at[t],
                device_id=around[k],
                device_id_type=MESH,
            ).start()

    def exchange_wait(t):
        pltpu.make_async_copy(halo_in.at[t], halo_in.at[t], halo_rsem.at[t]).wait()

    halo_out[0] = dot(halo_pick, nodes[...]).astype(BF16)
    pl.semaphore_wait(barrier, 4 + len(greeted))
    exchange_start(0)
    for peer in lines:
        pl.semaphore_signal(ready, inc=1, device_id=peer, device_id_type=MESH)

    for i in first[2:]:
        loads[i].wait()
    used = counts[0]
    slot = lax.broadcasted_iota(jnp.int32, (SLOTS // D, D), 0) * D + lax.broadcasted_iota(
        jnp.int32, (SLOTS // D, D), 1
    )
    snd_f = jnp.where(slot < used, snd[...], -1).astype(F32)
    rcv_f = jnp.where(slot < used, rcv[...], -1).astype(F32)
    down_f = lax.broadcasted_iota(jnp.int32, (NODES + 4 * HALO, D), 0).astype(F32)
    for r in range(SLOTS // D):
        at = pl.ds(r * D, D)
        s_row, r_row = snd_f[r : r + 1, :], rcv_f[r : r + 1, :]
        spread[0:384, at] = ones_where(down_f == s_row)
        spread[384:640, at] = ones_where(down_f[0:256] == r_row)
        s_col = jnp.broadcast_to(s_row, (D, D)).T
        r_col = jnp.broadcast_to(r_row, (D, D)).T
        own_pick[at, 0:128] = ones_where(s_col == lane_f)
        own_pick[at, 128:256] = ones_where(s_col == lane_f + 128.0)
        own_pick[at, 256:384] = ones_where(r_col == lane_f)
        own_pick[at, 384:512] = ones_where(r_col == lane_f + 128.0)
        rest[at, 0:128] = ones_where(s_col == lane_f + 256.0)
    rest[:, 128:256] = edges[...]
    for i in rest_loads:
        loads[i].wait()

    def forward(t):
        h = nodes[...] if t == 0 else h1[...]
        own_table = jnp.concatenate(
            [dot(h, ef[t, 0:128, :]).astype(BF16), dot(h, ef[t, 128:256, :]).astype(BF16)], axis=0
        )
        bias, gain = eb[t : t + 1, :], eg[t : t + 1, :]
        for i in range(SLOTS // CHUNK):
            at = pl.ds(i * CHUNK, CHUNK)
            part[at, :] = dot(own_pick[at, :], own_table) + bias
        exchange_wait(t)
        halo_in[t] = jnp.where(outside, 0.0, halo_in[t].astype(F32)).astype(BF16)
        rest_table = jnp.concatenate(
            [dot(halo_in[t], ef[t, 0:128, :]).astype(BF16), ef[t, 256:384, :]], axis=0
        )
        for i in range(SLOTS // CHUNK):
            at = pl.ds(i * CHUNK, CHUNK)
            lin = part[at, :] + dot(rest[at, :], rest_table)
            act, slope = activate(lin)
            act = act.astype(BF16)
            act_e[t, at, :] = act
            slope_e[t, at, :] = slope
            xhat, inv = normalized(dot(act, es[t]))
            xhat_e[t, at, :] = xhat
            inv_e[t, at, :] = inv
            new = (rest[at, 128:256].astype(F32) + xhat * gain).astype(BF16)
            edge_new[at, :] = new
        summed = dot(spread[384:640, :], edge_new[...]).astype(BF16)
        if t + 1 < STEPS:
            rest[:, 128:256] = edge_new[...]
        node_in[t, :, 0:128] = h
        node_in[t, :, 128:256] = summed
        act, slope = activate(dot(node_in[t], nf[t]) + nb[t : t + 1, :])
        act = act.astype(BF16)
        act_n[t] = act
        slope_n[t] = slope
        xhat, inv = normalized(dot(act, ns[t]))
        xhat_n[t] = xhat
        inv_n[t] = inv
        if t + 1 < STEPS:
            new_h = (h.astype(F32) + xhat * ng[t : t + 1, :]).astype(BF16)
            h1[...] = new_h
            halo_out[t + 1] = dot(halo_pick, new_h).astype(BF16)
            exchange_start(t + 1)

    def reduce_start(i, held=None, only=None):
        unit = units[i]

        def copy(j, peer):
            pltpu.make_async_remote_copy(
                src_ref=grads.at[pl.ds(pl.multiple_of(BASE[i] + j * unit, unit), unit)],
                dst_ref=got1[i].at[me1],
                send_sem=red_ssem.at[i, 0],
                recv_sem=red_rsem.at[i, 0],
                device_id=peer,
                device_id_type=MESH,
            ).start()

        if only is not None:
            at = only // (ZL * X * C), only // (X * C) % ZL, only // C % X, only % C
            peer = (((yh * YL + at[0]) * ZH + zh) * C + at[3], at[2] * ZL + at[1])
            pl.when(me1 != only)(lambda: copy(only, peer))
            return
        for j, peer in peers1:
            if held is None:
                copy(j, peer)
            else:
                pl.when(j != held)(functools.partial(copy, j, peer))

    def reduce_middle(i):
        unit = units[i]
        others = got1[i].at[pl.ds(1, g1 - 1)]
        pltpu.make_async_copy(others, others, red_rsem.at[i, 0]).wait()
        got1[i][me1] = grads[pl.ds(pl.multiple_of(BASE[i] + me1 * unit, unit), unit), :]
        acc = got1[i][0].astype(F32)
        for k in range(1, g1):
            acc = acc + got1[i][k].astype(F32)
        acc = acc.astype(BF16)
        block = pl.ds(BASE[i] // g1, unit)
        mid[block, :] = acc
        got2[i][me2] = acc

        for peer in peers2:
            pltpu.make_async_remote_copy(
                src_ref=mid.at[block],
                dst_ref=got2[i].at[me2],
                send_sem=red_ssem.at[i, 1],
                recv_sem=red_rsem.at[i, 1],
                device_id=peer,
                device_id_type=MESH,
            ).start()

    def reduce_last(i):
        unit = units[i]
        others = got2[i].at[pl.ds(1, g2 - 1)]
        pltpu.make_async_copy(others, others, red_rsem.at[i, 1]).wait()
        acc = got2[i][0].astype(F32)
        for k in range(1, g2):
            acc = acc + got2[i][k].astype(F32)
        scale = jnp.float32(NODES * n_sector * n_span) ** (-0.5)
        mine = pl.ds(pl.multiple_of(BASE[i] + me1 * unit, unit), unit)
        total[mine, :] = (acc * scale).astype(BF16)

        for _, peer in peers1:
            pltpu.make_async_remote_copy(
                src_ref=total.at[mine],
                dst_ref=total.at[mine],
                send_sem=red_ssem.at[i, 2],
                recv_sem=red_rsem.at[i, 2],
                device_id=peer,
                device_id_type=MESH,
            ).start()

    def reduce_finish(i):
        others = total.at[pl.ds(BASE[i], ROWS[i] - units[i])]
        pltpu.make_async_copy(others, others, red_rsem.at[i, 2]).wait()

    def reduce_sent(i):
        for phase, ref, count in ((0, got1[i], g1), (1, got2[i], g2), (2, got1[i], g1)):
            sent = ref.at[pl.ds(1, count - 1)]
            pltpu.make_async_copy(sent, sent, red_ssem.at[i, phase]).wait()

    def backward(t):
        last = t + 1 == STEPS
        h = nodes[...] if t == 0 else h1[...]
        dy = cot[...].astype(F32) if last else dh[...]
        dproj_n, dgain_n = normalized_back(dy, xhat_n[t], inv_n[t], ng[t : t + 1, :])
        dproj_n = dproj_n.astype(BF16)
        dlin_n = dot_last(dproj_n, ns[t]) * slope_n[t]
        dbias_n = jnp.sum(dlin_n, axis=0, keepdims=True)
        dlin_n = dlin_n.astype(BF16)
        dsummed = dot_last(dlin_n, nf[t, 128:256, :]).astype(BF16)
        node_at = BASE[STEP1] + 512 if last else BASE[NODE0]
        small_at = BASE[STEP1] + SMALL[STEP1] if last else BASE[NODE0] + SMALL[NODE0]
        held = SMALL[NODE0] // units[NODE0]

        def node_grads():
            grads[node_at : node_at + 256, :] = dot_first(node_in[t], dlin_n).astype(BF16)
            grads[node_at + 256 : node_at + 384, :] = dot_first(act_n[t], dproj_n).astype(BF16)

        small_rows = 128 if last else units[NODE0]
        if not last:
            node_grads()
            if small_rows < 128:
                grads[small_at + small_rows : small_at + 128, :] = jnp.zeros((128 - small_rows, D), BF16)
            reduce_start(NODE0, held=held)
        dgain_e = jnp.zeros((1, D), F32)
        gain = eg[t : t + 1, :]
        for i in range(SLOTS // CHUNK):
            at = pl.ds(i * CHUNK, CHUNK)
            dnew = dot(own_pick[at, 256:512], dsummed)
            if not last:
                dnew = dnew + de[at, :]
            dp, dg = normalized_back(dnew, xhat_e[t, at, :], inv_e[t, at, :], gain)
            dgain_e = dgain_e + dg
            dp = dp.astype(BF16)
            dproj[at, :] = dp
            dl = (dot_last(dp, es[t]) * slope_e[t, at, :]).astype(BF16)
            dlin[at, :] = dl
            dold = dnew + dot_last(dl, ef[t, 256:384, :])
            if last:
                de[at, :] = dold
            else:
                edge_grad[at, :] = dold.astype(BF16)
        sums = dot(spread[...], dlin[...])
        sums_b = sums.astype(BF16)
        dbias_e = jnp.sum(sums[384:640], axis=0, keepdims=True)

        def send_back():
            dhalo = dot_last(sums_b[256:384], ef[t, 0:128, :])
            halo_out[STEPS + t] = jnp.where(outside, 0.0, dhalo).astype(BF16)
            exchange_start(STEPS + t)

        edge_at = BASE[STEP1] if last else BASE[EDGE0]
        if last:
            send_back()
        grads[edge_at : edge_at + 128, :] = (
            dot_first(h, sums_b[0:256]) + dot_first(halo_in[t], sums_b[256:384])
        ).astype(BF16)
        grads[edge_at + 128 : edge_at + 256, :] = dot_first(h, sums_b[384:640]).astype(BF16)
        old = edges[...] if t == 0 else rest[:, 128:256]
        grads[edge_at + 256 : edge_at + 384, :] = dot_first(old, dlin[...]).astype(BF16)
        grads[edge_at + 384 : edge_at + 512, :] = dot_first(act_e[t], dproj[...]).astype(BF16)
        grads[small_at : small_at + small_rows, :] = jnp.concatenate(
            [dbias_e, dgain_e, dbias_n, dgain_n, jnp.zeros((small_rows - 4, D), F32)], axis=0
        ).astype(BF16)
        if last:
            node_grads()
            reduce_start(STEP1)
        else:
            reduce_start(EDGE0)
            reduce_start(NODE0, only=held)
            send_back()
        own = (
            dy
            + dot_last(dlin_n, nf[t, 0:128, :])
            + dot_last(sums_b[0:256], ef[t, 0:128, :])
            + dot_last(sums_b[384:640], ef[t, 128:256, :])
        )
        if not last:
            pl.semaphore_wait(ready, YH - 1)
            reduce_middle(STEP1)
            reduce_middle(NODE0)
        exchange_wait(STEPS + t)
        own = (own + dot(halo_spread, halo_in[STEPS + t])).astype(BF16)
        if last:
            dh[...] = own.astype(F32)
        else:
            node_grad[...] = own

    forward(0)
    forward(1)
    backward(1)
    backward(0)
    reduce_middle(EDGE0)
    for i in (STEP1, NODE0, EDGE0):
        reduce_last(i)
    for i in (STEP1, NODE0, EDGE0):
        reduce_finish(i)
    for i in (STEP1, NODE0, EDGE0):
        reduce_sent(i)
    for t in range(2 * STEPS):
        pltpu.make_async_copy(halo_out.at[t], halo_out.at[t], halo_ssem.at[t]).wait()


def finish(node_grad, edge_grad, total, *refs):
    outs, wide, small, sem = refs[:10], refs[10], refs[11], refs[12]
    copies = [pltpu.make_async_copy(edge_grad, outs[1], sem.at[0]), pltpu.make_async_copy(node_grad, outs[0], sem.at[1])]
    for copy in copies:
        copy.start()
    where = ((BASE[EDGE0], BASE[STEP1]), (BASE[NODE0], BASE[STEP1] + 512))
    for out, part, first, count in ((2, 0, 0, 384), (4, 0, 384, 128), (6, 1, 0, 256), (8, 1, 256, 128)):
        to = part * 512 + first
        for t in range(STEPS):
            start = where[part][t] + first
            wide[t, to : to + count, :] = total[start : start + count, :].astype(F32)
        copy = pltpu.make_async_copy(wide.at[:, pl.ds(to, count), :], outs[out], sem.at[out])
        copy.start()
        copies.append(copy)
    smalls = (BASE[NODE0] + SMALL[NODE0], BASE[STEP1] + SMALL[STEP1])
    for t in range(STEPS):
        rows = total[smalls[t] : smalls[t] + 16, :].astype(F32)
        for k in range(4):
            small[k, t : t + 1, :] = rows[k : k + 1, :]
    for k, out in enumerate((3, 5, 7, 9)):
        copy = pltpu.make_async_copy(small.at[k], outs[out], sem.at[out])
        copy.start()
        copies.append(copy)
    for copy in copies:
        copy.wait()


def per_device(
    node_latents, edge_latents, senders, receivers, halo_rows, counts, cotangent,
    edge_first, edge_bias, edge_second, edge_gain, node_first, node_bias, node_second, node_gain,
):
    g1, g2 = YL * ZL * X * C, YH * ZH
    vmem, anywhere = pl.BlockSpec(memory_space=pltpu.VMEM), pl.BlockSpec(memory_space=pl.ANY)
    smem, hbm = pl.BlockSpec(memory_space=pltpu.SMEM), pl.BlockSpec(memory_space=pltpu.HBM)
    weights = (edge_first, edge_bias, edge_second, edge_gain, node_first, node_bias, node_second, node_gain)
    args = (
        node_latents, edge_latents, senders.reshape(SLOTS // D, D), receivers.reshape(SLOTS // D, D),
        halo_rows, counts, cotangent, *weights,
    )
    parts = pl.pallas_call(
        kernel,
        out_shape=(
            jax.ShapeDtypeStruct((NODES, D), BF16),
            jax.ShapeDtypeStruct((SLOTS, D), BF16),
            jax.ShapeDtypeStruct((sum(ROWS), D), BF16),
        ),
        in_specs=[smem if i == 5 else hbm for i in range(15)],
        out_specs=[vmem] * 3,
        scratch_shapes=[
            *(pltpu.VMEM(a.shape, a.dtype) for i, a in enumerate(args) if i != 5),
            pltpu.VMEM((SLOTS, 512), BF16),
            pltpu.VMEM((SLOTS, 256), BF16),
            pltpu.VMEM((640, SLOTS), BF16),
            pltpu.VMEM((8, D), F32),
            pltpu.VMEM((NODES, D), BF16),
            pltpu.VMEM((SLOTS, D), F32),
            pltpu.VMEM((STEPS, SLOTS, D), BF16),
            pltpu.VMEM((STEPS, SLOTS, D), F32),
            pltpu.VMEM((STEPS, SLOTS, D), F32),
            pltpu.VMEM((STEPS, SLOTS, 1), F32),
            pltpu.VMEM((STEPS, NODES, D), BF16),
            pltpu.VMEM((STEPS, NODES, D), F32),
            pltpu.VMEM((STEPS, NODES, D), F32),
            pltpu.VMEM((STEPS, NODES, 1), F32),
            pltpu.VMEM((STEPS, NODES, 256), BF16),
            pltpu.VMEM((SLOTS, D), BF16),
            pltpu.VMEM((SLOTS, D), F32),
            pltpu.VMEM((SLOTS, D), BF16),
            pltpu.VMEM((SLOTS, D), BF16),
            pltpu.VMEM((NODES, D), F32),
            pltpu.VMEM((2 * STEPS, 4 * HALO, D), BF16),
            pltpu.VMEM((2 * STEPS, 4 * HALO, D), BF16),
            pltpu.VMEM((sum(ROWS), D), BF16),
            pltpu.VMEM((sum(ROWS) // g1, D), BF16),
            *(pltpu.VMEM((g1, n // g1, D), BF16) for n in ROWS),
            *(pltpu.VMEM((g2, n // g1, D), BF16) for n in ROWS),
            pltpu.SemaphoreType.DMA((14,)),
            pltpu.SemaphoreType.DMA((2 * STEPS,)),
            pltpu.SemaphoreType.DMA((2 * STEPS,)),
            pltpu.SemaphoreType.DMA((3, 3)),
            pltpu.SemaphoreType.DMA((3, 3)),
            pltpu.SemaphoreType.REGULAR,
        ],
        compiler_params=pltpu.CompilerParams(
            collective_id=0, has_side_effects=True, vmem_limit_bytes=40 * 1024 * 1024
        ),
        name="steps",
    )(*(a if i == 5 else pltpu.with_memory_space_constraint(a, pltpu.HBM) for i, a in enumerate(args)))
    return pl.pallas_call(
        finish,
        out_shape=(
            jax.ShapeDtypeStruct((NODES, D), BF16),
            jax.ShapeDtypeStruct((SLOTS, D), BF16),
            *(jax.ShapeDtypeStruct(w.shape, F32) for w in weights),
        ),
        in_specs=[vmem] * 3,
        out_specs=[anywhere] * 10,
        scratch_shapes=[
            pltpu.VMEM((STEPS, 896, D), F32),
            pltpu.VMEM((4, STEPS, D), F32),
            pltpu.SemaphoreType.DMA((10,)),
        ],
        compiler_params=pltpu.CompilerParams(vmem_limit_bytes=40 * 1024 * 1024),
        name="finish",
    )(*parts)


def solution(mesh):
    tile = P(("sector", "span"))
    rows = P(("sector", "span"), None)
    return jax.shard_map(
        per_device,
        mesh=mesh,
        in_specs=(rows, rows, tile, tile, P(("sector", "span"), None, None), tile, rows) + (P(),) * 8,
        out_specs=(rows, rows) + (P(),) * 8,
        check_vma=False,
    )
```

```python
import functools

import jax
import jax.numpy as jnp
from jax import lax
from jax.experimental import pallas as pl
from jax.experimental.pallas import tpu as pltpu
from jax.sharding import PartitionSpec as P

F32, BF16 = jnp.float32, jnp.bfloat16
MESH = pl.DeviceIdType.MESH
STEPS = 2
EPS = 1e-05
YH, YL, ZH, C, X, ZL = 4, 2, 4, 2, 4, 2
NODES, SLOTS, D, HALO = 256, 1024, 128, 32
CHUNK = 512
STEP1, NODE0, EDGE0 = 0, 1, 2
ROWS = (1024, 512, 512)
BASE = (0, 1024, 1536)
SMALL = (896, 384)


def dot(a, b):
    return jnp.dot(a, b, preferred_element_type=F32)


def dot_first(a, b):
    return lax.dot_general(a, b, (((0,), (0,)), ((), ())), preferred_element_type=F32)


def dot_last(a, b):
    return lax.dot_general(a, b, (((1,), (1,)), ((), ())), preferred_element_type=F32)


def ones_where(mask):
    return jnp.where(mask, 1.0, 0.0).astype(BF16)


def activate(lin):
    sig = 0.5 * jnp.tanh(0.5 * lin) + 0.5
    act = lin * sig
    return act, sig + act * (1.0 - sig)


def centred(weight):
    weight = weight.astype(F32)
    return weight - jnp.mean(weight, axis=-1, keepdims=True)


def normalized(proj):
    inv = lax.rsqrt(jnp.mean(proj * proj, axis=-1, keepdims=True) + EPS)
    return proj * inv, inv


def normalized_back(dout, xhat, inv, gain):
    prod = dout * xhat
    along = jnp.mean(prod * gain, axis=-1, keepdims=True)
    return inv * (dout * gain - xhat * along), jnp.sum(prod, axis=0, keepdims=True)


def kernel(
    *refs,
):
    sources, counts, outs, here, refs = refs[:5] + refs[6:15], refs[5], refs[15:18], refs[18:32], refs[32:]
    nodes, edges, snd, rcv, halo, cot, ef, eb, es, eg, nf, nb, ns, ng = here
    node_grad, edge_grad, total = outs
    (
    own_pick, rest, spread, hal_pad, h1, part, act_e, slope_e, xhat_e, inv_e, act_n, slope_n, xhat_n, inv_n,
    node_in, edge_new, de, dlin, dproj, dh,
    es_c, ns_c, halo_out, halo_in, grads, mid, got1_a, got1_b, got1_c, got2_a, got2_b, got2_c,
    in_sem, halo_ssem, halo_rsem, red_ssem, red_rsem, ready,
    ) = refs
    sector, span = lax.axis_index("sector"), lax.axis_index("span")
    n_sector, n_span = YH * YL * ZH * C, X * ZL
    yh, yl = sector // (YL * ZH * C), lax.rem(sector // (ZH * C), YL)
    zh, c = lax.rem(sector // C, ZH), lax.rem(sector, C)
    x, zl = span // ZL, lax.rem(span, ZL)
    g1, g2 = YL * ZL * X * C, YH * ZH
    me1, me2 = ((yl * ZL + zl) * X + x) * C + c, yh * ZH + zh
    units = tuple(n // g1 for n in ROWS)
    got1, got2 = (got1_a, got1_b, got1_c), (got2_a, got2_b, got2_c)

    def turned(at, size):
        return [at] + [lax.rem(at + k, size) for k in range(1, size)]

    yls, zls, xs, cs = turned(yl, YL), turned(zl, ZL), turned(x, X), turned(c, C)
    yhs, zhs = turned(yh, YH), turned(zh, ZH)
    offsets1 = [(a, b, d, e) for a in range(YL) for b in range(ZL) for d in range(X) for e in range(C)][1:]
    offsets1.sort(key=lambda o: -(o[0] + o[1] + min(o[2], X - o[2]) + 0.5 * o[3]))
    peers1 = [
        (
            ((yls[a] * ZL + zls[b]) * X + xs[d]) * C + cs[e],
            (((yh * YL + yls[a]) * ZH + zh) * C + cs[e], xs[d] * ZL + zls[b]),
        )
        for a, b, d, e in offsets1
    ]
    offsets2 = [(a, b) for a in range(YH) for b in range(ZH)][1:]
    offsets2.sort(key=lambda o: -(min(o[0], YH - o[0]) + min(o[1], ZH - o[1])))
    peers2 = [(((yhs[a] * YL + yl) * ZH + zhs[b]) * C + c, span) for a, b in offsets2]

    around = (
        (lax.rem(sector + n_sector - 1, n_sector), span),
        (lax.rem(sector + 1, n_sector), span),
        (sector, lax.rem(span + n_span - 1, n_span)),
        (sector, lax.rem(span + 1, n_span)),
    )

    barrier = pltpu.get_barrier_semaphore()
    for peer in around:
        pl.semaphore_signal(barrier, inc=1, device_id=peer, device_id_type=MESH)

    lines = [peer for peer, (a, b) in zip(peers2, offsets2) if b == 0]
    greeted = [peer for _, peer in peers1] + [peer for peer, (a, b) in zip(peers2, offsets2) if a == 0 or b == 0]
    for peer in greeted:
        pl.semaphore_signal(barrier, inc=1, device_id=peer, device_id_type=MESH)

    loads = [pltpu.make_async_copy(a, b, in_sem.at[i]) for i, (a, b) in enumerate(zip(sources, here))]
    first = (4, 0, 2, 3, 1)
    rest_loads = [i for i in range(14) if i not in first]
    for i in (*first, *rest_loads):
        loads[i].start()
    loads[4].wait()
    loads[0].wait()

    hal_pad[...] = jnp.zeros_like(hal_pad)
    hal_pad[0:4, 0:HALO] = halo[0].astype(F32)
    padded = hal_pad[...]
    lane = lax.broadcasted_iota(jnp.int32, (1, D), 1)
    flat = jnp.zeros((1, D), F32)
    for k in range(4):
        row = padded[k : k + 1, :] if k == 0 else pltpu.roll(padded, HALO * k, 1)[k : k + 1, :]
        flat = jnp.where((lane >= HALO * k) & (lane < HALO * (k + 1)), row, flat)
    lane_f = lax.broadcasted_iota(jnp.int32, (D, D), 1).astype(F32)
    down = jnp.broadcast_to(flat, (D, D)).T
    halo_pick = jnp.concatenate([ones_where(down == lane_f), ones_where(down == lane_f + D)], axis=1)
    halo_spread = ones_where(lax.broadcasted_iota(jnp.int32, (NODES, D), 0).astype(F32) == flat)

    row_id = lax.broadcasted_iota(jnp.int32, (4 * HALO, 1), 0)
    outside = ((row_id >= 2 * HALO) & (row_id < 3 * HALO) & (span == 0)) | (
        (row_id >= 3 * HALO) & (span == n_span - 1)
    )

    def exchange_start(t):
        for k in range(4):
            pltpu.make_async_remote_copy(
                src_ref=halo_out.at[t, pl.ds(k * HALO, HALO)],
                dst_ref=halo_in.at[t, pl.ds((k ^ 1) * HALO, HALO)],
                send_sem=halo_ssem.at[t],
                recv_sem=halo_rsem.at[t],
                device_id=around[k],
                device_id_type=MESH,
            ).start()

    def exchange_wait(t):
        pltpu.make_async_copy(halo_in.at[t], halo_in.at[t], halo_rsem.at[t]).wait()

    halo_out[0] = dot(halo_pick, nodes[...]).astype(BF16)
    pl.semaphore_wait(barrier, 4 + len(greeted))
    exchange_start(0)
    for peer in lines:
        pl.semaphore_signal(ready, inc=1, device_id=peer, device_id_type=MESH)

    for i in first[2:]:
        loads[i].wait()
    used = counts[0]
    slot = lax.broadcasted_iota(jnp.int32, (SLOTS // D, D), 0) * D + lax.broadcasted_iota(
        jnp.int32, (SLOTS // D, D), 1
    )
    snd_f = jnp.where(slot < used, snd[...], -1).astype(F32)
    rcv_f = jnp.where(slot < used, rcv[...], -1).astype(F32)
    down_f = lax.broadcasted_iota(jnp.int32, (NODES + 4 * HALO, D), 0).astype(F32)
    for r in range(SLOTS // D):
        at = pl.ds(r * D, D)
        s_row, r_row = snd_f[r : r + 1, :], rcv_f[r : r + 1, :]
        spread[0:384, at] = ones_where(down_f == s_row)
        spread[384:640, at] = ones_where(down_f[0:256] == r_row)
        s_col = jnp.broadcast_to(s_row, (D, D)).T
        r_col = jnp.broadcast_to(r_row, (D, D)).T
        own_pick[at, 0:128] = ones_where(s_col == lane_f)
        own_pick[at, 128:256] = ones_where(s_col == lane_f + 128.0)
        own_pick[at, 256:384] = ones_where(r_col == lane_f)
        own_pick[at, 384:512] = ones_where(r_col == lane_f + 128.0)
        rest[at, 0:128] = ones_where(s_col == lane_f + 256.0)
    rest[:, 128:256] = edges[...]
    for i in rest_loads:
        loads[i].wait()

    for t in range(STEPS):
        es_c[t] = centred(es[t]).astype(BF16)
        ns_c[t] = centred(ns[t]).astype(BF16)

    def forward(t):
        h = nodes[...] if t == 0 else h1[...]
        own_table = jnp.concatenate(
            [dot(h, ef[t, 0:128, :]).astype(BF16), dot(h, ef[t, 128:256, :]).astype(BF16)], axis=0
        )
        bias, gain = eb[t : t + 1, :], eg[t : t + 1, :]
        for i in range(SLOTS // CHUNK):
            at = pl.ds(i * CHUNK, CHUNK)
            part[at, :] = dot(own_pick[at, :], own_table) + bias
        exchange_wait(t)
        halo_in[t] = jnp.where(outside, 0.0, halo_in[t].astype(F32)).astype(BF16)
        rest_table = jnp.concatenate(
            [dot(halo_in[t], ef[t, 0:128, :]).astype(BF16), ef[t, 256:384, :]], axis=0
        )
        for i in range(SLOTS // CHUNK):
            at = pl.ds(i * CHUNK, CHUNK)
            lin = part[at, :] + dot(rest[at, :], rest_table)
            act, slope = activate(lin)
            act = act.astype(BF16)
            act_e[t, at, :] = act
            slope_e[t, at, :] = slope
            xhat, inv = normalized(dot(act, es_c[t]))
            xhat_e[t, at, :] = xhat
            inv_e[t, at, :] = inv
            new = (rest[at, 128:256].astype(F32) + xhat * gain).astype(BF16)
            edge_new[at, :] = new
        summed = dot(spread[384:640, :], edge_new[...]).astype(BF16)
        if t + 1 < STEPS:
            rest[:, 128:256] = edge_new[...]
        node_in[t, :, 0:128] = h
        node_in[t, :, 128:256] = summed
        act, slope = activate(dot(node_in[t], nf[t]) + nb[t : t + 1, :])
        act = act.astype(BF16)
        act_n[t] = act
        slope_n[t] = slope
        xhat, inv = normalized(dot(act, ns_c[t]))
        xhat_n[t] = xhat
        inv_n[t] = inv
        if t + 1 < STEPS:
            new_h = (h.astype(F32) + xhat * ng[t : t + 1, :]).astype(BF16)
            h1[...] = new_h
            halo_out[t + 1] = dot(halo_pick, new_h).astype(BF16)
            exchange_start(t + 1)

    def reduce_start(i, held=None, only=None):
        unit = units[i]

        def copy(j, peer):
            pltpu.make_async_remote_copy(
                src_ref=grads.at[pl.ds(pl.multiple_of(BASE[i] + j * unit, unit), unit)],
                dst_ref=got1[i].at[me1],
                send_sem=red_ssem.at[i, 0],
                recv_sem=red_rsem.at[i, 0],
                device_id=peer,
                device_id_type=MESH,
            ).start()

        if only is not None:
            at = only // (ZL * X * C), only // (X * C) % ZL, only // C % X, only % C
            peer = (((yh * YL + at[0]) * ZH + zh) * C + at[3], at[2] * ZL + at[1])
            pl.when(me1 != only)(lambda: copy(only, peer))
            return
        for j, peer in peers1:
            if held is None:
                copy(j, peer)
            else:
                pl.when(j != held)(functools.partial(copy, j, peer))

    def reduce_middle(i):
        unit = units[i]
        others = got1[i].at[pl.ds(1, g1 - 1)]
        pltpu.make_async_copy(others, others, red_rsem.at[i, 0]).wait()
        got1[i][me1] = grads[pl.ds(pl.multiple_of(BASE[i] + me1 * unit, unit), unit), :]
        acc = got1[i][0].astype(F32)
        for k in range(1, g1):
            acc = acc + got1[i][k].astype(F32)
        acc = acc.astype(BF16)
        block = pl.ds(BASE[i] // g1, unit)
        mid[block, :] = acc
        got2[i][me2] = acc

        for peer in peers2:
            pltpu.make_async_remote_copy(
                src_ref=mid.at[block],
                dst_ref=got2[i].at[me2],
                send_sem=red_ssem.at[i, 1],
                recv_sem=red_rsem.at[i, 1],
                device_id=peer,
                device_id_type=MESH,
            ).start()

    def reduce_last(i):
        unit = units[i]
        others = got2[i].at[pl.ds(1, g2 - 1)]
        pltpu.make_async_copy(others, others, red_rsem.at[i, 1]).wait()
        acc = got2[i][0].astype(F32)
        for k in range(1, g2):
            acc = acc + got2[i][k].astype(F32)
        scale = jnp.float32(NODES * n_sector * n_span) ** (-0.5)
        mine = pl.ds(pl.multiple_of(BASE[i] + me1 * unit, unit), unit)
        total[mine, :] = (acc * scale).astype(BF16)

        for _, peer in peers1:
            pltpu.make_async_remote_copy(
                src_ref=total.at[mine],
                dst_ref=total.at[mine],
                send_sem=red_ssem.at[i, 2],
                recv_sem=red_rsem.at[i, 2],
                device_id=peer,
                device_id_type=MESH,
            ).start()

    def reduce_finish(i):
        others = total.at[pl.ds(BASE[i], ROWS[i] - units[i])]
        pltpu.make_async_copy(others, others, red_rsem.at[i, 2]).wait()

    def reduce_sent(i):
        for phase, ref, count in ((0, got1[i], g1), (1, got2[i], g2), (2, got1[i], g1)):
            sent = ref.at[pl.ds(1, count - 1)]
            pltpu.make_async_copy(sent, sent, red_ssem.at[i, phase]).wait()

    def backward(t):
        last = t + 1 == STEPS
        h = nodes[...] if t == 0 else h1[...]
        dy = cot[...].astype(F32) if last else dh[...]
        dproj_n, dgain_n = normalized_back(dy, xhat_n[t], inv_n[t], ng[t : t + 1, :])
        dproj_n = dproj_n.astype(BF16)
        dlin_n = dot_last(dproj_n, ns_c[t]) * slope_n[t]
        dbias_n = jnp.sum(dlin_n, axis=0, keepdims=True)
        dlin_n = dlin_n.astype(BF16)
        dsummed = dot_last(dlin_n, nf[t, 128:256, :]).astype(BF16)
        node_at = BASE[STEP1] + 512 if last else BASE[NODE0]
        small_at = BASE[STEP1] + SMALL[STEP1] if last else BASE[NODE0] + SMALL[NODE0]
        held = SMALL[NODE0] // units[NODE0]

        def node_grads():
            grads[node_at : node_at + 256, :] = dot_first(node_in[t], dlin_n).astype(BF16)
            grads[node_at + 256 : node_at + 384, :] = centred(dot_first(act_n[t], dproj_n)).astype(BF16)

        small_rows = 128 if last else units[NODE0]
        if not last:
            node_grads()
            if small_rows < 128:
                grads[small_at + small_rows : small_at + 128, :] = jnp.zeros((128 - small_rows, D), BF16)
            reduce_start(NODE0, held=held)
        dgain_e = jnp.zeros((1, D), F32)
        gain = eg[t : t + 1, :]
        for i in range(SLOTS // CHUNK):
            at = pl.ds(i * CHUNK, CHUNK)
            dnew = dot(own_pick[at, 256:512], dsummed)
            if not last:
                dnew = dnew + de[at, :]
            dp, dg = normalized_back(dnew, xhat_e[t, at, :], inv_e[t, at, :], gain)
            dgain_e = dgain_e + dg
            dp = dp.astype(BF16)
            dproj[at, :] = dp
            dl = (dot_last(dp, es_c[t]) * slope_e[t, at, :]).astype(BF16)
            dlin[at, :] = dl
            dold = dnew + dot_last(dl, ef[t, 256:384, :])
            if last:
                de[at, :] = dold
            else:
                edge_grad[at, :] = dold.astype(BF16)
        sums = dot(spread[...], dlin[...])
        sums_b = sums.astype(BF16)
        dbias_e = jnp.sum(sums[384:640], axis=0, keepdims=True)

        def send_back():
            dhalo = dot_last(sums_b[256:384], ef[t, 0:128, :])
            halo_out[STEPS + t] = jnp.where(outside, 0.0, dhalo).astype(BF16)
            exchange_start(STEPS + t)

        edge_at = BASE[STEP1] if last else BASE[EDGE0]
        if last:
            send_back()
        grads[edge_at : edge_at + 128, :] = (
            dot_first(h, sums_b[0:256]) + dot_first(halo_in[t], sums_b[256:384])
        ).astype(BF16)
        grads[edge_at + 128 : edge_at + 256, :] = dot_first(h, sums_b[384:640]).astype(BF16)
        old = edges[...] if t == 0 else rest[:, 128:256]
        grads[edge_at + 256 : edge_at + 384, :] = dot_first(old, dlin[...]).astype(BF16)
        grads[edge_at + 384 : edge_at + 512, :] = centred(dot_first(act_e[t], dproj[...])).astype(BF16)
        grads[small_at : small_at + small_rows, :] = jnp.concatenate(
            [dbias_e, dgain_e, dbias_n, dgain_n, jnp.zeros((small_rows - 4, D), F32)], axis=0
        ).astype(BF16)
        if last:
            node_grads()
            reduce_start(STEP1)
        else:
            reduce_start(EDGE0)
            reduce_start(NODE0, only=held)
            send_back()
        own = (
            dy
            + dot_last(dlin_n, nf[t, 0:128, :])
            + dot_last(sums_b[0:256], ef[t, 0:128, :])
            + dot_last(sums_b[384:640], ef[t, 128:256, :])
        )
        if not last:
            pl.semaphore_wait(ready, YH - 1)
            reduce_middle(STEP1)
            reduce_middle(NODE0)
        exchange_wait(STEPS + t)
        own = (own + dot(halo_spread, halo_in[STEPS + t])).astype(BF16)
        if last:
            dh[...] = own.astype(F32)
        else:
            node_grad[...] = own

    forward(0)
    forward(1)
    backward(1)
    backward(0)
    reduce_middle(EDGE0)
    for i in (STEP1, NODE0, EDGE0):
        reduce_last(i)
    for i in (STEP1, NODE0, EDGE0):
        reduce_finish(i)
    for i in (STEP1, NODE0, EDGE0):
        reduce_sent(i)
    for t in range(2 * STEPS):
        pltpu.make_async_copy(halo_out.at[t], halo_out.at[t], halo_ssem.at[t]).wait()


def finish(node_grad, edge_grad, total, *refs):
    outs, wide, small, sem = refs[:10], refs[10], refs[11], refs[12]
    copies = [pltpu.make_async_copy(edge_grad, outs[1], sem.at[0]), pltpu.make_async_copy(node_grad, outs[0], sem.at[1])]
    for copy in copies:
        copy.start()
    where = ((BASE[EDGE0], BASE[STEP1]), (BASE[NODE0], BASE[STEP1] + 512))
    for out, part, first, count in ((2, 0, 0, 384), (4, 0, 384, 128), (6, 1, 0, 256), (8, 1, 256, 128)):
        to = part * 512 + first
        for t in range(STEPS):
            start = where[part][t] + first
            wide[t, to : to + count, :] = total[start : start + count, :].astype(F32)
        copy = pltpu.make_async_copy(wide.at[:, pl.ds(to, count), :], outs[out], sem.at[out])
        copy.start()
        copies.append(copy)
    smalls = (BASE[NODE0] + SMALL[NODE0], BASE[STEP1] + SMALL[STEP1])
    for t in range(STEPS):
        rows = total[smalls[t] : smalls[t] + 16, :].astype(F32)
        for k in range(4):
            small[k, t : t + 1, :] = rows[k : k + 1, :]
    for k, out in enumerate((3, 5, 7, 9)):
        copy = pltpu.make_async_copy(small.at[k], outs[out], sem.at[out])
        copy.start()
        copies.append(copy)
    for copy in copies:
        copy.wait()


def per_device(
    node_latents, edge_latents, senders, receivers, halo_rows, counts, cotangent,
    edge_first, edge_bias, edge_second, edge_gain, node_first, node_bias, node_second, node_gain,
):
    g1, g2 = YL * ZL * X * C, YH * ZH
    vmem, anywhere = pl.BlockSpec(memory_space=pltpu.VMEM), pl.BlockSpec(memory_space=pl.ANY)
    smem, hbm = pl.BlockSpec(memory_space=pltpu.SMEM), pl.BlockSpec(memory_space=pltpu.HBM)
    weights = (edge_first, edge_bias, edge_second, edge_gain, node_first, node_bias, node_second, node_gain)
    args = (
        node_latents, edge_latents, senders.reshape(SLOTS // D, D), receivers.reshape(SLOTS // D, D),
        halo_rows, counts, cotangent, *weights,
    )
    parts = pl.pallas_call(
        kernel,
        out_shape=(
            jax.ShapeDtypeStruct((NODES, D), BF16),
            jax.ShapeDtypeStruct((SLOTS, D), BF16),
            jax.ShapeDtypeStruct((sum(ROWS), D), BF16),
        ),
        in_specs=[smem if i == 5 else hbm for i in range(15)],
        out_specs=[vmem] * 3,
        scratch_shapes=[
            *(pltpu.VMEM(a.shape, a.dtype) for i, a in enumerate(args) if i != 5),
            pltpu.VMEM((SLOTS, 512), BF16),
            pltpu.VMEM((SLOTS, 256), BF16),
            pltpu.VMEM((640, SLOTS), BF16),
            pltpu.VMEM((8, D), F32),
            pltpu.VMEM((NODES, D), BF16),
            pltpu.VMEM((SLOTS, D), F32),
            pltpu.VMEM((STEPS, SLOTS, D), BF16),
            pltpu.VMEM((STEPS, SLOTS, D), F32),
            pltpu.VMEM((STEPS, SLOTS, D), F32),
            pltpu.VMEM((STEPS, SLOTS, 1), F32),
            pltpu.VMEM((STEPS, NODES, D), BF16),
            pltpu.VMEM((STEPS, NODES, D), F32),
            pltpu.VMEM((STEPS, NODES, D), F32),
            pltpu.VMEM((STEPS, NODES, 1), F32),
            pltpu.VMEM((STEPS, NODES, 256), BF16),
            pltpu.VMEM((SLOTS, D), BF16),
            pltpu.VMEM((SLOTS, D), F32),
            pltpu.VMEM((SLOTS, D), BF16),
            pltpu.VMEM((SLOTS, D), BF16),
            pltpu.VMEM((NODES, D), F32),
            pltpu.VMEM((STEPS, D, D), BF16),
            pltpu.VMEM((STEPS, D, D), BF16),
            pltpu.VMEM((2 * STEPS, 4 * HALO, D), BF16),
            pltpu.VMEM((2 * STEPS, 4 * HALO, D), BF16),
            pltpu.VMEM((sum(ROWS), D), BF16),
            pltpu.VMEM((sum(ROWS) // g1, D), BF16),
            *(pltpu.VMEM((g1, n // g1, D), BF16) for n in ROWS),
            *(pltpu.VMEM((g2, n // g1, D), BF16) for n in ROWS),
            pltpu.SemaphoreType.DMA((14,)),
            pltpu.SemaphoreType.DMA((2 * STEPS,)),
            pltpu.SemaphoreType.DMA((2 * STEPS,)),
            pltpu.SemaphoreType.DMA((3, 3)),
            pltpu.SemaphoreType.DMA((3, 3)),
            pltpu.SemaphoreType.REGULAR,
        ],
        compiler_params=pltpu.CompilerParams(
            collective_id=0, has_side_effects=True, vmem_limit_bytes=40 * 1024 * 1024
        ),
        name="steps",
    )(*(a if i == 5 else pltpu.with_memory_space_constraint(a, pltpu.HBM) for i, a in enumerate(args)))
    return pl.pallas_call(
        finish,
        out_shape=(
            jax.ShapeDtypeStruct((NODES, D), BF16),
            jax.ShapeDtypeStruct((SLOTS, D), BF16),
            *(jax.ShapeDtypeStruct(w.shape, F32) for w in weights),
        ),
        in_specs=[vmem] * 3,
        out_specs=[anywhere] * 10,
        scratch_shapes=[
            pltpu.VMEM((STEPS, 896, D), F32),
            pltpu.VMEM((4, STEPS, D), F32),
            pltpu.SemaphoreType.DMA((10,)),
        ],
        compiler_params=pltpu.CompilerParams(vmem_limit_bytes=40 * 1024 * 1024),
        name="finish",
    )(*parts)


def solution(mesh):
    tile = P(("sector", "span"))
    rows = P(("sector", "span"), None)
    return jax.shard_map(
        per_device,
        mesh=mesh,
        in_specs=(rows, rows, tile, tile, P(("sector", "span"), None, None), tile, rows) + (P(),) * 8,
        out_specs=(rows, rows) + (P(),) * 8,
        check_vma=False,
    )
```

```python
import functools

import jax
import jax.numpy as jnp
from jax import lax
from jax.experimental import pallas as pl
from jax.experimental.pallas import tpu as pltpu
from jax.sharding import PartitionSpec as P

F32, BF16 = jnp.float32, jnp.bfloat16
MESH = pl.DeviceIdType.MESH
STEPS = 2
EPS = 1e-05
YH, YL, ZH, C, X, ZL = 4, 2, 4, 2, 4, 2
NODES, SLOTS, D, HALO = 256, 1024, 128, 32
CHUNK, BACK_CHUNK = 512, 1024
STEP1, NODE0, EDGE0 = 0, 1, 2
ROWS = (1024, 512, 512)
BASE = (0, 1024, 1536)
SMALL = (896, 384)


def dot(a, b):
    return jnp.dot(a, b, preferred_element_type=F32)


def dot_first(a, b):
    return lax.dot_general(a, b, (((0,), (0,)), ((), ())), preferred_element_type=F32)


def dot_last(a, b):
    return lax.dot_general(a, b, (((1,), (1,)), ((), ())), preferred_element_type=F32)


def ones_where(mask):
    return jnp.where(mask, 1.0, 0.0).astype(BF16)


def activate(lin):
    sig = 0.5 * jnp.tanh(0.5 * lin) + 0.5
    act = lin * sig
    return act, sig + act * (1.0 - sig)


def centred(weight):
    weight = weight.astype(F32)
    return weight - jnp.mean(weight, axis=-1, keepdims=True)


def normalized(proj):
    inv = lax.rsqrt(jnp.mean(proj * proj, axis=-1, keepdims=True) + EPS)
    return proj * inv, inv


def normalized_back(dout, xhat, inv, gain):
    prod = dout * xhat
    along = jnp.mean(prod * gain, axis=-1, keepdims=True)
    return inv * (dout * gain - xhat * along), jnp.sum(prod, axis=0, keepdims=True)


def kernel(
    *refs,
):
    sources, counts, outs, here, refs = refs[:5] + refs[6:15], refs[5], refs[15:18], refs[18:32], refs[32:]
    nodes, edges, snd, rcv, halo, cot, ef, eb, es, eg, nf, nb, ns, ng = here
    node_grad, edge_grad, total = outs
    (
    own_pick, rest, spread, hal_pad, h1, part, act_e, slope_e, xhat_e, inv_e, act_n, slope_n, xhat_n, inv_n,
    node_in, edge_new, de, dlin, dproj, dh,
    edges_t, act_t, es_c, ns_c, halo_out, halo_in, grads, mid, got1_a, got1_b, got1_c, got2_a, got2_b, got2_c,
    in_sem, halo_ssem, halo_rsem, red_ssem, red_rsem, ready,
    ) = refs
    sector, span = lax.axis_index("sector"), lax.axis_index("span")
    n_sector, n_span = YH * YL * ZH * C, X * ZL
    yh, yl = sector // (YL * ZH * C), lax.rem(sector // (ZH * C), YL)
    zh, c = lax.rem(sector // C, ZH), lax.rem(sector, C)
    x, zl = span // ZL, lax.rem(span, ZL)
    g1, g2 = YL * ZL * X * C, YH * ZH
    me1, me2 = ((yl * ZL + zl) * X + x) * C + c, yh * ZH + zh
    units = tuple(n // g1 for n in ROWS)
    got1, got2 = (got1_a, got1_b, got1_c), (got2_a, got2_b, got2_c)

    def turned(at, size):
        return [at] + [lax.rem(at + k, size) for k in range(1, size)]

    yls, zls, xs, cs = turned(yl, YL), turned(zl, ZL), turned(x, X), turned(c, C)
    yhs, zhs = turned(yh, YH), turned(zh, ZH)
    offsets1 = [(a, b, d, e) for a in range(YL) for b in range(ZL) for d in range(X) for e in range(C)][1:]
    offsets1.sort(key=lambda o: -(o[0] + o[1] + min(o[2], X - o[2]) + 0.5 * o[3]))
    peers1 = [
        (
            ((yls[a] * ZL + zls[b]) * X + xs[d]) * C + cs[e],
            (((yh * YL + yls[a]) * ZH + zh) * C + cs[e], xs[d] * ZL + zls[b]),
        )
        for a, b, d, e in offsets1
    ]
    offsets2 = [(a, b) for a in range(YH) for b in range(ZH)][1:]
    offsets2.sort(key=lambda o: -(min(o[0], YH - o[0]) + min(o[1], ZH - o[1])))
    peers2 = [(((yhs[a] * YL + yl) * ZH + zhs[b]) * C + c, span) for a, b in offsets2]

    around = (
        (lax.rem(sector + n_sector - 1, n_sector), span),
        (lax.rem(sector + 1, n_sector), span),
        (sector, lax.rem(span + n_span - 1, n_span)),
        (sector, lax.rem(span + 1, n_span)),
    )

    barrier = pltpu.get_barrier_semaphore()
    for peer in around:
        pl.semaphore_signal(barrier, inc=1, device_id=peer, device_id_type=MESH)

    lines = [peer for peer, (a, b) in zip(peers2, offsets2) if b == 0]
    greeted = [peer for _, peer in peers1] + [peer for peer, (a, b) in zip(peers2, offsets2) if a == 0 or b == 0]
    for peer in greeted:
        pl.semaphore_signal(barrier, inc=1, device_id=peer, device_id_type=MESH)

    loads = [pltpu.make_async_copy(a, b, in_sem.at[i]) for i, (a, b) in enumerate(zip(sources, here))]
    first = (4, 0, 2, 3, 1)
    rest_loads = [i for i in range(14) if i not in first]
    for i in (*first, *rest_loads):
        loads[i].start()
    loads[4].wait()
    loads[0].wait()

    hal_pad[...] = jnp.zeros_like(hal_pad)
    hal_pad[0:4, 0:HALO] = halo[0].astype(F32)
    padded = hal_pad[...]
    lane = lax.broadcasted_iota(jnp.int32, (1, D), 1)
    flat = jnp.zeros((1, D), F32)
    for k in range(4):
        row = padded[k : k + 1, :] if k == 0 else pltpu.roll(padded, HALO * k, 1)[k : k + 1, :]
        flat = jnp.where((lane >= HALO * k) & (lane < HALO * (k + 1)), row, flat)
    lane_f = lax.broadcasted_iota(jnp.int32, (D, D), 1).astype(F32)
    down = jnp.broadcast_to(flat, (D, D)).T
    halo_pick = jnp.concatenate([ones_where(down == lane_f), ones_where(down == lane_f + D)], axis=1)
    halo_spread = ones_where(lax.broadcasted_iota(jnp.int32, (NODES, D), 0).astype(F32) == flat)

    row_id = lax.broadcasted_iota(jnp.int32, (4 * HALO, 1), 0)
    outside = ((row_id >= 2 * HALO) & (row_id < 3 * HALO) & (span == 0)) | (
        (row_id >= 3 * HALO) & (span == n_span - 1)
    )

    apart = pl.when(sector >= 0)

    def exchange_start(t):
        for k in range(4):
            pltpu.make_async_remote_copy(
                src_ref=halo_out.at[t, pl.ds(k * HALO, HALO)],
                dst_ref=halo_in.at[t, pl.ds((k ^ 1) * HALO, HALO)],
                send_sem=halo_ssem.at[t],
                recv_sem=halo_rsem.at[t],
                device_id=around[k],
                device_id_type=MESH,
            ).start()

    def exchange_wait(t):
        pltpu.make_async_copy(halo_in.at[t], halo_in.at[t], halo_rsem.at[t]).wait()

    halo_out[0] = dot(halo_pick, nodes[...]).astype(BF16)
    pl.semaphore_wait(barrier, 4 + len(greeted))
    exchange_start(0)
    for peer in lines:
        pl.semaphore_signal(ready, inc=1, device_id=peer, device_id_type=MESH)

    for i in first[2:]:
        loads[i].wait()
    used = counts[0]
    slot = lax.broadcasted_iota(jnp.int32, (SLOTS // D, D), 0) * D + lax.broadcasted_iota(
        jnp.int32, (SLOTS // D, D), 1
    )
    snd_f = jnp.where(slot < used, snd[...], -1).astype(F32)
    rcv_f = jnp.where(slot < used, rcv[...], -1).astype(F32)
    down_f = lax.broadcasted_iota(jnp.int32, (NODES + 4 * HALO, D), 0).astype(F32)
    for r in range(SLOTS // D):
        at = pl.ds(r * D, D)
        s_row, r_row = snd_f[r : r + 1, :], rcv_f[r : r + 1, :]
        spread[0:384, at] = ones_where(down_f == s_row)
        spread[384:640, at] = ones_where(down_f[0:256] == r_row)
        s_col = jnp.broadcast_to(s_row, (D, D)).T
        r_col = jnp.broadcast_to(r_row, (D, D)).T
        own_pick[at, 0:128] = ones_where(s_col == lane_f)
        own_pick[at, 128:256] = ones_where(s_col == lane_f + 128.0)
        own_pick[at, 256:384] = ones_where(r_col == lane_f)
        own_pick[at, 384:512] = ones_where(r_col == lane_f + 128.0)
        rest[at, 0:128] = ones_where(s_col == lane_f + 256.0)
    rest[:, 128:256] = edges[...]
    for i in rest_loads:
        loads[i].wait()

    edges_t[...] = edges[...].T
    for t in range(STEPS):
        es_c[t] = centred(es[t]).astype(BF16)
        ns_c[t] = centred(ns[t]).astype(BF16)

    def forward(t):
        h = nodes[...] if t == 0 else h1[...]
        bias, gain = eb[t : t + 1, :], eg[t : t + 1, :]

        @apart
        def _():
            own_table = jnp.concatenate(
                [dot(h, ef[t, 0:128, :]).astype(BF16), dot(h, ef[t, 128:256, :]).astype(BF16)], axis=0
            )
            for i in range(SLOTS // CHUNK):
                at = pl.ds(i * CHUNK, CHUNK)
                part[at, :] = dot(own_pick[at, :], own_table) + bias
            if t == 1:
                act_t[...] = act_e[0].T

        exchange_wait(t)
        halo_in[t] = jnp.where(outside, 0.0, halo_in[t].astype(F32)).astype(BF16)
        rest_table = jnp.concatenate(
            [dot(halo_in[t], ef[t, 0:128, :]).astype(BF16), ef[t, 256:384, :]], axis=0
        )
        for i in range(SLOTS // CHUNK):
            at = pl.ds(i * CHUNK, CHUNK)
            lin = part[at, :] + dot(rest[at, :], rest_table)
            act, slope = activate(lin)
            act = act.astype(BF16)
            act_e[t, at, :] = act
            slope_e[t, at, :] = slope
            xhat, inv = normalized(dot(act, es_c[t]))
            xhat_e[t, at, :] = xhat
            inv_e[t, at, :] = inv
            new = (rest[at, 128:256].astype(F32) + xhat * gain).astype(BF16)
            edge_new[at, :] = new
        summed = dot(spread[384:640, :], edge_new[...]).astype(BF16)
        if t + 1 < STEPS:
            rest[:, 128:256] = edge_new[...]
        node_in[t, :, 0:128] = h
        node_in[t, :, 128:256] = summed
        act, slope = activate(dot(node_in[t], nf[t]) + nb[t : t + 1, :])
        act = act.astype(BF16)
        act_n[t] = act
        slope_n[t] = slope
        xhat, inv = normalized(dot(act, ns_c[t]))
        xhat_n[t] = xhat
        inv_n[t] = inv
        if t + 1 < STEPS:
            new_h = (h.astype(F32) + xhat * ng[t : t + 1, :]).astype(BF16)
            h1[...] = new_h
            halo_out[t + 1] = dot(halo_pick, new_h).astype(BF16)
            exchange_start(t + 1)

    def reduce_start(i, held=None, only=None):
        unit = units[i]

        def copy(j, peer):
            pltpu.make_async_remote_copy(
                src_ref=grads.at[pl.ds(pl.multiple_of(BASE[i] + j * unit, unit), unit)],
                dst_ref=got1[i].at[me1],
                send_sem=red_ssem.at[i, 0],
                recv_sem=red_rsem.at[i, 0],
                device_id=peer,
                device_id_type=MESH,
            ).start()

        if only is not None:
            at = only // (ZL * X * C), only // (X * C) % ZL, only // C % X, only % C
            peer = (((yh * YL + at[0]) * ZH + zh) * C + at[3], at[2] * ZL + at[1])
            pl.when(me1 != only)(lambda: copy(only, peer))
            return
        for j, peer in peers1:
            if held is None:
                copy(j, peer)
            else:
                pl.when(j != held)(functools.partial(copy, j, peer))

    def reduce_middle(i):
        unit = units[i]
        others = got1[i].at[pl.ds(1, g1 - 1)]
        pltpu.make_async_copy(others, others, red_rsem.at[i, 0]).wait()
        got1[i][me1] = grads[pl.ds(pl.multiple_of(BASE[i] + me1 * unit, unit), unit), :]
        acc = got1[i][0].astype(F32)
        for k in range(1, g1):
            acc = acc + got1[i][k].astype(F32)
        acc = acc.astype(BF16)
        block = pl.ds(BASE[i] // g1, unit)
        mid[block, :] = acc
        got2[i][me2] = acc

        for peer in peers2:
            pltpu.make_async_remote_copy(
                src_ref=mid.at[block],
                dst_ref=got2[i].at[me2],
                send_sem=red_ssem.at[i, 1],
                recv_sem=red_rsem.at[i, 1],
                device_id=peer,
                device_id_type=MESH,
            ).start()

    def reduce_last(i):
        unit = units[i]
        others = got2[i].at[pl.ds(1, g2 - 1)]
        pltpu.make_async_copy(others, others, red_rsem.at[i, 1]).wait()
        acc = got2[i][0].astype(F32)
        for k in range(1, g2):
            acc = acc + got2[i][k].astype(F32)
        scale = jnp.float32(NODES * n_sector * n_span) ** (-0.5)
        mine = pl.ds(pl.multiple_of(BASE[i] + me1 * unit, unit), unit)
        total[mine, :] = (acc * scale).astype(BF16)

        for _, peer in peers1:
            pltpu.make_async_remote_copy(
                src_ref=total.at[mine],
                dst_ref=total.at[mine],
                send_sem=red_ssem.at[i, 2],
                recv_sem=red_rsem.at[i, 2],
                device_id=peer,
                device_id_type=MESH,
            ).start()

    def reduce_finish(i):
        others = total.at[pl.ds(BASE[i], ROWS[i] - units[i])]
        pltpu.make_async_copy(others, others, red_rsem.at[i, 2]).wait()

    def reduce_sent(i):
        for phase, ref, count in ((0, got1[i], g1), (1, got2[i], g2), (2, got1[i], g1)):
            sent = ref.at[pl.ds(1, count - 1)]
            pltpu.make_async_copy(sent, sent, red_ssem.at[i, phase]).wait()

    def backward(t):
        last = t + 1 == STEPS
        h = nodes[...] if t == 0 else h1[...]
        dy = cot[...].astype(F32) if last else dh[...]
        dproj_n, dgain_n = normalized_back(dy, xhat_n[t], inv_n[t], ng[t : t + 1, :])
        dproj_n = dproj_n.astype(BF16)
        dlin_n = dot_last(dproj_n, ns_c[t]) * slope_n[t]
        dbias_n = jnp.sum(dlin_n, axis=0, keepdims=True)
        dlin_n = dlin_n.astype(BF16)
        dsummed = dot_last(dlin_n, nf[t, 128:256, :]).astype(BF16)
        node_at = BASE[STEP1] + 512 if last else BASE[NODE0]
        small_at = BASE[STEP1] + SMALL[STEP1] if last else BASE[NODE0] + SMALL[NODE0]
        held = SMALL[NODE0] // units[NODE0]

        def node_grads():
            grads[node_at : node_at + 256, :] = dot_first(node_in[t], dlin_n).astype(BF16)
            grads[node_at + 256 : node_at + 384, :] = centred(dot_first(act_n[t], dproj_n)).astype(BF16)

        small_rows = 128 if last else units[NODE0]
        if not last:
            node_grads()
            if small_rows < 128:
                grads[small_at + small_rows : small_at + 128, :] = jnp.zeros((128 - small_rows, D), BF16)
            reduce_start(NODE0, held=held)
        dgain_e = jnp.zeros((1, D), F32)
        gain = eg[t : t + 1, :]
        for i in range(SLOTS // BACK_CHUNK):
            at = pl.ds(i * BACK_CHUNK, BACK_CHUNK)
            dnew = dot(own_pick[at, 256:512], dsummed)
            if not last:
                dnew = dnew + de[at, :]
            de[at, :] = dnew
            dp, dg = normalized_back(dnew, xhat_e[t, at, :], inv_e[t, at, :], gain)
            dgain_e = dgain_e + dg
            dp = dp.astype(BF16)
            dproj[at, :] = dp
            dl = (dot_last(dp, es_c[t]) * slope_e[t, at, :]).astype(BF16)
            dlin[at, :] = dl

        def send_back(sums):
            dhalo = dot_last(sums.astype(BF16), ef[t, 0:128, :])
            halo_out[STEPS + t] = jnp.where(outside, 0.0, dhalo).astype(BF16)
            exchange_start(STEPS + t)

        edge_at = BASE[STEP1] if last else BASE[EDGE0]

        def edge_grads(sums, sums_b):
            grads[edge_at : edge_at + 128, :] = (
                dot_first(h, sums_b[0:256]) + dot_first(halo_in[t], sums_b[256:384])
            ).astype(BF16)
            grads[edge_at + 128 : edge_at + 256, :] = dot_first(h, sums_b[384:640]).astype(BF16)
            grads[edge_at + 256 : edge_at + 384, :] = (dot_first(rest[:, 128:256], dlin[...]) if last else dot(edges_t[...], dlin[...])).astype(BF16)
            grads[edge_at + 384 : edge_at + 512, :] = centred(
                dot_first(act_e[t], dproj[...]) if last else dot(act_t[...], dproj[...])
            ).astype(BF16)
            dbias_e = jnp.sum(sums[384:640], axis=0, keepdims=True)
            grads[small_at : small_at + small_rows, :] = jnp.concatenate(
                [dbias_e, dgain_e, dbias_n, dgain_n, jnp.zeros((small_rows - 4, D), F32)], axis=0
            ).astype(BF16)

        def own_part(sums_b):
            dh[...] = (
                dy
                + dot_last(dlin_n, nf[t, 0:128, :])
                + dot_last(sums_b[0:256], ef[t, 0:128, :])
                + dot_last(sums_b[384:640], ef[t, 128:256, :])
            )

        def older_edges():
            for i in range(SLOTS // BACK_CHUNK):
                at = pl.ds(i * BACK_CHUNK, BACK_CHUNK)
                dold = de[at, :] + dot_last(dlin[at, :], ef[t, 256:384, :])
                if last:
                    de[at, :] = dold
                else:
                    edge_grad[at, :] = dold.astype(BF16)

        if last:
            send_back(dot(spread[256:384, :], dlin[...]))

            @apart
            def _():
                sums = dot(spread[...], dlin[...])
                sums_b = sums.astype(BF16)
                edge_grads(sums, sums_b)
                node_grads()
                reduce_start(STEP1)
                own_part(sums_b)
                older_edges()
        else:
            sums = dot(spread[...], dlin[...])
            sums_b = sums.astype(BF16)
            edge_grads(sums, sums_b)
            reduce_start(EDGE0)
            reduce_start(NODE0, only=held)

            @apart
            def _():
                send_back(sums[256:384])
                own_part(sums_b)
                older_edges()

        if not last:
            pl.semaphore_wait(ready, YH - 1)
            reduce_middle(STEP1)
            reduce_middle(NODE0)
        exchange_wait(STEPS + t)
        own = (dh[...] + dot(halo_spread, halo_in[STEPS + t])).astype(BF16)
        if last:
            dh[...] = own.astype(F32)
        else:
            node_grad[...] = own

    forward(0)
    forward(1)
    backward(1)
    backward(0)
    reduce_middle(EDGE0)
    for i in (STEP1, NODE0, EDGE0):
        reduce_last(i)
    for i in (STEP1, NODE0, EDGE0):
        reduce_finish(i)
    for i in (STEP1, NODE0, EDGE0):
        reduce_sent(i)
    for t in range(2 * STEPS):
        pltpu.make_async_copy(halo_out.at[t], halo_out.at[t], halo_ssem.at[t]).wait()


def finish(node_grad, edge_grad, total, *refs):
    outs, wide, small, sem = refs[:10], refs[10], refs[11], refs[12]
    copies = [pltpu.make_async_copy(edge_grad, outs[1], sem.at[0]), pltpu.make_async_copy(node_grad, outs[0], sem.at[1])]
    for copy in copies:
        copy.start()
    where = ((BASE[EDGE0], BASE[STEP1]), (BASE[NODE0], BASE[STEP1] + 512))
    for out, part, first, count in ((2, 0, 0, 384), (4, 0, 384, 128), (6, 1, 0, 256), (8, 1, 256, 128)):
        to = part * 512 + first
        for t in range(STEPS):
            start = where[part][t] + first
            wide[t, to : to + count, :] = total[start : start + count, :].astype(F32)
        copy = pltpu.make_async_copy(wide.at[:, pl.ds(to, count), :], outs[out], sem.at[out])
        copy.start()
        copies.append(copy)
    smalls = (BASE[NODE0] + SMALL[NODE0], BASE[STEP1] + SMALL[STEP1])
    for t in range(STEPS):
        rows = total[smalls[t] : smalls[t] + 16, :].astype(F32)
        for k in range(4):
            small[k, t : t + 1, :] = rows[k : k + 1, :]
    for k, out in enumerate((3, 5, 7, 9)):
        copy = pltpu.make_async_copy(small.at[k], outs[out], sem.at[out])
        copy.start()
        copies.append(copy)
    for copy in copies:
        copy.wait()


def per_device(
    node_latents, edge_latents, senders, receivers, halo_rows, counts, cotangent,
    edge_first, edge_bias, edge_second, edge_gain, node_first, node_bias, node_second, node_gain,
):
    g1, g2 = YL * ZL * X * C, YH * ZH
    vmem, anywhere = pl.BlockSpec(memory_space=pltpu.VMEM), pl.BlockSpec(memory_space=pl.ANY)
    smem, hbm = pl.BlockSpec(memory_space=pltpu.SMEM), pl.BlockSpec(memory_space=pltpu.HBM)
    weights = (edge_first, edge_bias, edge_second, edge_gain, node_first, node_bias, node_second, node_gain)
    args = (
        node_latents, edge_latents, senders.reshape(SLOTS // D, D), receivers.reshape(SLOTS // D, D),
        halo_rows, counts, cotangent, *weights,
    )
    parts = pl.pallas_call(
        kernel,
        out_shape=(
            jax.ShapeDtypeStruct((NODES, D), BF16),
            jax.ShapeDtypeStruct((SLOTS, D), BF16),
            jax.ShapeDtypeStruct((sum(ROWS), D), BF16),
        ),
        in_specs=[smem if i == 5 else hbm for i in range(15)],
        out_specs=[vmem] * 3,
        scratch_shapes=[
            *(pltpu.VMEM(a.shape, a.dtype) for i, a in enumerate(args) if i != 5),
            pltpu.VMEM((SLOTS, 512), BF16),
            pltpu.VMEM((SLOTS, 256), BF16),
            pltpu.VMEM((640, SLOTS), BF16),
            pltpu.VMEM((8, D), F32),
            pltpu.VMEM((NODES, D), BF16),
            pltpu.VMEM((SLOTS, D), F32),
            pltpu.VMEM((STEPS, SLOTS, D), BF16),
            pltpu.VMEM((STEPS, SLOTS, D), F32),
            pltpu.VMEM((STEPS, SLOTS, D), F32),
            pltpu.VMEM((STEPS, SLOTS, 1), F32),
            pltpu.VMEM((STEPS, NODES, D), BF16),
            pltpu.VMEM((STEPS, NODES, D), F32),
            pltpu.VMEM((STEPS, NODES, D), F32),
            pltpu.VMEM((STEPS, NODES, 1), F32),
            pltpu.VMEM((STEPS, NODES, 256), BF16),
            pltpu.VMEM((SLOTS, D), BF16),
            pltpu.VMEM((SLOTS, D), F32),
            pltpu.VMEM((SLOTS, D), BF16),
            pltpu.VMEM((SLOTS, D), BF16),
            pltpu.VMEM((NODES, D), F32),
            pltpu.VMEM((D, SLOTS), BF16),
            pltpu.VMEM((D, SLOTS), BF16),
            pltpu.VMEM((STEPS, D, D), BF16),
            pltpu.VMEM((STEPS, D, D), BF16),
            pltpu.VMEM((2 * STEPS, 4 * HALO, D), BF16),
            pltpu.VMEM((2 * STEPS, 4 * HALO, D), BF16),
            pltpu.VMEM((sum(ROWS), D), BF16),
            pltpu.VMEM((sum(ROWS) // g1, D), BF16),
            *(pltpu.VMEM((g1, n // g1, D), BF16) for n in ROWS),
            *(pltpu.VMEM((g2, n // g1, D), BF16) for n in ROWS),
            pltpu.SemaphoreType.DMA((14,)),
            pltpu.SemaphoreType.DMA((2 * STEPS,)),
            pltpu.SemaphoreType.DMA((2 * STEPS,)),
            pltpu.SemaphoreType.DMA((3, 3)),
            pltpu.SemaphoreType.DMA((3, 3)),
            pltpu.SemaphoreType.REGULAR,
        ],
        compiler_params=pltpu.CompilerParams(
            collective_id=0, has_side_effects=True, vmem_limit_bytes=40 * 1024 * 1024
        ),
        name="steps",
    )(*(a if i == 5 else pltpu.with_memory_space_constraint(a, pltpu.HBM) for i, a in enumerate(args)))
    return pl.pallas_call(
        finish,
        out_shape=(
            jax.ShapeDtypeStruct((NODES, D), BF16),
            jax.ShapeDtypeStruct((SLOTS, D), BF16),
            *(jax.ShapeDtypeStruct(w.shape, F32) for w in weights),
        ),
        in_specs=[vmem] * 3,
        out_specs=[anywhere] * 10,
        scratch_shapes=[
            pltpu.VMEM((STEPS, 896, D), F32),
            pltpu.VMEM((4, STEPS, D), F32),
            pltpu.SemaphoreType.DMA((10,)),
        ],
        compiler_params=pltpu.CompilerParams(vmem_limit_bytes=40 * 1024 * 1024),
        name="finish",
    )(*parts)


def solution(mesh):
    tile = P(("sector", "span"))
    rows = P(("sector", "span"), None)
    return jax.shard_map(
        per_device,
        mesh=mesh,
        in_specs=(rows, rows, tile, tile, P(("sector", "span"), None, None), tile, rows) + (P(),) * 8,
        out_specs=(rows, rows) + (P(),) * 8,
        check_vma=False,
    )
```

```python
import functools

import jax
import jax.numpy as jnp
from jax import lax
from jax.experimental import pallas as pl
from jax.experimental.pallas import tpu as pltpu
from jax.sharding import PartitionSpec as P

F32, BF16 = jnp.float32, jnp.bfloat16
MESH = pl.DeviceIdType.MESH
STEPS = 2
EPS = 1e-05
YH, YL, ZH, C, X, ZL = 4, 2, 4, 2, 4, 2
NODES, SLOTS, D, HALO = 256, 1024, 128, 32
CHUNK, BACK_CHUNK = 512, 1024
STEP1, NODE0, EDGE0 = 0, 1, 2
ROWS = (1024, 512, 512)
BASE = (0, 1024, 1536)
SMALL = (896, 384)
JOINED = ((STEP1,), (NODE0, EDGE0))


def dot(a, b):
    return jnp.dot(a, b, preferred_element_type=F32)


def dot_first(a, b):
    return lax.dot_general(a, b, (((0,), (0,)), ((), ())), preferred_element_type=F32)


def dot_last(a, b):
    return lax.dot_general(a, b, (((1,), (1,)), ((), ())), preferred_element_type=F32)


def ones_where(mask):
    return jnp.where(mask, 1.0, 0.0).astype(BF16)


def activate(lin):
    sig = 0.5 * jnp.tanh(0.5 * lin) + 0.5
    act = lin * sig
    return act, sig + act * (1.0 - sig)


def centred(weight):
    weight = weight.astype(F32)
    return weight - jnp.mean(weight, axis=-1, keepdims=True)


def normalized(proj):
    inv = lax.rsqrt(jnp.mean(proj * proj, axis=-1, keepdims=True) + EPS)
    return proj * inv, inv


def normalized_back(dout, xhat, inv, gain):
    prod = dout * xhat
    along = jnp.mean(prod * gain, axis=-1, keepdims=True)
    return inv * (dout * gain - xhat * along), jnp.sum(prod, axis=0, keepdims=True)


def kernel(
    *refs,
):
    sources, counts, outs, here, refs = refs[:5] + refs[6:15], refs[5], refs[15:18], refs[18:32], refs[32:]
    nodes, edges, snd, rcv, halo, cot, ef, eb, es, eg, nf, nb, ns, ng = here
    node_grad, edge_grad, total = outs
    (
    own_pick, rest, spread, hal_pad, h1, part, act_e, slope_e, xhat_e, inv_e, act_n, slope_n, xhat_n, inv_n,
    node_in, edge_new, de, dlin, dproj, dh,
    edges_t, act_t, es_c, ns_c, halo_out, halo_in, grads, mid, got1_a, got1_b, got1_c, got2_a, got2_b,
    in_sem, halo_ssem, halo_rsem, red_ssem, red_rsem, ready,
    ) = refs
    sector, span = lax.axis_index("sector"), lax.axis_index("span")
    n_sector, n_span = YH * YL * ZH * C, X * ZL
    yh, yl = sector // (YL * ZH * C), lax.rem(sector // (ZH * C), YL)
    zh, c = lax.rem(sector // C, ZH), lax.rem(sector, C)
    x, zl = span // ZL, lax.rem(span, ZL)
    g1, g2 = YL * ZL * X * C, YH * ZH
    me1, me2 = ((yl * ZL + zl) * X + x) * C + c, yh * ZH + zh
    units = tuple(n // g1 for n in ROWS)
    got1, got2 = (got1_a, got1_b, got1_c), (got2_a, got2_b)
    wide = tuple(sum(units[i] for i in members) for members in JOINED)
    wide_base = tuple(BASE[members[0]] for members in JOINED)

    def turned(at, size):
        return [at] + [lax.rem(at + k, size) for k in range(1, size)]

    yls, zls, xs, cs = turned(yl, YL), turned(zl, ZL), turned(x, X), turned(c, C)
    yhs, zhs = turned(yh, YH), turned(zh, ZH)
    offsets1 = [(a, b, d, e) for a in range(YL) for b in range(ZL) for d in range(X) for e in range(C)][1:]
    offsets1.sort(key=lambda o: -(o[0] + o[1] + min(o[2], X - o[2]) + 0.5 * o[3]))
    peers1 = [
        (
            ((yls[a] * ZL + zls[b]) * X + xs[d]) * C + cs[e],
            (((yh * YL + yls[a]) * ZH + zh) * C + cs[e], xs[d] * ZL + zls[b]),
        )
        for a, b, d, e in offsets1
    ]
    offsets2 = [(a, b) for a in range(YH) for b in range(ZH)][1:]
    offsets2.sort(key=lambda o: -(min(o[0], YH - o[0]) + min(o[1], ZH - o[1])))
    peers2 = [(((yhs[a] * YL + yl) * ZH + zhs[b]) * C + c, span) for a, b in offsets2]

    around = (
        (lax.rem(sector + n_sector - 1, n_sector), span),
        (lax.rem(sector + 1, n_sector), span),
        (sector, lax.rem(span + n_span - 1, n_span)),
        (sector, lax.rem(span + 1, n_span)),
    )

    barrier = pltpu.get_barrier_semaphore()
    for peer in around:
        pl.semaphore_signal(barrier, inc=1, device_id=peer, device_id_type=MESH)

    lines = [peer for peer, (a, b) in zip(peers2, offsets2) if b == 0]
    greeted = [peer for _, peer in peers1] + [peer for peer, (a, b) in zip(peers2, offsets2) if a == 0 or b == 0]
    for peer in greeted:
        pl.semaphore_signal(barrier, inc=1, device_id=peer, device_id_type=MESH)

    loads = [pltpu.make_async_copy(a, b, in_sem.at[i]) for i, (a, b) in enumerate(zip(sources, here))]
    first = (4, 0, 2, 3, 1)
    rest_loads = [i for i in range(14) if i not in first]
    for i in (*first, *rest_loads):
        loads[i].start()
    loads[4].wait()
    loads[0].wait()

    hal_pad[...] = jnp.zeros_like(hal_pad)
    hal_pad[0:4, 0:HALO] = halo[0].astype(F32)
    padded = hal_pad[...]
    lane = lax.broadcasted_iota(jnp.int32, (1, D), 1)
    flat = jnp.zeros((1, D), F32)
    for k in range(4):
        row = padded[k : k + 1, :] if k == 0 else pltpu.roll(padded, HALO * k, 1)[k : k + 1, :]
        flat = jnp.where((lane >= HALO * k) & (lane < HALO * (k + 1)), row, flat)
    lane_f = lax.broadcasted_iota(jnp.int32, (D, D), 1).astype(F32)
    down = jnp.broadcast_to(flat, (D, D)).T
    halo_pick = jnp.concatenate([ones_where(down == lane_f), ones_where(down == lane_f + D)], axis=1)
    halo_spread = ones_where(lax.broadcasted_iota(jnp.int32, (NODES, D), 0).astype(F32) == flat)

    row_id = lax.broadcasted_iota(jnp.int32, (4 * HALO, 1), 0)
    outside = ((row_id >= 2 * HALO) & (row_id < 3 * HALO) & (span == 0)) | (
        (row_id >= 3 * HALO) & (span == n_span - 1)
    )

    apart = pl.when(sector >= 0)

    def exchange_start(t):
        for k in range(4):
            pltpu.make_async_remote_copy(
                src_ref=halo_out.at[t, pl.ds(k * HALO, HALO)],
                dst_ref=halo_in.at[t, pl.ds((k ^ 1) * HALO, HALO)],
                send_sem=halo_ssem.at[t],
                recv_sem=halo_rsem.at[t],
                device_id=around[k],
                device_id_type=MESH,
            ).start()

    def exchange_wait(t):
        pltpu.make_async_copy(halo_in.at[t], halo_in.at[t], halo_rsem.at[t]).wait()

    halo_out[0] = dot(halo_pick, nodes[...]).astype(BF16)
    pl.semaphore_wait(barrier, 4 + len(greeted))
    exchange_start(0)
    for peer in lines:
        pl.semaphore_signal(ready, inc=1, device_id=peer, device_id_type=MESH)

    for i in first[2:]:
        loads[i].wait()
    used = counts[0]
    slot = lax.broadcasted_iota(jnp.int32, (SLOTS // D, D), 0) * D + lax.broadcasted_iota(
        jnp.int32, (SLOTS // D, D), 1
    )
    snd_f = jnp.where(slot < used, snd[...], -1).astype(F32)
    rcv_f = jnp.where(slot < used, rcv[...], -1).astype(F32)
    down_f = lax.broadcasted_iota(jnp.int32, (NODES + 4 * HALO, D), 0).astype(F32)
    for r in range(SLOTS // D):
        at = pl.ds(r * D, D)
        s_row, r_row = snd_f[r : r + 1, :], rcv_f[r : r + 1, :]
        spread[0:384, at] = ones_where(down_f == s_row)
        spread[384:640, at] = ones_where(down_f[0:256] == r_row)
        s_col = jnp.broadcast_to(s_row, (D, D)).T
        r_col = jnp.broadcast_to(r_row, (D, D)).T
        own_pick[at, 0:128] = ones_where(s_col == lane_f)
        own_pick[at, 128:256] = ones_where(s_col == lane_f + 128.0)
        own_pick[at, 256:384] = ones_where(r_col == lane_f)
        own_pick[at, 384:512] = ones_where(r_col == lane_f + 128.0)
        rest[at, 0:128] = ones_where(s_col == lane_f + 256.0)
    rest[:, 128:256] = edges[...]
    for i in rest_loads:
        loads[i].wait()

    edges_t[...] = edges[...].T
    for t in range(STEPS):
        es_c[t] = centred(es[t]).astype(BF16)
        ns_c[t] = centred(ns[t]).astype(BF16)

    def forward(t):
        h = nodes[...] if t == 0 else h1[...]
        bias, gain = eb[t : t + 1, :], eg[t : t + 1, :]

        @apart
        def _():
            own_table = jnp.concatenate(
                [dot(h, ef[t, 0:128, :]).astype(BF16), dot(h, ef[t, 128:256, :]).astype(BF16)], axis=0
            )
            for i in range(SLOTS // CHUNK):
                at = pl.ds(i * CHUNK, CHUNK)
                part[at, :] = dot(own_pick[at, :], own_table) + bias
            if t == 1:
                act_t[...] = act_e[0].T

        exchange_wait(t)
        halo_in[t] = jnp.where(outside, 0.0, halo_in[t].astype(F32)).astype(BF16)
        rest_table = jnp.concatenate(
            [dot(halo_in[t], ef[t, 0:128, :]).astype(BF16), ef[t, 256:384, :]], axis=0
        )
        for i in range(SLOTS // CHUNK):
            at = pl.ds(i * CHUNK, CHUNK)
            lin = part[at, :] + dot(rest[at, :], rest_table)
            act, slope = activate(lin)
            act = act.astype(BF16)
            act_e[t, at, :] = act
            slope_e[t, at, :] = slope
            xhat, inv = normalized(dot(act, es_c[t]))
            xhat_e[t, at, :] = xhat
            inv_e[t, at, :] = inv
            new = (rest[at, 128:256].astype(F32) + xhat * gain).astype(BF16)
            edge_new[at, :] = new
        summed = dot(spread[384:640, :], edge_new[...]).astype(BF16)
        if t + 1 < STEPS:
            rest[:, 128:256] = edge_new[...]
        node_in[t, :, 0:128] = h
        node_in[t, :, 128:256] = summed
        act, slope = activate(dot(node_in[t], nf[t]) + nb[t : t + 1, :])
        act = act.astype(BF16)
        act_n[t] = act
        slope_n[t] = slope
        xhat, inv = normalized(dot(act, ns_c[t]))
        xhat_n[t] = xhat
        inv_n[t] = inv
        if t + 1 < STEPS:
            new_h = (h.astype(F32) + xhat * ng[t : t + 1, :]).astype(BF16)
            h1[...] = new_h
            halo_out[t + 1] = dot(halo_pick, new_h).astype(BF16)
            exchange_start(t + 1)

    def reduce_start(i, held=None, only=None):
        unit = units[i]

        def copy(j, peer):
            pltpu.make_async_remote_copy(
                src_ref=grads.at[pl.ds(pl.multiple_of(BASE[i] + j * unit, unit), unit)],
                dst_ref=got1[i].at[me1],
                send_sem=red_ssem.at[i, 0],
                recv_sem=red_rsem.at[i, 0],
                device_id=peer,
                device_id_type=MESH,
            ).start()

        if only is not None:
            at = only // (ZL * X * C), only // (X * C) % ZL, only // C % X, only % C
            peer = (((yh * YL + at[0]) * ZH + zh) * C + at[3], at[2] * ZL + at[1])
            pl.when(me1 != only)(lambda: copy(only, peer))
            return
        for j, peer in peers1:
            if held is None:
                copy(j, peer)
            else:
                pl.when(j != held)(functools.partial(copy, j, peer))

    def reduce_middle(w):
        for i in JOINED[w]:
            unit = units[i]
            others = got1[i].at[pl.ds(1, g1 - 1)]
            pltpu.make_async_copy(others, others, red_rsem.at[i, 0]).wait()
            got1[i][me1] = grads[pl.ds(pl.multiple_of(BASE[i] + me1 * unit, unit), unit), :]
            acc = got1[i][0].astype(F32)
            for k in range(1, g1):
                acc = acc + got1[i][k].astype(F32)
            mid[pl.ds(BASE[i] // g1, unit), :] = acc.astype(BF16)
        block = pl.ds(wide_base[w] // g1, wide[w])
        got2[w][me2] = mid[block, :]
        for peer in peers2:
            pltpu.make_async_remote_copy(
                src_ref=mid.at[block],
                dst_ref=got2[w].at[me2],
                send_sem=red_ssem.at[w, 1],
                recv_sem=red_rsem.at[w, 1],
                device_id=peer,
                device_id_type=MESH,
            ).start()

    def reduce_last(w):
        others = got2[w].at[pl.ds(1, g2 - 1)]
        pltpu.make_async_copy(others, others, red_rsem.at[w, 1]).wait()
        acc = got2[w][0].astype(F32)
        for k in range(1, g2):
            acc = acc + got2[w][k].astype(F32)
        scale = jnp.float32(NODES * n_sector * n_span) ** (-0.5)
        mine = pl.ds(pl.multiple_of(wide_base[w] + me1 * wide[w], wide[w]), wide[w])
        total[mine, :] = (acc * scale).astype(BF16)
        for _, peer in peers1:
            pltpu.make_async_remote_copy(
                src_ref=total.at[mine],
                dst_ref=total.at[mine],
                send_sem=red_ssem.at[w, 2],
                recv_sem=red_rsem.at[w, 2],
                device_id=peer,
                device_id_type=MESH,
            ).start()

    def reduce_finish(w):
        others = total.at[pl.ds(wide_base[w], (g1 - 1) * wide[w])]
        pltpu.make_async_copy(others, others, red_rsem.at[w, 2]).wait()

    def reduce_sent():
        for i in (STEP1, NODE0, EDGE0):
            sent = got1[i].at[pl.ds(1, g1 - 1)]
            pltpu.make_async_copy(sent, sent, red_ssem.at[i, 0]).wait()
        for w in range(2):
            sent = got2[w].at[pl.ds(1, g2 - 1)]
            pltpu.make_async_copy(sent, sent, red_ssem.at[w, 1]).wait()
            sent = total.at[pl.ds(wide_base[w], (g1 - 1) * wide[w])]
            pltpu.make_async_copy(sent, sent, red_ssem.at[w, 2]).wait()

    def backward(t):
        last = t + 1 == STEPS
        h = nodes[...] if t == 0 else h1[...]
        dy = cot[...].astype(F32) if last else dh[...]
        dproj_n, dgain_n = normalized_back(dy, xhat_n[t], inv_n[t], ng[t : t + 1, :])
        dproj_n = dproj_n.astype(BF16)
        dlin_n = dot_last(dproj_n, ns_c[t]) * slope_n[t]
        dbias_n = jnp.sum(dlin_n, axis=0, keepdims=True)
        dlin_n = dlin_n.astype(BF16)
        dsummed = dot_last(dlin_n, nf[t, 128:256, :]).astype(BF16)
        node_at = BASE[STEP1] + 512 if last else BASE[NODE0]
        small_at = BASE[STEP1] + SMALL[STEP1] if last else BASE[NODE0] + SMALL[NODE0]
        held = SMALL[NODE0] // units[NODE0]

        def node_grads():
            grads[node_at : node_at + 256, :] = dot_first(node_in[t], dlin_n).astype(BF16)
            grads[node_at + 256 : node_at + 384, :] = centred(dot_first(act_n[t], dproj_n)).astype(BF16)

        small_rows = 128 if last else units[NODE0]
        if not last:
            node_grads()
            if small_rows < 128:
                grads[small_at + small_rows : small_at + 128, :] = jnp.zeros((128 - small_rows, D), BF16)
            reduce_start(NODE0, held=held)
        dgain_e = jnp.zeros((1, D), F32)
        gain = eg[t : t + 1, :]
        for i in range(SLOTS // BACK_CHUNK):
            at = pl.ds(i * BACK_CHUNK, BACK_CHUNK)
            dnew = dot(own_pick[at, 256:512], dsummed)
            if not last:
                dnew = dnew + de[at, :]
            de[at, :] = dnew
            dp, dg = normalized_back(dnew, xhat_e[t, at, :], inv_e[t, at, :], gain)
            dgain_e = dgain_e + dg
            dp = dp.astype(BF16)
            dproj[at, :] = dp
            dl = (dot_last(dp, es_c[t]) * slope_e[t, at, :]).astype(BF16)
            dlin[at, :] = dl

        def send_back(sums):
            dhalo = dot_last(sums.astype(BF16), ef[t, 0:128, :])
            halo_out[STEPS + t] = jnp.where(outside, 0.0, dhalo).astype(BF16)
            exchange_start(STEPS + t)

        edge_at = BASE[STEP1] if last else BASE[EDGE0]

        def edge_grads(sums, sums_b):
            grads[edge_at : edge_at + 128, :] = (
                dot_first(h, sums_b[0:256]) + dot_first(halo_in[t], sums_b[256:384])
            ).astype(BF16)
            grads[edge_at + 128 : edge_at + 256, :] = dot_first(h, sums_b[384:640]).astype(BF16)
            grads[edge_at + 256 : edge_at + 384, :] = (dot_first(rest[:, 128:256], dlin[...]) if last else dot(edges_t[...], dlin[...])).astype(BF16)
            grads[edge_at + 384 : edge_at + 512, :] = centred(
                dot_first(act_e[t], dproj[...]) if last else dot(act_t[...], dproj[...])
            ).astype(BF16)
            dbias_e = jnp.sum(sums[384:640], axis=0, keepdims=True)
            grads[small_at : small_at + small_rows, :] = jnp.concatenate(
                [dbias_e, dgain_e, dbias_n, dgain_n, jnp.zeros((small_rows - 4, D), F32)], axis=0
            ).astype(BF16)

        def own_part(sums_b):
            dh[...] = (
                dy
                + dot_last(dlin_n, nf[t, 0:128, :])
                + dot_last(sums_b[0:256], ef[t, 0:128, :])
                + dot_last(sums_b[384:640], ef[t, 128:256, :])
            )

        def older_edges():
            for i in range(SLOTS // BACK_CHUNK):
                at = pl.ds(i * BACK_CHUNK, BACK_CHUNK)
                dold = de[at, :] + dot_last(dlin[at, :], ef[t, 256:384, :])
                if last:
                    de[at, :] = dold
                else:
                    edge_grad[at, :] = dold.astype(BF16)

        if last:
            send_back(dot(spread[256:384, :], dlin[...]))

            @apart
            def _():
                sums = dot(spread[...], dlin[...])
                sums_b = sums.astype(BF16)
                edge_grads(sums, sums_b)
                node_grads()
                reduce_start(STEP1)
                own_part(sums_b)
                older_edges()
        else:
            sums = dot(spread[...], dlin[...])
            sums_b = sums.astype(BF16)
            edge_grads(sums, sums_b)
            reduce_start(EDGE0)
            reduce_start(NODE0, only=held)

            @apart
            def _():
                send_back(sums[256:384])
                own_part(sums_b)
                older_edges()

        if not last:
            pl.semaphore_wait(ready, YH - 1)
            reduce_middle(0)
            reduce_middle(1)
        exchange_wait(STEPS + t)
        own = (dh[...] + dot(halo_spread, halo_in[STEPS + t])).astype(BF16)
        if last:
            dh[...] = own.astype(F32)
        else:
            node_grad[...] = own

    forward(0)
    forward(1)
    backward(1)
    backward(0)
    for w in range(2):
        reduce_last(w)
    for w in range(2):
        reduce_finish(w)
    reduce_sent()
    for t in range(2 * STEPS):
        pltpu.make_async_copy(halo_out.at[t], halo_out.at[t], halo_ssem.at[t]).wait()


def finish(node_grad, edge_grad, total, *refs):
    outs, wide, small, sem = refs[:10], refs[10], refs[11], refs[12]
    copies = [pltpu.make_async_copy(edge_grad, outs[1], sem.at[0]), pltpu.make_async_copy(node_grad, outs[0], sem.at[1])]
    for copy in copies:
        copy.start()
    unit = ROWS[NODE0] // (YL * ZL * X * C)
    joined = total[BASE[NODE0] :, :].astype(F32).reshape(-1, 2 * unit, D)
    node0, edge0 = joined[:, :unit].reshape(ROWS[NODE0], D), joined[:, unit:].reshape(ROWS[EDGE0], D)
    for out, step0, first, count, at in (
        (2, edge0, 0, 384, 0), (4, edge0, 384, 128, 384), (6, node0, 0, 256, 512), (8, node0, 256, 128, 768)
    ):
        wide[0, at : at + count, :] = step0[first : first + count, :]
        wide[1, at : at + count, :] = total[at : at + count, :].astype(F32)
        copy = pltpu.make_async_copy(wide.at[:, pl.ds(at, count), :], outs[out], sem.at[out])
        copy.start()
        copies.append(copy)
    for t, rows in enumerate((node0[384:400], total[SMALL[STEP1] : SMALL[STEP1] + 16, :].astype(F32))):
        for k in range(4):
            small[k, t : t + 1, :] = rows[k : k + 1, :]
    for k, out in enumerate((3, 5, 7, 9)):
        copy = pltpu.make_async_copy(small.at[k], outs[out], sem.at[out])
        copy.start()
        copies.append(copy)
    for copy in copies:
        copy.wait()


def per_device(
    node_latents, edge_latents, senders, receivers, halo_rows, counts, cotangent,
    edge_first, edge_bias, edge_second, edge_gain, node_first, node_bias, node_second, node_gain,
):
    g1, g2 = YL * ZL * X * C, YH * ZH
    vmem, anywhere = pl.BlockSpec(memory_space=pltpu.VMEM), pl.BlockSpec(memory_space=pl.ANY)
    smem, hbm = pl.BlockSpec(memory_space=pltpu.SMEM), pl.BlockSpec(memory_space=pltpu.HBM)
    weights = (edge_first, edge_bias, edge_second, edge_gain, node_first, node_bias, node_second, node_gain)
    args = (
        node_latents, edge_latents, senders.reshape(SLOTS // D, D), receivers.reshape(SLOTS // D, D),
        halo_rows, counts, cotangent, *weights,
    )
    parts = pl.pallas_call(
        kernel,
        out_shape=(
            jax.ShapeDtypeStruct((NODES, D), BF16),
            jax.ShapeDtypeStruct((SLOTS, D), BF16),
            jax.ShapeDtypeStruct((sum(ROWS), D), BF16),
        ),
        in_specs=[smem if i == 5 else hbm for i in range(15)],
        out_specs=[vmem] * 3,
        scratch_shapes=[
            *(pltpu.VMEM(a.shape, a.dtype) for i, a in enumerate(args) if i != 5),
            pltpu.VMEM((SLOTS, 512), BF16),
            pltpu.VMEM((SLOTS, 256), BF16),
            pltpu.VMEM((640, SLOTS), BF16),
            pltpu.VMEM((8, D), F32),
            pltpu.VMEM((NODES, D), BF16),
            pltpu.VMEM((SLOTS, D), F32),
            pltpu.VMEM((STEPS, SLOTS, D), BF16),
            pltpu.VMEM((STEPS, SLOTS, D), F32),
            pltpu.VMEM((STEPS, SLOTS, D), F32),
            pltpu.VMEM((STEPS, SLOTS, 1), F32),
            pltpu.VMEM((STEPS, NODES, D), BF16),
            pltpu.VMEM((STEPS, NODES, D), F32),
            pltpu.VMEM((STEPS, NODES, D), F32),
            pltpu.VMEM((STEPS, NODES, 1), F32),
            pltpu.VMEM((STEPS, NODES, 256), BF16),
            pltpu.VMEM((SLOTS, D), BF16),
            pltpu.VMEM((SLOTS, D), F32),
            pltpu.VMEM((SLOTS, D), BF16),
            pltpu.VMEM((SLOTS, D), BF16),
            pltpu.VMEM((NODES, D), F32),
            pltpu.VMEM((D, SLOTS), BF16),
            pltpu.VMEM((D, SLOTS), BF16),
            pltpu.VMEM((STEPS, D, D), BF16),
            pltpu.VMEM((STEPS, D, D), BF16),
            pltpu.VMEM((2 * STEPS, 4 * HALO, D), BF16),
            pltpu.VMEM((2 * STEPS, 4 * HALO, D), BF16),
            pltpu.VMEM((sum(ROWS), D), BF16),
            pltpu.VMEM((sum(ROWS) // g1, D), BF16),
            *(pltpu.VMEM((g1, n // g1, D), BF16) for n in ROWS),
            *(pltpu.VMEM((g2, sum(ROWS[i] for i in members) // g1, D), BF16) for members in JOINED),
            pltpu.SemaphoreType.DMA((14,)),
            pltpu.SemaphoreType.DMA((2 * STEPS,)),
            pltpu.SemaphoreType.DMA((2 * STEPS,)),
            pltpu.SemaphoreType.DMA((3, 3)),
            pltpu.SemaphoreType.DMA((3, 3)),
            pltpu.SemaphoreType.REGULAR,
        ],
        compiler_params=pltpu.CompilerParams(
            collective_id=0, has_side_effects=True, vmem_limit_bytes=40 * 1024 * 1024
        ),
        name="steps",
    )(*(a if i == 5 else pltpu.with_memory_space_constraint(a, pltpu.HBM) for i, a in enumerate(args)))
    return pl.pallas_call(
        finish,
        out_shape=(
            jax.ShapeDtypeStruct((NODES, D), BF16),
            jax.ShapeDtypeStruct((SLOTS, D), BF16),
            *(jax.ShapeDtypeStruct(w.shape, F32) for w in weights),
        ),
        in_specs=[vmem] * 3,
        out_specs=[anywhere] * 10,
        scratch_shapes=[
            pltpu.VMEM((STEPS, 896, D), F32),
            pltpu.VMEM((4, STEPS, D), F32),
            pltpu.SemaphoreType.DMA((10,)),
        ],
        compiler_params=pltpu.CompilerParams(vmem_limit_bytes=40 * 1024 * 1024),
        name="finish",
    )(*parts)


def solution(mesh):
    tile = P(("sector", "span"))
    rows = P(("sector", "span"), None)
    return jax.shard_map(
        per_device,
        mesh=mesh,
        in_specs=(rows, rows, tile, tile, P(("sector", "span"), None, None), tile, rows) + (P(),) * 8,
        out_specs=(rows, rows) + (P(),) * 8,
        check_vma=False,
    )
```

```python
import functools

import jax
import jax.numpy as jnp
from jax import lax
from jax.experimental import pallas as pl
from jax.experimental.pallas import tpu as pltpu
from jax.sharding import PartitionSpec as P

F32, BF16 = jnp.float32, jnp.bfloat16
MESH = pl.DeviceIdType.MESH
STEPS = 2
EPS = 1e-05
YH, YL, ZH, C, X, ZL = 4, 2, 4, 2, 4, 2
NODES, SLOTS, D, HALO = 256, 1024, 128, 32
CHUNK, BACK_CHUNK = 512, 1024
STEP1, NODE0, EDGE0 = 0, 1, 2
ROWS = (1024, 512, 512)
BASE = (0, 1024, 1536)
SMALL = (896, 384)
JOINED = ((STEP1,), (NODE0, EDGE0))


def dot(a, b):
    return jnp.dot(a, b, preferred_element_type=F32)


def dot_first(a, b):
    return lax.dot_general(a, b, (((0,), (0,)), ((), ())), preferred_element_type=F32)


def dot_last(a, b):
    return lax.dot_general(a, b, (((1,), (1,)), ((), ())), preferred_element_type=F32)


def ones_where(mask):
    return jnp.where(mask, 1.0, 0.0).astype(BF16)


def activate(lin):
    sig = 0.5 * jnp.tanh(0.5 * lin) + 0.5
    act = lin * sig
    return act, sig + act * (1.0 - sig)


def centred(weight):
    weight = weight.astype(F32)
    return weight - jnp.mean(weight, axis=-1, keepdims=True)


def normalized(proj):
    inv = lax.rsqrt(jnp.mean(proj * proj, axis=-1, keepdims=True) + EPS)
    return proj * inv, inv


def normalized_back(dout, xhat, inv, gain):
    prod = dout * xhat
    along = jnp.mean(prod * gain, axis=-1, keepdims=True)
    return inv * (dout * gain - xhat * along), jnp.sum(prod, axis=0, keepdims=True)


def kernel(
    *refs,
):
    sources, counts, outs, here, refs = refs[:5] + refs[6:15], refs[5], refs[15:18], refs[18:32], refs[32:]
    nodes, edges, snd, rcv, halo, cot, ef, eb, es, eg, nf, nb, ns, ng = here
    node_grad, edge_grad, total = outs
    (
    own_pick, rest, spread, hal_pad, h1, part, act_e, slope_e, xhat_e, inv_e, act_n, slope_n, xhat_n, inv_n,
    node_in, edge_new, de, dlin, dproj, dh,
    edges_t, act_t, es_c, ns_c, halo_out, halo_in, grads, mid, got1_a, got1_b, got1_c, got2_a, got2_b,
    in_sem, halo_ssem, halo_rsem, red_ssem, red_rsem, ready,
    ) = refs
    sector, span = lax.axis_index("sector"), lax.axis_index("span")
    n_sector, n_span = YH * YL * ZH * C, X * ZL
    yh, yl = sector // (YL * ZH * C), lax.rem(sector // (ZH * C), YL)
    zh, c = lax.rem(sector // C, ZH), lax.rem(sector, C)
    x, zl = span // ZL, lax.rem(span, ZL)
    g1, g2 = YL * ZL * X * C, YH * ZH
    me1, me2 = ((yl * ZL + zl) * X + x) * C + c, yh * ZH + zh
    units = tuple(n // g1 for n in ROWS)
    got1, got2 = (got1_a, got1_b, got1_c), (got2_a, got2_b)
    wide = tuple(sum(units[i] for i in members) for members in JOINED)
    wide_base = tuple(BASE[members[0]] for members in JOINED)

    def turned(at, size):
        return [at] + [lax.rem(at + k, size) for k in range(1, size)]

    yls, zls, xs, cs = turned(yl, YL), turned(zl, ZL), turned(x, X), turned(c, C)
    yhs, zhs = turned(yh, YH), turned(zh, ZH)
    offsets1 = [(a, b, d, e) for a in range(YL) for b in range(ZL) for d in range(X) for e in range(C)][1:]
    offsets1.sort(key=lambda o: -(o[0] + o[1] + min(o[2], X - o[2]) + 0.5 * o[3]))
    peers1 = [
        (
            ((yls[a] * ZL + zls[b]) * X + xs[d]) * C + cs[e],
            (((yh * YL + yls[a]) * ZH + zh) * C + cs[e], xs[d] * ZL + zls[b]),
        )
        for a, b, d, e in offsets1
    ]
    offsets2 = [(a, b) for a in range(YH) for b in range(ZH)][1:]
    offsets2.sort(key=lambda o: -(min(o[0], YH - o[0]) + min(o[1], ZH - o[1])))
    peers2 = [(((yhs[a] * YL + yl) * ZH + zhs[b]) * C + c, span) for a, b in offsets2]

    around = (
        (lax.rem(sector + n_sector - 1, n_sector), span),
        (lax.rem(sector + 1, n_sector), span),
        (sector, lax.rem(span + n_span - 1, n_span)),
        (sector, lax.rem(span + 1, n_span)),
    )

    barrier = pltpu.get_barrier_semaphore()
    for peer in around:
        pl.semaphore_signal(barrier, inc=1, device_id=peer, device_id_type=MESH)

    beside = [
        peer
        for peer, (a, b) in zip(peers2, offsets2)
        if (b == 0 and a in (1, YH - 1)) or (a == 0 and b in (1, ZH - 1))
    ]
    greeted = beside + [
        peer for (_, peer), o in zip(peers1, offsets1) if o[0] + o[1] + min(o[2], X - o[2]) <= 3
    ]
    beside = beside + [peer for (_, peer), o in zip(peers1, offsets1) if o[0] and o[1:] == (0, 0, 0)]

    def tell(turn):
        for peer in beside:
            pl.semaphore_signal(ready.at[turn], inc=1, device_id=peer, device_id_type=MESH)

    def hear(turn):
        pl.semaphore_wait(ready.at[turn], len(beside))

    for peer in greeted:
        pl.semaphore_signal(barrier, inc=1, device_id=peer, device_id_type=MESH)

    loads = [pltpu.make_async_copy(a, b, in_sem.at[i]) for i, (a, b) in enumerate(zip(sources, here))]
    first = (4, 0, 2, 3, 1)
    rest_loads = [i for i in range(14) if i not in first]
    for i in (*first, *rest_loads):
        loads[i].start()
    loads[4].wait()
    loads[0].wait()

    hal_pad[...] = jnp.zeros_like(hal_pad)
    hal_pad[0:4, 0:HALO] = halo[0].astype(F32)
    padded = hal_pad[...]
    lane = lax.broadcasted_iota(jnp.int32, (1, D), 1)
    flat = jnp.zeros((1, D), F32)
    for k in range(4):
        row = padded[k : k + 1, :] if k == 0 else pltpu.roll(padded, HALO * k, 1)[k : k + 1, :]
        flat = jnp.where((lane >= HALO * k) & (lane < HALO * (k + 1)), row, flat)
    lane_f = lax.broadcasted_iota(jnp.int32, (D, D), 1).astype(F32)
    down = jnp.broadcast_to(flat, (D, D)).T
    halo_pick = jnp.concatenate([ones_where(down == lane_f), ones_where(down == lane_f + D)], axis=1)
    halo_spread = ones_where(lax.broadcasted_iota(jnp.int32, (NODES, D), 0).astype(F32) == flat)

    row_id = lax.broadcasted_iota(jnp.int32, (4 * HALO, 1), 0)
    outside = ((row_id >= 2 * HALO) & (row_id < 3 * HALO) & (span == 0)) | (
        (row_id >= 3 * HALO) & (span == n_span - 1)
    )

    apart = pl.when(sector >= 0)

    def exchange_start(t):
        for k in range(4):
            pltpu.make_async_remote_copy(
                src_ref=halo_out.at[t, pl.ds(k * HALO, HALO)],
                dst_ref=halo_in.at[t, pl.ds((k ^ 1) * HALO, HALO)],
                send_sem=halo_ssem.at[t],
                recv_sem=halo_rsem.at[t],
                device_id=around[k],
                device_id_type=MESH,
            ).start()

    def exchange_wait(t):
        pltpu.make_async_copy(halo_in.at[t], halo_in.at[t], halo_rsem.at[t]).wait()

    halo_out[0] = dot(halo_pick, nodes[...]).astype(BF16)
    pl.semaphore_wait(barrier, 4 + len(greeted))
    exchange_start(0)
    tell(0)

    for i in first[2:]:
        loads[i].wait()
    used = counts[0]
    slot = lax.broadcasted_iota(jnp.int32, (SLOTS // D, D), 0) * D + lax.broadcasted_iota(
        jnp.int32, (SLOTS // D, D), 1
    )
    snd_f = jnp.where(slot < used, snd[...], -1).astype(F32)
    rcv_f = jnp.where(slot < used, rcv[...], -1).astype(F32)
    down_f = lax.broadcasted_iota(jnp.int32, (NODES + 4 * HALO, D), 0).astype(F32)
    for r in range(SLOTS // D):
        at = pl.ds(r * D, D)
        s_row, r_row = snd_f[r : r + 1, :], rcv_f[r : r + 1, :]
        spread[0:384, at] = ones_where(down_f == s_row)
        spread[384:640, at] = ones_where(down_f[0:256] == r_row)
        s_col = jnp.broadcast_to(s_row, (D, D)).T
        r_col = jnp.broadcast_to(r_row, (D, D)).T
        own_pick[at, 0:128] = ones_where(s_col == lane_f)
        own_pick[at, 128:256] = ones_where(s_col == lane_f + 128.0)
        own_pick[at, 256:384] = ones_where(r_col == lane_f)
        own_pick[at, 384:512] = ones_where(r_col == lane_f + 128.0)
        rest[at, 0:128] = ones_where(s_col == lane_f + 256.0)
    rest[:, 128:256] = edges[...]
    for i in rest_loads:
        loads[i].wait()

    edges_t[...] = edges[...].T
    for t in range(STEPS):
        es_c[t] = centred(es[t]).astype(BF16)
        ns_c[t] = centred(ns[t]).astype(BF16)

    def forward(t):
        h = nodes[...] if t == 0 else h1[...]
        bias, gain = eb[t : t + 1, :], eg[t : t + 1, :]

        @apart
        def _():
            own_table = jnp.concatenate(
                [dot(h, ef[t, 0:128, :]).astype(BF16), dot(h, ef[t, 128:256, :]).astype(BF16)], axis=0
            )
            for i in range(SLOTS // CHUNK):
                at = pl.ds(i * CHUNK, CHUNK)
                part[at, :] = dot(own_pick[at, :], own_table) + bias
            if t == 1:
                act_t[...] = act_e[0].T

        exchange_wait(t)
        halo_in[t] = jnp.where(outside, 0.0, halo_in[t].astype(F32)).astype(BF16)
        rest_table = jnp.concatenate(
            [dot(halo_in[t], ef[t, 0:128, :]).astype(BF16), ef[t, 256:384, :]], axis=0
        )
        for i in range(SLOTS // CHUNK):
            at = pl.ds(i * CHUNK, CHUNK)
            lin = part[at, :] + dot(rest[at, :], rest_table)
            act, slope = activate(lin)
            act = act.astype(BF16)
            act_e[t, at, :] = act
            slope_e[t, at, :] = slope
            xhat, inv = normalized(dot(act, es_c[t]))
            xhat_e[t, at, :] = xhat
            inv_e[t, at, :] = inv
            new = (rest[at, 128:256].astype(F32) + xhat * gain).astype(BF16)
            edge_new[at, :] = new
        summed = dot(spread[384:640, :], edge_new[...]).astype(BF16)
        if t + 1 < STEPS:
            rest[:, 128:256] = edge_new[...]
        node_in[t, :, 0:128] = h
        node_in[t, :, 128:256] = summed
        act, slope = activate(dot(node_in[t], nf[t]) + nb[t : t + 1, :])
        act = act.astype(BF16)
        act_n[t] = act
        slope_n[t] = slope
        xhat, inv = normalized(dot(act, ns_c[t]))
        xhat_n[t] = xhat
        inv_n[t] = inv
        if t + 1 < STEPS:
            new_h = (h.astype(F32) + xhat * ng[t : t + 1, :]).astype(BF16)
            h1[...] = new_h
            halo_out[t + 1] = dot(halo_pick, new_h).astype(BF16)
            exchange_start(t + 1)

    def reduce_start(i, held=None, only=None):
        unit = units[i]

        def copy(j, peer):
            pltpu.make_async_remote_copy(
                src_ref=grads.at[pl.ds(pl.multiple_of(BASE[i] + j * unit, unit), unit)],
                dst_ref=got1[i].at[me1],
                send_sem=red_ssem.at[i, 0],
                recv_sem=red_rsem.at[i, 0],
                device_id=peer,
                device_id_type=MESH,
            ).start()

        if only is not None:
            at = only // (ZL * X * C), only // (X * C) % ZL, only // C % X, only % C
            peer = (((yh * YL + at[0]) * ZH + zh) * C + at[3], at[2] * ZL + at[1])
            pl.when(me1 != only)(lambda: copy(only, peer))
            return
        for j, peer in peers1:
            if held is None:
                copy(j, peer)
            else:
                pl.when(j != held)(functools.partial(copy, j, peer))

    def reduce_middle(w):
        for i in JOINED[w]:
            unit = units[i]
            others = got1[i].at[pl.ds(1, g1 - 1)]
            pltpu.make_async_copy(others, others, red_rsem.at[i, 0]).wait()
            got1[i][me1] = grads[pl.ds(pl.multiple_of(BASE[i] + me1 * unit, unit), unit), :]
            acc = got1[i][0].astype(F32)
            for k in range(1, g1):
                acc = acc + got1[i][k].astype(F32)
            mid[pl.ds(BASE[i] // g1, unit), :] = acc.astype(BF16)
        block = pl.ds(wide_base[w] // g1, wide[w])
        got2[w][me2] = mid[block, :]
        for peer in peers2:
            pltpu.make_async_remote_copy(
                src_ref=mid.at[block],
                dst_ref=got2[w].at[me2],
                send_sem=red_ssem.at[w, 1],
                recv_sem=red_rsem.at[w, 1],
                device_id=peer,
                device_id_type=MESH,
            ).start()

    def reduce_last(w):
        others = got2[w].at[pl.ds(1, g2 - 1)]
        pltpu.make_async_copy(others, others, red_rsem.at[w, 1]).wait()
        acc = got2[w][0].astype(F32)
        for k in range(1, g2):
            acc = acc + got2[w][k].astype(F32)
        scale = jnp.float32(NODES * n_sector * n_span) ** (-0.5)
        mine = pl.ds(pl.multiple_of(wide_base[w] + me1 * wide[w], wide[w]), wide[w])
        total[mine, :] = (acc * scale).astype(BF16)
        for _, peer in peers1:
            pltpu.make_async_remote_copy(
                src_ref=total.at[mine],
                dst_ref=total.at[mine],
                send_sem=red_ssem.at[w, 2],
                recv_sem=red_rsem.at[w, 2],
                device_id=peer,
                device_id_type=MESH,
            ).start()

    def reduce_finish(w):
        others = total.at[pl.ds(wide_base[w], (g1 - 1) * wide[w])]
        pltpu.make_async_copy(others, others, red_rsem.at[w, 2]).wait()

    def reduce_sent():
        for i in (STEP1, NODE0, EDGE0):
            sent = got1[i].at[pl.ds(1, g1 - 1)]
            pltpu.make_async_copy(sent, sent, red_ssem.at[i, 0]).wait()
        for w in range(2):
            sent = got2[w].at[pl.ds(1, g2 - 1)]
            pltpu.make_async_copy(sent, sent, red_ssem.at[w, 1]).wait()
            sent = total.at[pl.ds(wide_base[w], (g1 - 1) * wide[w])]
            pltpu.make_async_copy(sent, sent, red_ssem.at[w, 2]).wait()

    def backward(t):
        last = t + 1 == STEPS
        h = nodes[...] if t == 0 else h1[...]
        dy = cot[...].astype(F32) if last else dh[...]
        dproj_n, dgain_n = normalized_back(dy, xhat_n[t], inv_n[t], ng[t : t + 1, :])
        dproj_n = dproj_n.astype(BF16)
        dlin_n = dot_last(dproj_n, ns_c[t]) * slope_n[t]
        dbias_n = jnp.sum(dlin_n, axis=0, keepdims=True)
        dlin_n = dlin_n.astype(BF16)
        dsummed = dot_last(dlin_n, nf[t, 128:256, :]).astype(BF16)
        node_at = BASE[STEP1] + 512 if last else BASE[NODE0]
        small_at = BASE[STEP1] + SMALL[STEP1] if last else BASE[NODE0] + SMALL[NODE0]
        held = SMALL[NODE0] // units[NODE0]

        def node_grads():
            grads[node_at : node_at + 256, :] = dot_first(node_in[t], dlin_n).astype(BF16)
            grads[node_at + 256 : node_at + 384, :] = centred(dot_first(act_n[t], dproj_n)).astype(BF16)

        small_rows = 128 if last else units[NODE0]
        if not last:
            node_grads()
            if small_rows < 128:
                grads[small_at + small_rows : small_at + 128, :] = jnp.zeros((128 - small_rows, D), BF16)
            reduce_start(NODE0, held=held)
        dgain_e = jnp.zeros((1, D), F32)
        gain = eg[t : t + 1, :]
        for i in range(SLOTS // BACK_CHUNK):
            at = pl.ds(i * BACK_CHUNK, BACK_CHUNK)
            dnew = dot(own_pick[at, 256:512], dsummed)
            if not last:
                dnew = dnew + de[at, :]
            de[at, :] = dnew
            dp, dg = normalized_back(dnew, xhat_e[t, at, :], inv_e[t, at, :], gain)
            dgain_e = dgain_e + dg
            dp = dp.astype(BF16)
            dproj[at, :] = dp
            dl = (dot_last(dp, es_c[t]) * slope_e[t, at, :]).astype(BF16)
            dlin[at, :] = dl

        def send_back(sums):
            dhalo = dot_last(sums.astype(BF16), ef[t, 0:128, :])
            halo_out[STEPS + t] = jnp.where(outside, 0.0, dhalo).astype(BF16)
            exchange_start(STEPS + t)

        edge_at = BASE[STEP1] if last else BASE[EDGE0]

        def edge_grads(sums, sums_b):
            grads[edge_at : edge_at + 128, :] = (
                dot_first(h, sums_b[0:256]) + dot_first(halo_in[t], sums_b[256:384])
            ).astype(BF16)
            grads[edge_at + 128 : edge_at + 256, :] = dot_first(h, sums_b[384:640]).astype(BF16)
            grads[edge_at + 256 : edge_at + 384, :] = (dot_first(rest[:, 128:256], dlin[...]) if last else dot(edges_t[...], dlin[...])).astype(BF16)
            grads[edge_at + 384 : edge_at + 512, :] = centred(
                dot_first(act_e[t], dproj[...]) if last else dot(act_t[...], dproj[...])
            ).astype(BF16)
            dbias_e = jnp.sum(sums[384:640], axis=0, keepdims=True)
            grads[small_at : small_at + small_rows, :] = jnp.concatenate(
                [dbias_e, dgain_e, dbias_n, dgain_n, jnp.zeros((small_rows - 4, D), F32)], axis=0
            ).astype(BF16)

        def own_part(sums_b):
            dh[...] = (
                dy
                + dot_last(dlin_n, nf[t, 0:128, :])
                + dot_last(sums_b[0:256], ef[t, 0:128, :])
                + dot_last(sums_b[384:640], ef[t, 128:256, :])
            )

        def older_edges():
            for i in range(SLOTS // BACK_CHUNK):
                at = pl.ds(i * BACK_CHUNK, BACK_CHUNK)
                dold = de[at, :] + dot_last(dlin[at, :], ef[t, 256:384, :])
                if last:
                    de[at, :] = dold
                else:
                    edge_grad[at, :] = dold.astype(BF16)

        if last:
            send_back(dot(spread[256:384, :], dlin[...]))

            @apart
            def _():
                sums = dot(spread[...], dlin[...])
                sums_b = sums.astype(BF16)
                edge_grads(sums, sums_b)
                node_grads()
                reduce_start(STEP1)
                own_part(sums_b)
                older_edges()
        else:
            sums = dot(spread[...], dlin[...])
            sums_b = sums.astype(BF16)
            edge_grads(sums, sums_b)
            reduce_start(EDGE0)
            reduce_start(NODE0, only=held)

            @apart
            def _():
                send_back(sums[256:384])
                own_part(sums_b)
                older_edges()

        if not last:
            hear(2)
            reduce_middle(0)
            reduce_middle(1)
        exchange_wait(STEPS + t)
        own = (dh[...] + dot(halo_spread, halo_in[STEPS + t])).astype(BF16)
        if last:
            dh[...] = own.astype(F32)
        else:
            node_grad[...] = own

    forward(0)
    hear(0)
    tell(1)
    forward(1)
    hear(1)
    tell(2)
    backward(1)
    backward(0)
    for w in range(2):
        reduce_last(w)
    for w in range(2):
        reduce_finish(w)
    reduce_sent()
    for t in range(2 * STEPS):
        pltpu.make_async_copy(halo_out.at[t], halo_out.at[t], halo_ssem.at[t]).wait()


def finish(node_grad, edge_grad, total, *refs):
    outs, wide, small, sem = refs[:10], refs[10], refs[11], refs[12]
    copies = [pltpu.make_async_copy(edge_grad, outs[1], sem.at[0]), pltpu.make_async_copy(node_grad, outs[0], sem.at[1])]
    for copy in copies:
        copy.start()
    unit = ROWS[NODE0] // (YL * ZL * X * C)
    joined = total[BASE[NODE0] :, :].astype(F32).reshape(-1, 2 * unit, D)
    node0, edge0 = joined[:, :unit].reshape(ROWS[NODE0], D), joined[:, unit:].reshape(ROWS[EDGE0], D)
    for out, step0, first, count, at in (
        (2, edge0, 0, 384, 0), (4, edge0, 384, 128, 384), (6, node0, 0, 256, 512), (8, node0, 256, 128, 768)
    ):
        wide[0, at : at + count, :] = step0[first : first + count, :]
        wide[1, at : at + count, :] = total[at : at + count, :].astype(F32)
        copy = pltpu.make_async_copy(wide.at[:, pl.ds(at, count), :], outs[out], sem.at[out])
        copy.start()
        copies.append(copy)
    for t, rows in enumerate((node0[384:400], total[SMALL[STEP1] : SMALL[STEP1] + 16, :].astype(F32))):
        for k in range(4):
            small[k, t : t + 1, :] = rows[k : k + 1, :]
    for k, out in enumerate((3, 5, 7, 9)):
        copy = pltpu.make_async_copy(small.at[k], outs[out], sem.at[out])
        copy.start()
        copies.append(copy)
    for copy in copies:
        copy.wait()


def per_device(
    node_latents, edge_latents, senders, receivers, halo_rows, counts, cotangent,
    edge_first, edge_bias, edge_second, edge_gain, node_first, node_bias, node_second, node_gain,
):
    g1, g2 = YL * ZL * X * C, YH * ZH
    vmem, anywhere = pl.BlockSpec(memory_space=pltpu.VMEM), pl.BlockSpec(memory_space=pl.ANY)
    smem, hbm = pl.BlockSpec(memory_space=pltpu.SMEM), pl.BlockSpec(memory_space=pltpu.HBM)
    weights = (edge_first, edge_bias, edge_second, edge_gain, node_first, node_bias, node_second, node_gain)
    args = (
        node_latents, edge_latents, senders.reshape(SLOTS // D, D), receivers.reshape(SLOTS // D, D),
        halo_rows, counts, cotangent, *weights,
    )
    parts = pl.pallas_call(
        kernel,
        out_shape=(
            jax.ShapeDtypeStruct((NODES, D), BF16),
            jax.ShapeDtypeStruct((SLOTS, D), BF16),
            jax.ShapeDtypeStruct((sum(ROWS), D), BF16),
        ),
        in_specs=[smem if i == 5 else hbm for i in range(15)],
        out_specs=[vmem] * 3,
        scratch_shapes=[
            *(pltpu.VMEM(a.shape, a.dtype) for i, a in enumerate(args) if i != 5),
            pltpu.VMEM((SLOTS, 512), BF16),
            pltpu.VMEM((SLOTS, 256), BF16),
            pltpu.VMEM((640, SLOTS), BF16),
            pltpu.VMEM((8, D), F32),
            pltpu.VMEM((NODES, D), BF16),
            pltpu.VMEM((SLOTS, D), F32),
            pltpu.VMEM((STEPS, SLOTS, D), BF16),
            pltpu.VMEM((STEPS, SLOTS, D), F32),
            pltpu.VMEM((STEPS, SLOTS, D), F32),
            pltpu.VMEM((STEPS, SLOTS, 1), F32),
            pltpu.VMEM((STEPS, NODES, D), BF16),
            pltpu.VMEM((STEPS, NODES, D), F32),
            pltpu.VMEM((STEPS, NODES, D), F32),
            pltpu.VMEM((STEPS, NODES, 1), F32),
            pltpu.VMEM((STEPS, NODES, 256), BF16),
            pltpu.VMEM((SLOTS, D), BF16),
            pltpu.VMEM((SLOTS, D), F32),
            pltpu.VMEM((SLOTS, D), BF16),
            pltpu.VMEM((SLOTS, D), BF16),
            pltpu.VMEM((NODES, D), F32),
            pltpu.VMEM((D, SLOTS), BF16),
            pltpu.VMEM((D, SLOTS), BF16),
            pltpu.VMEM((STEPS, D, D), BF16),
            pltpu.VMEM((STEPS, D, D), BF16),
            pltpu.VMEM((2 * STEPS, 4 * HALO, D), BF16),
            pltpu.VMEM((2 * STEPS, 4 * HALO, D), BF16),
            pltpu.VMEM((sum(ROWS), D), BF16),
            pltpu.VMEM((sum(ROWS) // g1, D), BF16),
            *(pltpu.VMEM((g1, n // g1, D), BF16) for n in ROWS),
            *(pltpu.VMEM((g2, sum(ROWS[i] for i in members) // g1, D), BF16) for members in JOINED),
            pltpu.SemaphoreType.DMA((14,)),
            pltpu.SemaphoreType.DMA((2 * STEPS,)),
            pltpu.SemaphoreType.DMA((2 * STEPS,)),
            pltpu.SemaphoreType.DMA((3, 3)),
            pltpu.SemaphoreType.DMA((3, 3)),
            pltpu.SemaphoreType.REGULAR((3,)),
        ],
        compiler_params=pltpu.CompilerParams(
            collective_id=0, has_side_effects=True, vmem_limit_bytes=40 * 1024 * 1024
        ),
        name="steps",
    )(*(a if i == 5 else pltpu.with_memory_space_constraint(a, pltpu.HBM) for i, a in enumerate(args)))
    return pl.pallas_call(
        finish,
        out_shape=(
            jax.ShapeDtypeStruct((NODES, D), BF16),
            jax.ShapeDtypeStruct((SLOTS, D), BF16),
            *(jax.ShapeDtypeStruct(w.shape, F32) for w in weights),
        ),
        in_specs=[vmem] * 3,
        out_specs=[anywhere] * 10,
        scratch_shapes=[
            pltpu.VMEM((STEPS, 896, D), F32),
            pltpu.VMEM((4, STEPS, D), F32),
            pltpu.SemaphoreType.DMA((10,)),
        ],
        compiler_params=pltpu.CompilerParams(vmem_limit_bytes=40 * 1024 * 1024),
        name="finish",
    )(*parts)


def solution(mesh):
    tile = P(("sector", "span"))
    rows = P(("sector", "span"), None)
    return jax.shard_map(
        per_device,
        mesh=mesh,
        in_specs=(rows, rows, tile, tile, P(("sector", "span"), None, None), tile, rows) + (P(),) * 8,
        out_specs=(rows, rows) + (P(),) * 8,
        check_vma=False,
    )
```
